256 devices in a mesh: band: 64 (over x, y_hi, z), chan: 4 (over y_lo, core).
Axes of the slice: x: 4, y: 4 (y_hi: 2, y_lo: 2; y = y_hi * 2 + y_lo), z: 8, core: 2. Of those that a mesh axis runs over, the one named last changes fastest.
Arguments:
- atmos: bfloat16 [256, 368640], P('chan', 'band'), may hold values from -6 to 6
- kernels: float32 [1, 3, 256], P(None, None, 'chan'), may hold values from -3 to 3
- w_one: bfloat16 [1, 256, 1024], P(None, None, 'chan'), may hold values from -0.375 to 0.375
- w_two: bfloat16 [1, 1024, 256], P(None, 'chan'), may hold values from -0.1875 to 0.1875
- w_flux: bfloat16 [256, 128], P('chan'), may hold values from -0.375 to 0.375
- sea_mask: int32 [368640], P('band'), may hold values 0 or 1
- route: int32 [2880, 1], P('band'), may hold values from 0 to 63; in each aligned block of 45 rows (0 to 44, 45 to 89, ...) at most 2 rows name the same one
- ocean_state: bfloat16 [128, 64, 128, 128], P(None, 'band'), may hold values from -6 to 6
- ct_atmos: bfloat16 [256, 368640], P('chan', 'band'), may hold values from -6 to 6
- ct_ocean: bfloat16 [128, 64, 128, 128], P(None, 'band'), may hold values from -6 to 6
- wo_one: bfloat16 [256, 512], P(None, 'chan'), may hold values from -0.375 to 0.375
- wo_two: bfloat16 [512, 128], P('chan'), may hold values from -0.25 to 0.25
Outputs:
- d_atmos: bfloat16 [256, 368640], P('chan', 'band')
- d_kernels: float32 [1, 3, 256], P(None, None, 'chan')
- d_w_one: float32 [1, 256, 1024], P(None, None, 'chan')
- d_w_two: float32 [1, 1024, 256], P(None, 'chan')
- d_w_flux: float32 [256, 128], P('chan')
- d_ocean_state: bfloat16 [128, 64, 128, 128], P('chan', 'band')
- d_wo_one: float32 [256, 512], P(None, 'chan')
- d_wo_two: float32 [512, 128], P('chan')
The draws below stay inside these ranges and needn't reach their ends.
Inputs may be any that keep to these rules, and one draw needn't show every extreme that they name: route[k, 0] is the ocean tile that takes block k; among the 45 blocks of one row group no tile is named more than 2 times, a bound that some block reaches.
All inputs are finite; a program needn't handle non-finite values. No bound on the sum of `sea_mask` on one device may be relied on, other than what follows from the above.
Results may differ from the reference program's by a relative error of at most 0.028.
Values may be sent and summed in bfloat16 or wider, within the bound.
A program may use at most 128 MiB of HBM per device.

```python
import math
import jax
import jax.numpy as jnp
import numpy as np
from jax import lax

C = 256
HID = 1024
OL = 128
OH = 512
PTS = 128
LON = 1440
LAYERS = 1
ROWS_DEV = 4
LAT = 256
BLK_DEV = 45
NBLK = 2880
CAP = 2
SLOTS = 128
N_BAND = 64
N_CHAN = 4


def place_ends(drawn, stream_key, least, top_value):
    shape = drawn.shape
    index_at = [jax.random.randint(jax.random.fold_in(stream_key, axis), (), 0, shape[axis]) for axis in range(len(shape))]
    drawn = drawn.at[tuple(index_at)].set(least)
    longest = shape.index(max(shape))
    index_at[longest] = (index_at[longest] + 1) % shape[longest]
    return drawn.at[tuple(index_at)].set(top_value)


def steps_of(rng, dims, shards, low, largest):
    level = 1.0
    for dim, shards_of in shards:
        heights = jax.random.uniform(jax.random.fold_in(jax.random.fold_in(rng, 6), dim), (shards_of,), jnp.float32, low / len(shards), largest / len(shards))
        level = level * jnp.repeat(jnp.exp(heights), dims[dim] // shards_of).reshape((-1,) + (1,) * (len(dims) - 1 - dim))
    return level


def assign_block(stream_key, own, number, rows, number_of, top, bound, lean):
    sequence = jax.random.permutation(stream_key, number_of)
    crowded, ordinary = portions_of(number_of, rows * top, bound, lean, True), portions_of(number_of, rows * top, bound, lean, False)
    places = jnp.arange(number_of)

    def named(lengths, rotation):
        used = int((lengths > 0).sum())
        fixed = max(1, used // 4)
        moved = fixed + (places - fixed + rotation * (used - fixed)) % max(1, number_of - fixed)
        return jnp.zeros((number_of,), jnp.int32).at[sequence[jnp.where(places < fixed, places, moved)]].set(jnp.asarray(lengths, jnp.int32))

    lengths = jnp.where(number % 4 == 0, named(crowded, number // 4), named(ordinary, number - number // 4 - 1))
    mixed = jax.random.permutation(jax.random.fold_in(own, 3), number_of)
    giver, taker = mixed[0:number_of // 2 * 2:2], mixed[1:number_of // 2 * 2:2]
    margin = jnp.minimum(lengths[giver] - 1, bound - lengths[taker]) // 2
    margin = jnp.where((giver == sequence[0]) | (taker == sequence[0]) | (lengths[taker] == 0), 0, jnp.maximum(margin, 0))
    moved = jax.random.randint(jax.random.fold_in(own, 4), (number_of // 2,), 0, 1 << 20) % (margin + 1)
    lengths = lengths.at[giver].add(-moved).at[taker].add(moved)
    members = jnp.searchsorted(jnp.cumsum(lengths), jnp.arange(rows * top), side="right").astype(jnp.int32)
    grid = members.reshape(top, rows).T
    grid = grid[jax.random.permutation(jax.random.fold_in(own, 1), rows)]
    rotation = jax.random.randint(jax.random.fold_in(own, 2), (rows, 1), 0, top)
    return jnp.take_along_axis(grid, (jnp.arange(top)[None, :] + rotation) % top, axis=1)


def portions_of(amount, total, reach, lean, full):
    portions = [(1 << 20) // math.isqrt(grade ** lean) + 1 for grade in range(1, amount + 1)]
    largest = reach if full else min(reach, max(-(-total // amount), total * portions[0] // sum(portions)))
    least = 1 if total - largest >= amount - 1 else 0
    given, spare = [largest] + [least] * (amount - 1), total - largest - least * (amount - 1)
    while spare > 0:
        free = [i for i in range(1, amount) if given[i] < largest] or [i for i in range(1, amount) if given[i] < reach]
        whole, remaining = sum([portions[i] for i in free]), spare
        for i in free:
            addition = min(reach - given[i], max(1, remaining * portions[i] // whole), spare)
            given[i] = given[i] + addition
            spare = spare - addition
    return np.array(given)


def scatter_about(rng, shape, deviation, bound, cuts=(), kind=jnp.bfloat16):
    gain = steps_of(rng, shape, cuts, -0.22, 0.18) if cuts else 1.0
    drawn = jax.random.normal(rng, shape, jnp.float32) * deviation * gain
    return jnp.minimum(jnp.maximum(drawn, -bound), bound).astype(kind)


def setup_inputs(seed: int = 0) -> dict:
    seeds = jax.random.split(jax.random.key(seed), 13)
    atmos = scatter_about(seeds[0], (C, LAT * LON), 1.0, 6.0, ((0, 4), (1, 64)))
    kernels = scatter_about(seeds[1], (LAYERS, 3, C), 0.6, 3.0, ((2, 4),), jnp.float32)
    w_one = scatter_about(seeds[2], (LAYERS, C, HID), C ** -0.5, 0.375, ((2, 4),))
    w_two = scatter_about(seeds[3], (LAYERS, HID, C), HID ** -0.5, 0.1875, ((1, 4),))
    w_flux = scatter_about(seeds[4], (C, OL), C ** -0.5, 0.375, ((0, 4),))
    sea_mask = place_ends((jax.random.randint(seeds[5], (LAT * LON,), 0, 3) < 2).astype(jnp.int32), jax.random.fold_in(seeds[5], 1), 0, 1)
    route_keys = jax.random.split(jax.random.fold_in(seeds[6], 1), NBLK // BLK_DEV)
    route_turns = jax.random.permutation(jax.random.fold_in(seeds[6], 3), NBLK // BLK_DEV)
    route = jax.vmap(lambda own, number: assign_block(jax.random.fold_in(seeds[6], 2), own, number, BLK_DEV, N_BAND, 1, CAP, 1))(route_keys, route_turns).reshape((NBLK, 1))
    ocean_state = scatter_about(seeds[7], (PTS, N_BAND, SLOTS, OL), 1.0, 6.0, ((1, 64),))
    ct_atmos = scatter_about(seeds[8], (C, LAT * LON), 1.0, 6.0, ((0, 4), (1, 64)))
    ct_ocean = scatter_about(seeds[9], (PTS, N_BAND, SLOTS, OL), 1.0, 6.0, ((1, 64),))
    wo_one = scatter_about(seeds[10], (2 * OL, OH), (2 * OL) ** -0.5, 0.375, ((1, 4),))
    wo_two = scatter_about(seeds[11], (OH, OL), OH ** -0.5, 0.25, ((0, 4),))
    return {"atmos": atmos, "kernels": kernels, "w_one": w_one, "w_two": w_two, "w_flux": w_flux, "sea_mask": sea_mask, "route": route, "ocean_state": ocean_state, "ct_atmos": ct_atmos, "ct_ocean": ct_ocean, "wo_one": wo_one, "wo_two": wo_two}


def silu_grad(values):
    sigma = jax.nn.sigmoid(values)
    return sigma * (1.0 + values * (1.0 - sigma))

def rounded(values):
    return lax.optimization_barrier(values.astype(jnp.bfloat16)).astype(jnp.float32)

def contract(left, right, left_dim, right_dim):
    return lax.dot_general(left, right, (((left_dim,), (right_dim,)), ((), ())), preferred_element_type=jnp.float32)

def convolve(padded, kernel_taps):
    return kernel_taps[0][:, None, None] * padded[:, :-2] + kernel_taps[1][:, None, None] * padded[:, 1:-1] + kernel_taps[2][:, None, None] * padded[:, 2:]

def by_band(field):
    return jnp.moveaxis(field.reshape(C, N_BAND, ROWS_DEV * LON), 1, 0)

def from_band(field):
    return jnp.moveaxis(field, 0, 1).reshape(C, LAT, LON)

def reference(atmos, kernels, w_one, w_two, w_flux, sea_mask, route, ocean_state, ct_atmos, ct_ocean, wo_one, wo_two):
    atmos = atmos.reshape(C, LAT, LON)
    ct_atmos = ct_atmos.reshape(C, LAT, LON)
    group_hidden_units = HID // N_CHAN
    group_chan = C // N_CHAN
    group_ocean = OH // N_CHAN
    grid_points = ROWS_DEV * LON
    state = atmos
    inputs = []
    for layer_idx in range(LAYERS):
        padded = jnp.pad(state, ((0, 0), (1, 1), (0, 0)))
        mixed_in = convolve(padded, kernels[layer_idx]).astype(jnp.bfloat16)
        w_first = w_one[layer_idx]
        second_weight = w_two[layer_idx].reshape(N_CHAN, group_hidden_units, C).astype(jnp.float32)

        def forward_band(column):
            hidden_layer = jax.nn.silu(contract(w_first, column, 0, 0)).astype(jnp.bfloat16)
            part_pieces = jnp.einsum('wka,wkt->wat', second_weight, hidden_layer.reshape(N_CHAN, group_hidden_units, grid_points).astype(jnp.float32))
            return lax.optimization_barrier(jnp.sum(rounded(part_pieces), axis=0))
        update = from_band(lax.map(forward_band, by_band(mixed_in)))
        inputs.append(state)
        state = (state.astype(jnp.float32) + update).astype(jnp.bfloat16)
    final_state = state
    flux_weight = w_flux.reshape(N_CHAN, group_chan, OL).astype(jnp.float32)

    def flux_band(column):
        part_pieces = jnp.einsum('gcbp,gco->gpbo', column.reshape(N_CHAN, group_chan, BLK_DEV, PTS).astype(jnp.float32), flux_weight)
        return lax.optimization_barrier(jnp.sum(rounded(part_pieces), axis=0))
    flux = lax.map(flux_band, by_band(final_state))
    mask_pts = jnp.transpose(sea_mask.reshape(N_BAND, BLK_DEV, PTS), (0, 2, 1)).astype(jnp.float32)
    forcing = (flux * mask_pts[..., None]).astype(jnp.bfloat16)
    target = route[:, 0].reshape(N_BAND, BLK_DEV)
    order = jnp.arange(BLK_DEV, dtype=jnp.int32)
    earlier = (target[:, None, :] == target[:, :, None]) & (order[None, None, :] < order[None, :, None])
    rank = lax.optimization_barrier(jnp.sum(earlier.astype(jnp.int32), axis=2))
    source = jnp.arange(N_BAND, dtype=jnp.int32)[:, None]
    slot_of = (target * SLOTS + source * CAP + rank).reshape(NBLK).astype(jnp.int32)
    flat_forcing = jnp.transpose(forcing, (1, 0, 2, 3)).reshape(PTS, NBLK, OL)
    ocean_forcing = jnp.zeros((PTS, N_BAND * SLOTS, OL), jnp.bfloat16).at[:, slot_of].set(flat_forcing)
    ocean_forcing = ocean_forcing.reshape(PTS, N_BAND, SLOTS, OL)
    upper = wo_one[:OL]
    lower = wo_one[OL:]
    upper_groups = upper.reshape(OL, N_CHAN, group_ocean).astype(jnp.float32)
    lower_groups = lower.reshape(OL, N_CHAN, group_ocean).astype(jnp.float32)
    total_rows = PTS * SLOTS

    def ocean_tile(tile_args):
        tile_state, tile_forcing, tile_cotan = tile_args
        flat_state = tile_state.reshape(total_rows, OL)
        flat_force = tile_forcing.reshape(total_rows, OL)
        flat_cotan = tile_cotan.reshape(total_rows, OL)
        pre_ocean = contract(flat_state, upper, 1, 0) + contract(flat_force, lower, 1, 0)
        act_ocean = jax.nn.silu(pre_ocean).astype(jnp.bfloat16)
        grad_ocean = (contract(flat_cotan, wo_two, 1, 1) * silu_grad(pre_ocean)).astype(jnp.bfloat16)
        grad_second = contract(act_ocean, flat_cotan, 0, 0)
        grad_first = jnp.concatenate([contract(flat_state, grad_ocean, 0, 0), contract(flat_force, grad_ocean, 0, 0)], axis=0)
        grad_groups = grad_ocean.reshape(total_rows, N_CHAN, group_ocean).astype(jnp.float32)
        state_parts = jnp.einsum('rgh,ogh->gro', grad_groups, upper_groups)
        force_parts = jnp.einsum('rgh,ogh->gro', grad_groups, lower_groups)
        d_state = (flat_cotan.astype(jnp.float32) + lax.optimization_barrier(jnp.sum(rounded(state_parts), axis=0))).astype(jnp.bfloat16)
        d_force = lax.optimization_barrier(jnp.sum(rounded(force_parts), axis=0)).astype(jnp.bfloat16)
        return (d_state.reshape(PTS, SLOTS, OL), d_force.reshape(PTS, SLOTS, OL), grad_first, grad_second)
    tile_inputs = (jnp.moveaxis(ocean_state, 1, 0), jnp.moveaxis(ocean_forcing, 1, 0), jnp.moveaxis(ct_ocean, 1, 0))
    d_states, d_forces, firsts, seconds = lax.map(ocean_tile, tile_inputs)
    d_ocean_state = jnp.moveaxis(d_states, 0, 1)
    d_wo_one = lax.optimization_barrier(jnp.sum(firsts, axis=0))
    d_wo_two = lax.optimization_barrier(jnp.sum(seconds, axis=0))
    back_slots = jnp.moveaxis(d_forces, 0, 1).reshape(PTS, N_BAND * SLOTS, OL)
    back_blocks = back_slots[:, slot_of, :].reshape(PTS, N_BAND, BLK_DEV, OL)
    d_flux = (back_blocks.astype(jnp.float32) * jnp.transpose(mask_pts, (1, 0, 2))[..., None]).astype(jnp.bfloat16)
    state_blocks = final_state.reshape(C, N_BAND, BLK_DEV, PTS).astype(jnp.float32)
    flux_grad = d_flux.astype(jnp.float32)
    d_w_flux = jnp.einsum('cnbp,pnbo->co', state_blocks, flux_grad)
    back_state = jnp.einsum('pnbo,co->cnbp', flux_grad, w_flux.astype(jnp.float32)).reshape(C, LAT, LON)
    cotan = (ct_atmos.astype(jnp.float32) + back_state).astype(jnp.bfloat16)
    tap_grads = [None] * LAYERS
    one_grads = [None] * LAYERS
    two_grads = [None] * LAYERS
    for layer_idx in reversed(range(LAYERS)):
        state_in = inputs[layer_idx]
        padded = jnp.pad(state_in, ((0, 0), (1, 1), (0, 0)))
        kernel_taps = kernels[layer_idx]
        mixed_in = convolve(padded, kernel_taps).astype(jnp.bfloat16)
        w_first = w_one[layer_idx]
        second_weight = w_two[layer_idx]
        leading_groups = w_first.reshape(C, N_CHAN, group_hidden_units).astype(jnp.float32)

        def backward_band(band_args):
            column, cotan_col = band_args
            pre_act = contract(w_first, column, 0, 0)
            hidden_layer = jax.nn.silu(pre_act).astype(jnp.bfloat16)
            hidden_layer_gradient = (contract(second_weight, cotan_col, 1, 0) * silu_grad(pre_act)).astype(jnp.bfloat16)
            grad_second = contract(hidden_layer, cotan_col, 1, 1)
            grad_first = contract(column, hidden_layer_gradient, 1, 1)
            part_pieces = jnp.einsum('kqy,qym->qkm', leading_groups, hidden_layer_gradient.reshape(N_CHAN, group_hidden_units, grid_points).astype(jnp.float32))
            return (lax.optimization_barrier(jnp.sum(rounded(part_pieces), axis=0)).astype(jnp.bfloat16), grad_first, grad_second)
        conv_bands, firsts, seconds = lax.map(backward_band, (by_band(mixed_in), by_band(cotan)))
        conv_grad = from_band(conv_bands)
        conv_pad = jnp.pad(conv_grad, ((0, 0), (1, 1), (0, 0)))
        tap_grads[layer_idx] = jnp.stack([lax.optimization_barrier(jnp.sum(padded[:, offset:offset + LAT].astype(jnp.float32) * conv_grad.astype(jnp.float32), axis=(1, 2))) for offset in range(3)])
        one_grads[layer_idx] = lax.optimization_barrier(jnp.sum(firsts, axis=0))
        two_grads[layer_idx] = lax.optimization_barrier(jnp.sum(seconds, axis=0))
        spread = kernel_taps[0][:, None, None] * conv_pad[:, 2:] + kernel_taps[1][:, None, None] * conv_pad[:, 1:-1] + kernel_taps[2][:, None, None] * conv_pad[:, :-2]
        cotan = (cotan.astype(jnp.float32) + spread).astype(jnp.bfloat16)
    return (cotan.reshape(C, LAT * LON), jnp.stack(tap_grads), jnp.stack(one_grads), jnp.stack(two_grads), d_w_flux, d_ocean_state, d_wo_one, d_wo_two)
```

```python
import functools

import jax
import jax.numpy as jnp
from jax import lax
from jax.experimental import pallas as pl
from jax.experimental.pallas import tpu as pltpu
from jax.sharding import PartitionSpec as P

PTS = 128
LON = 1440
MESH = pl.DeviceIdType.MESH
F32 = jnp.float32
BF16 = jnp.bfloat16
VMEM = pltpu.VMEM
DMA = pltpu.SemaphoreType.DMA
ZLEN = 8
LIMIT = 56 * 1024 * 1024


def nn(a, b):
    return lax.dot_general(a, b, (((1,), (0,)), ((), ())), preferred_element_type=F32)


def tn(a, b):
    return lax.dot_general(a, b, (((0,), (0,)), ((), ())), preferred_element_type=F32)


def nt(a, b):
    return lax.dot_general(a, b, (((1,), (1,)), ((), ())), preferred_element_type=F32)


def sigmoid(v):
    return 0.5 * jnp.tanh(0.5 * v) + 0.5


def place():
    b, c = lax.axis_index("band"), lax.axis_index("chan")
    mate = (c // 2) * 2 + (1 - c % 2)
    return b, c, mate, (c + 2) % 4, (mate + 2) % 4


def send(src, dst, ssem, rsem, b, c):
    copy = pltpu.make_async_remote_copy(
        src_ref=src,
        dst_ref=dst,
        send_sem=ssem,
        recv_sem=rsem,
        device_id=(b, c),
        device_id_type=MESH,
    )
    copy.start()
    return copy


def drain(ref, sem):
    pltpu.make_async_copy(ref, ref, sem).wait()


def signal(b, c):
    pl.semaphore_signal(
        pltpu.get_barrier_semaphore(), inc=1, device_id=(b, c), device_id_type=MESH
    )


def shifted(ref, start, extra, width):
    wide = ref[:, start : start + width + 128].astype(F32)
    return pltpu.roll(wide, width + 128 - extra, axis=1)[:, :width]


def forward_kernel(
    atmos, taps, w_one, w_two, w_flux,
    ext, zb, al, w1, w2, wf, fp,
    zc, ab, fx,
    hs, hr, ws, wr, zs, zr, as_, ar, fs, fr,
):
    b, c, mate, across, diag = place()
    bands = lax.axis_size("band")
    up, down = (b + bands - 1) % bands, (b + 1) % bands
    rows, points = atmos.shape
    share = zb.shape[1]
    quarter = fp.shape[1]
    signal(up, c)
    signal(down, c)
    for d in (1, 2, 3):
        signal(b, (c + d) % 4)
    pl.semaphore_wait(pltpu.get_barrier_semaphore(), 5)

    halo = [
        send(atmos.at[:, points - share :], ext.at[:, :share], hs.at[0], hr.at[0], down, c),
        send(atmos.at[:, :share], ext.at[:, share + points :], hs.at[1], hr.at[1], up, c),
    ]
    mine = pl.ds(pl.multiple_of(c * rows, rows), rows)
    theirs = pl.ds(pl.multiple_of(across * rows, rows), rows)
    sources = (w_one, w_two, w_flux)
    slots = (w1.at[c], w2.at[c], wf.at[mine, :])
    far = (w1.at[across], w2.at[across], wf.at[theirs, :])
    first, second = [], []
    for i in range(3):
        second.append(send(sources[i], slots[i], ws.at[1, i], wr.at[1, i], b, across))
        first.append(send(sources[i], slots[i], ws.at[0, i], wr.at[0, i], b, mate))
    w1[c] = w_one[...]
    w2[c] = w_two[...]
    wf[mine, :] = w_flux[...]
    ext[:, share : share + points] = atmos[...]
    zc[:, points:] = jnp.zeros((rows, zc.shape[1] - points), BF16)
    for copy in halo:
        copy.wait()

    @pl.when(b == 0)
    def _():
        ext[:, :share] = jnp.zeros((rows, share), BF16)

    @pl.when(b == bands - 1)
    def _():
        ext[:, share + points :] = jnp.zeros((rows, share), BF16)

    t0, t1, t2 = taps[:, 0:1], taps[:, 1:2], taps[:, 2:3]
    width = 384
    low = share - LON
    high = share + LON
    for at in range(0, points, width):
        zc[:, at : at + width] = (
            t0 * shifted(ext, at + low // 128 * 128, low % 128, width)
            + t1 * ext[:, at + share : at + share + width].astype(F32)
            + t2 * shifted(ext, at + high // 128 * 128, high % 128, width)
        ).astype(BF16)
    zcopies, acopies = [], []
    for d in (2, 1, 3):
        to = (c + d) % 4
        cols = pl.ds(pl.multiple_of(share * to, share), share)
        zcopies.append(send(zc.at[:, cols], zb.at[mine, :], zs.at[d], zr.at[d], b, to))
    third = []
    for i in range(3):
        second[i].wait_recv()
        third.append(send(far[i], far[i], ws.at[2, i], wr.at[2, i], b, mate))
    for d in (2, 1, 3):
        to = (c + d) % 4
        cols = pl.ds(pl.multiple_of(share * to + share, share), share)
        acopies.append(send(ext.at[:, cols], ab.at[mine, :], as_.at[d], ar.at[d], b, to))
    zb[mine, :] = zc[:, pl.ds(pl.multiple_of(share * c, share), share)]
    ab[mine, :] = ext[:, pl.ds(pl.multiple_of(share * c + share, share), share)]
    for copy in first + third:
        copy.wait()
    for copy in second:
        copy.wait_send()
    for copy in zcopies:
        copy.wait()
    fcopies = []
    width = 512
    per = width // PTS
    for n in range(share // width):
        cols = slice(n * width, (n + 1) * width)
        zcol = zb[:, cols]
        total = None
        for i in range(4):
            u = tn(w1[i], zcol)
            h = (u * sigmoid(u)).astype(BF16)
            part = tn(w2[i], h)
            total = part if total is None else total + part
        if n == 0:
            for copy in acopies:
                copy.wait()
        acol = (ab[:, cols].astype(F32) + total).astype(BF16)
        al[:, cols] = acol
        fx[n * per : (n + 1) * per] = tn(acol, wf[...]).astype(BF16).reshape(per, PTS, PTS)
        for d in (2, 1, 3):
            to = (c + d) % 4
            part = pl.ds(pl.multiple_of(quarter * to, quarter), quarter)
            fcopies.append(
                send(
                    fx.at[n * per : (n + 1) * per, part, :],
                    fp.at[pl.ds(c * (share // PTS) + n * per, per)],
                    fs.at[n, d], fr.at[n, d], b, to,
                )
            )
    part = pl.ds(pl.multiple_of(quarter * c, quarter), quarter)
    fp[pl.ds(c * (share // PTS), share // PTS)] = fx[:, part, :]
    for copy in fcopies:
        copy.wait()


def ocean_kernel(
    inv, slot, fp, mask, ct, wo_one, wo_two, state_all, cot_all,
    dstate, dfp, ctb, go1, go2,
    cts, fm, sp, rf, bk, rb, st, ctv, wa, wb, perm,
    lsem, cs, cr, ws, wr, ss, sr, rs, rr,
):
    b, c, mate, across, diag = place()
    bands = lax.axis_size("band")
    q, z = b // ZLEN, b % ZLEN
    groups = bands // ZLEN
    quarter = st.shape[0]
    blocks = fp.shape[0]
    rows, points = ct.shape
    share = ctb.shape[1]

    def greet(i, _):
        signal((b + i) % bands, c)
        return 0

    lax.fori_loop(1, bands, greet, 0)
    for d in (1, 2, 3):
        signal(b, (c + d) % 4)
    loads = []
    for i, (src, dst) in enumerate(((state_all, st), (cot_all, ctv))):
        loads.append(
            pltpu.make_async_copy(
                src.at[pl.ds(pl.multiple_of(quarter * c, quarter), quarter), 0], dst, lsem.at[i]
            )
        )
        loads[-1].start()
    fm[:blocks] = fp[...] * mask[...]
    fm[blocks] = jnp.zeros(fm.shape[1:], BF16)

    def pack(s, _):
        sp[s] = fm[inv[s]]
        return 0

    lax.fori_loop(0, 2 * bands, pack, 0)
    pl.semaphore_wait(pltpu.get_barrier_semaphore(), bands - 1 + 3)

    def couple(i, _):
        d = i // ZLEN
        to = ((q + d) % groups) * ZLEN + (z + i % ZLEN) % ZLEN
        send(sp.at[pl.ds(2 * to, 2)], rf.at[pl.ds(2 * b, 2)], ss, sr.at[d], to, c)
        return 0

    lax.fori_loop(1, bands, couple, 0)
    wide = wo_one.shape[1]
    mine_wide = pl.ds(pl.multiple_of(c * wide, wide), wide)
    mine = pl.ds(pl.multiple_of(c * rows, rows), rows)
    copies, late = [], []
    cts[:, :points] = ct[...]
    cts[:, points:] = jnp.zeros((rows, cts.shape[1] - points), BF16)
    for d in (2, 1, 3):
        to = (c + d) % 4
        copies.append(send(wo_one, wa.at[:, mine_wide], ws.at[0, d], wr.at[0, d], b, to))
        copies.append(send(wo_two, wb.at[mine_wide, :], ws.at[1, d], wr.at[1, d], b, to))
    for d in (2, 1, 3):
        to = (c + d) % 4
        cols = pl.ds(pl.multiple_of(share * to, share), share)
        late.append(send(cts.at[:, cols], ctb.at[mine, :], cs.at[d], cr.at[d], b, to))
    wa[:, mine_wide] = wo_one[...]
    wb[mine_wide, :] = wo_two[...]
    ctb[mine, :] = cts[:, pl.ds(pl.multiple_of(share * c, share), share)]
    rf[pl.ds(2 * b, 2)] = sp[pl.ds(2 * b, 2)]
    span = 2 * ZLEN
    size = span * quarter
    r = lax.broadcasted_iota(jnp.int32, (size, size), 0)
    k = lax.broadcasted_iota(jnp.int32, (size, size), 1)
    perm[...] = jnp.where((r % span) * quarter + r // span == k, 1.0, 0.0).astype(BF16)
    go1[...] = jnp.zeros(go1.shape, F32)
    go2[...] = jnp.zeros(go2.shape, F32)
    for load in loads:
        load.wait()
    for copy in copies:
        copy.wait()
    drain(rf.at[pl.ds(0, span - 2)], sr.at[0])

    def step(d, _):
        @pl.when(d > 0)
        def _():
            drain(rf.at[pl.ds(0, span)], sr.at[d])

        src = (q + groups - d) % groups
        at = pl.ds(pl.multiple_of(src * span, span), span)
        force = nn(perm[...], rf[at].reshape(size, PTS)).astype(BF16)
        both = jnp.concatenate([st[:, at, :].reshape(size, PTS), force], axis=1)
        cot = ctv[:, at, :].reshape(size, PTS)
        pre = nn(both, wa[...])
        sig = sigmoid(pre)
        act = pre * sig
        grad = (nt(cot, wb[...]) * (sig + act * (1.0 - sig))).astype(BF16)
        go2[...] += tn(cot, act.astype(BF16))
        go1[...] += tn(both, grad)
        back = nt(grad, wa[...])
        dstate[:, at, :] = (
            (cot.astype(F32) + back[:, :PTS]).astype(BF16).reshape(quarter, span, PTS)
        )
        bk[at] = tn(perm[...], back[:, PTS:].astype(BF16)).astype(BF16).reshape(span, quarter, PTS)

        def give(i, _):
            @pl.when(d + i > 0)
            def _():
                to = src * ZLEN + (z + i) % ZLEN
                send(bk.at[pl.ds(2 * to, 2)], rb.at[pl.ds(2 * b, 2)], rs, rr, to, c)

            return 0

        lax.fori_loop(0, ZLEN, give, 0)
        return 0

    lax.fori_loop(0, groups, step, 0)
    rb[pl.ds(2 * b, 2)] = bk[pl.ds(2 * b, 2)]
    drain(sp.at[pl.ds(0, 2 * bands - 2)], ss)
    drain(bk.at[pl.ds(0, 2 * bands - 2)], rs)
    drain(rb.at[pl.ds(0, 2 * bands - 2)], rr)

    def unpack(k, _):
        dfp[k] = rb[slot[k]] * mask[k]
        return 0

    lax.fori_loop(0, blocks, unpack, 0)
    for copy in late:
        copy.wait()


def backward_kernel(
    dfp, zb, al, ctb, w1, w2, wf, ext, taps,
    datmos, gw1, gw2, gwf, gk,
    dfb, hid, slope, gb, gc, dzb, dzc, dext,
    ds_, dr, gs, gr, zs, zr, hs, hr,
):
    b, c, mate, across, diag = place()
    bands = lax.axis_size("band")
    up, down = (b + bands - 1) % bands, (b + 1) % bands
    rows, points = datmos.shape
    share = zb.shape[1]
    own_blocks = share // PTS
    quarter = dfp.shape[1]
    signal(up, c)
    signal(down, c)
    for d in (1, 2, 3):
        signal(b, (c + d) % 4)
    pl.semaphore_wait(pltpu.get_barrier_semaphore(), 5)
    part = pl.ds(pl.multiple_of(quarter * c, quarter), quarter)
    dcopies = []
    for d in (2, 1, 3):
        to = (c + d) % 4
        dcopies.append(
            send(
                dfp.at[pl.ds(own_blocks * to, own_blocks)], dfb.at[:, part, :],
                ds_.at[d], dr.at[d], b, to,
            )
        )
    dfb[:, part, :] = dfp[pl.ds(own_blocks * c, own_blocks)]
    width = 512
    for n in range(share // width):
        cols = slice(n * width, (n + 1) * width)
        for i in range(4):
            u = tn(w1[i], zb[:, cols])
            sig = sigmoid(u)
            act = u * sig
            hid[i, :, cols] = act.astype(BF16)
            slope[i, :, cols] = sig + act * (1.0 - sig)
    for copy in dcopies:
        copy.wait()
    flux = dfb[...].reshape(share, PTS)
    gwf[...] = nn(al[...], flux)
    gb[...] = (ctb[...].astype(F32) + nt(wf[...], flux)).astype(BF16)
    gcopies, zcopies = [], []
    lanes = pl.ds(pl.multiple_of(share * c, share), share)
    for d in (2, 1, 3):
        to = (c + d) % 4
        theirs = pl.ds(pl.multiple_of(rows * to, rows), rows)
        gcopies.append(send(gb.at[theirs, :], gc.at[:, lanes], gs.at[d], gr.at[d], b, to))
    mine = pl.ds(pl.multiple_of(rows * c, rows), rows)
    gc[:, lanes] = gb[mine, :]
    for n in range(share // width):
        cols = slice(n * width, (n + 1) * width)
        gcol = gb[:, cols]
        zcol = zb[:, cols]
        total = None
        for i in range(4):
            du = (nn(w2[i], gcol) * slope[i, :, cols]).astype(BF16)
            g2 = nt(hid[i, :, cols], gcol)
            g1 = nt(zcol, du)
            gw2[i] = g2 if n == 0 else gw2[i] + g2
            gw1[i] = g1 if n == 0 else gw1[i] + g1
            piece = nn(w1[i], du)
            total = piece if total is None else total + piece
        dzb[:, cols] = total.astype(BF16)
        for d in (2, 1, 3):
            to = (c + d) % 4
            theirs = pl.ds(pl.multiple_of(rows * to, rows), rows)
            at = pl.ds(pl.multiple_of(share * c + n * width, width), width)
            zcopies.append(
                send(dzb.at[theirs, cols], dzc.at[:, at], zs.at[n, d], zr.at[n, d], b, to)
            )
    dzc[:, lanes] = dzb[mine, :]
    for copy in zcopies:
        copy.wait()
    halo = [
        send(dzc.at[:, points - share : points], dext.at[:, :share], hs.at[0], hr.at[0], down, c),
        send(dzc.at[:, :share], dext.at[:, share + points :], hs.at[1], hr.at[1], up, c),
    ]
    dext[:, share : share + points] = dzc[:, :points]
    width = 384
    low = share - LON
    high = share + LON
    sums = [jnp.zeros((rows, 128), F32) for _ in range(3)]
    for at in range(0, points, width):
        grad = dzc[:, at : at + width].astype(F32)
        views = (
            shifted(ext, at + low // 128 * 128, low % 128, width),
            ext[:, at + share : at + share + width].astype(F32),
            shifted(ext, at + high // 128 * 128, high % 128, width),
        )
        for i in range(3):
            prod = views[i] * grad
            for o in range(0, width, 128):
                sums[i] = sums[i] + prod[:, o : o + 128]
    lane = lax.broadcasted_iota(jnp.int32, (rows, 128), 1)
    whole = [jnp.sum(s, axis=1, keepdims=True) for s in sums]
    gk[...] = jnp.where(
        lane == 0, whole[0], jnp.where(lane == 1, whole[1], jnp.where(lane == 2, whole[2], 0.0))
    )
    for copy in gcopies:
        copy.wait()
    for copy in halo:
        copy.wait()

    @pl.when(b == 0)
    def _():
        dext[:, :share] = jnp.zeros((rows, share), BF16)

    @pl.when(b == bands - 1)
    def _():
        dext[:, share + points :] = jnp.zeros((rows, share), BF16)

    t0, t1, t2 = taps[:, 0:1], taps[:, 1:2], taps[:, 2:3]
    for at in range(0, points, width):
        datmos[:, at : at + width] = (
            gc[:, at : at + width].astype(F32)
            + t0 * shifted(dext, at + high // 128 * 128, high % 128, width)
            + t1 * dext[:, at + share : at + share + width].astype(F32)
            + t2 * shifted(dext, at + low // 128 * 128, low % 128, width)
        ).astype(BF16)


def reduce_kernel(
    gw1, gw2, gwf, gk, go1, go2,
    dw1, dw2, dwf, dk, do1, do2,
    gs, ra, rx, hx, own, t, r1, fs, r2, fr, ag, tb, out,
    s0, q0, s1, q1, s2, q2, s3, q3, s4, q4,
):
    b, c, mate, across, diag = place()
    bands = lax.axis_size("band")
    q, z = b // ZLEN, b % ZLEN
    groups = bands // ZLEN
    for d in (1, 2, 3):
        signal(b, (c + d) % 4)
    for d in range(1, groups):
        signal(((q + d) % groups) * ZLEN + z, c)
    for d in range(1, ZLEN):
        signal(q * ZLEN + (z + d) % ZLEN, c)
    for i in range(4):
        for j in range(2):
            gs[i, j * 256 : j * 256 + 256] = gw1[i, :, j * 128 : j * 128 + 128].astype(BF16)
            gs[i, 512 + j * 256 : 768 + j * 256] = gw2[i, :, j * 128 : j * 128 + 128].astype(BF16)
        gs[i, 1024:1280] = go1[:, i * 128 : i * 128 + 128].astype(BF16)
        gs[i, 1280:1408] = go2[:, i * 128 : i * 128 + 128].astype(BF16)
        gs[i, 1408:1472] = gwf[i * 64 : i * 64 + 64, :].astype(BF16)
        gs[i, 1472:1536] = jnp.zeros((64, 128), BF16)
    gs[c, 1472:1536] = gk[...].astype(BF16)
    pl.semaphore_wait(pltpu.get_barrier_semaphore(), 3 + groups - 1 + ZLEN - 1)
    ca = send(gs.at[diag], ra.at[1], s0.at[1], q0.at[1], b, mate)
    cb = send(gs.at[mate], ra.at[0], s0.at[0], q0.at[0], b, mate)
    ca.wait()
    hx[...] = (gs[across].astype(F32) + ra[1].astype(F32)).astype(BF16)
    cc = send(hx, rx, s0.at[2], q0.at[2], b, across)
    cb.wait()
    own[...] = gs[c].astype(F32) + ra[0].astype(F32)
    cc.wait()
    size = t.shape[1]
    for i in range(groups):
        rows = slice(i * size, (i + 1) * size)
        t[i] = (own[rows] + rx[rows].astype(F32)).astype(BF16)
    copies = []
    for d in range(1, groups):
        to = (q + d) % groups
        copies.append(send(t.at[to], r1.at[q], s1.at[d], q1.at[d], to * ZLEN + z, c))
    r1[q] = t[q]
    for copy in copies:
        copy.wait()
    total = r1[0].astype(F32)
    for i in range(1, groups):
        total = total + r1[i].astype(F32)
    fs[...] = total.reshape(fs.shape)
    copies = []
    for d in range(1, ZLEN):
        to = (z + d) % ZLEN
        copies.append(send(fs.at[to], r2.at[z], s2.at[d], q2.at[d], q * ZLEN + to, c))
    r2[z] = fs[z]
    for copy in copies:
        copy.wait()
    total = r2[0]
    for i in range(1, ZLEN):
        total = total + r2[i]
    fr[...] = total
    copies = []
    for d in range(1, ZLEN):
        to = (z + d) % ZLEN
        copies.append(send(fr, ag.at[z], s3.at[d], q3.at[d], q * ZLEN + to, c))
    ag[z] = total
    for copy in copies:
        copy.wait()
    tb[...] = ag[...].reshape(size, 128).astype(BF16)
    copies = []
    for d in range(1, groups):
        to = (q + d) % groups
        copies.append(send(tb, out.at[q], s4.at[d], q4.at[d], to * ZLEN + z, c))
    out[q] = tb[...]
    for copy in copies:
        copy.wait()
    flat = out[...].reshape(groups * size, 128).astype(F32)
    for j in range(2):
        dw1[:, j * 128 : j * 128 + 128] = flat[j * 256 : j * 256 + 256]
        dw2[:, j * 128 : j * 128 + 128] = flat[512 + j * 256 : 768 + j * 256]
    do1[...] = flat[1024:1280]
    do2[...] = flat[1280:1408].T
    dwf[...] = flat[1408:1472]
    dk[...] = flat[1472:1536]


def call(body, ident, outs, scratch, args, specs):
    return pl.pallas_call(
        body,
        out_shape=[jax.ShapeDtypeStruct(s, t) for s, t in outs],
        in_specs=specs,
        out_specs=[pl.BlockSpec(memory_space=VMEM)] * len(outs),
        scratch_shapes=scratch,
        compiler_params=pltpu.CompilerParams(
            collective_id=ident, has_side_effects=True, vmem_limit_bytes=LIMIT
        ),
    )(*args)


def local(
    atmos, kernels, w_one, w_two, w_flux, sea_mask, route,
    ocean_state, ct_atmos, ct_ocean, wo_one, wo_two,
):
    c = lax.axis_index("chan")
    chans = lax.axis_size("chan")
    bands = lax.axis_size("band")
    rows, points = atmos.shape
    blocks = points // PTS
    own_blocks = -(-blocks // chans)
    share = own_blocks * PTS
    padded = own_blocks * chans
    quarter = PTS // chans
    slots = ocean_state.shape[2]
    hid = w_one.shape[2]
    full = rows * chans
    whole = hid * chans
    wide = wo_one.shape[1]
    total = wide * chans
    vm = pl.BlockSpec(memory_space=VMEM)
    sm = pl.BlockSpec(memory_space=pltpu.SMEM)
    anywhere = pl.BlockSpec(memory_space=pl.ANY)

    target = route[:, 0]
    order = jnp.arange(blocks, dtype=jnp.int32)
    earlier = (target[None, :] == target[:, None]) & (order[None, :] < order[:, None])
    slot_of = target * (slots // bands) + jnp.sum(earlier.astype(jnp.int32), axis=1)
    hit = slot_of[:, None] == jnp.arange(slots, dtype=jnp.int32)[None, :]
    inv = padded + jnp.sum(jnp.where(hit, order[:, None] - padded, 0), axis=0)
    slot_of = jnp.pad(slot_of, (0, padded - blocks))
    mask = lax.dynamic_slice_in_dim(sea_mask.reshape(blocks, PTS), c * quarter, quarter, 1)
    mask = jnp.pad(mask.astype(BF16), ((0, padded - blocks), (0, 0)))
    mask = jnp.broadcast_to(mask[:, :, None], (padded, quarter, PTS))
    taps = kernels[0].T

    ext, zb, al, w1, w2, wf, fp = call(
        forward_kernel, 0,
        [
            ((rows, points + 2 * share), BF16),
            ((full, share), BF16),
            ((full, share), BF16),
            ((chans, full, hid), BF16),
            ((chans, hid, full), BF16),
            ((full, PTS), BF16),
            ((padded, quarter, PTS), BF16),
        ],
        [
            VMEM((rows, padded * PTS), BF16),
            VMEM((full, share), BF16),
            VMEM((own_blocks, PTS, PTS), BF16),
            DMA((2,)), DMA((2,)), DMA((3, 3)), DMA((3, 3)), DMA((4,)), DMA((4,)),
            DMA((4,)), DMA((4,)), DMA((3, 4)), DMA((3, 4)),
        ],
        (atmos, taps, w_one[0], w_two[0], w_flux),
        [vm] * 5,
    )
    dstate, dfp, ctb, go1, go2 = call(
        ocean_kernel, 1,
        [
            ((quarter, slots, PTS), BF16),
            ((padded, quarter, PTS), BF16),
            ((full, share), BF16),
            ((2 * PTS, total), F32),
            ((PTS, total), F32),
        ],
        [
            VMEM((rows, padded * PTS), BF16),
            VMEM((padded + 1, quarter, PTS), BF16),
            VMEM((slots, quarter, PTS), BF16),
            VMEM((slots, quarter, PTS), BF16),
            VMEM((slots, quarter, PTS), BF16),
            VMEM((slots, quarter, PTS), BF16),
            VMEM((quarter, slots, PTS), BF16),
            VMEM((quarter, slots, PTS), BF16),
            VMEM((2 * PTS, total), BF16),
            VMEM((total, PTS), BF16),
            VMEM((2 * ZLEN * quarter, 2 * ZLEN * quarter), BF16),
            DMA((2,)), DMA((4,)), DMA((4,)), DMA((2, 4)), DMA((2, 4)),
            DMA, DMA((bands // ZLEN,)), DMA, DMA,
        ],
        (inv, slot_of, fp, mask, ct_atmos, wo_one, wo_two, ocean_state, ct_ocean),
        [sm, sm, vm, vm, vm, vm, vm, anywhere, anywhere],
    )
    datmos, gw1, gw2, gwf, gk = call(
        backward_kernel, 2,
        [
            ((rows, points), BF16),
            ((chans, full, hid), F32),
            ((chans, hid, full), F32),
            ((full, PTS), F32),
            ((rows, 128), F32),
        ],
        [
            VMEM((own_blocks, PTS, PTS), BF16),
            VMEM((chans, hid, share), BF16),
            VMEM((chans, hid, share), F32),
            VMEM((full, share), BF16),
            VMEM((rows, padded * PTS), BF16),
            VMEM((full, share), BF16),
            VMEM((rows, padded * PTS), BF16),
            VMEM((rows, points + 2 * share), BF16),
            DMA((4,)), DMA((4,)), DMA((4,)), DMA((4,)), DMA((3, 4)), DMA((3, 4)),
            DMA((2,)), DMA((2,)),
        ],
        (dfp, zb, al, ctb, w1, w2, wf, ext, taps),
        [vm] * 9,
    )
    groups = bands // ZLEN
    flat = 1536
    size = flat // groups
    small = size // ZLEN
    dw1, dw2, dwf, dk, do1, do2 = call(
        reduce_kernel, 3,
        [
            ((full, hid), F32),
            ((hid, full), F32),
            ((rows, PTS), F32),
            ((rows, 128), F32),
            ((2 * PTS, wide), F32),
            ((wide, PTS), F32),
        ],
        [
            VMEM((4, flat, 128), BF16),
            VMEM((2, flat, 128), BF16),
            VMEM((flat, 128), BF16),
            VMEM((flat, 128), BF16),
            VMEM((flat, 128), F32),
            VMEM((groups, size, 128), BF16),
            VMEM((groups, size, 128), BF16),
            VMEM((ZLEN, small, 128), F32),
            VMEM((ZLEN, small, 128), F32),
            VMEM((small, 128), F32),
            VMEM((ZLEN, small, 128), F32),
            VMEM((size, 128), BF16),
            VMEM((groups, size, 128), BF16),
            DMA((3,)), DMA((3,)), DMA((groups,)), DMA((groups,)), DMA((ZLEN,)), DMA((ZLEN,)),
            DMA((ZLEN,)), DMA((ZLEN,)), DMA((groups,)), DMA((groups,)),
        ],
        (gw1, gw2, gwf, gk, go1, go2),
        [vm] * 6,
    )
    return (
        datmos, dk[:, :3].T[None], dw1[None], dw2[None], dwf, dstate[:, None], do1, do2,
    )


def solution(mesh):
    in_specs = (
        P("chan", "band"),
        P(None, None, "chan"),
        P(None, None, "chan"),
        P(None, "chan", None),
        P("chan", None),
        P("band"),
        P("band", None),
        P(None, "band", None, None),
        P("chan", "band"),
        P(None, "band", None, None),
        P(None, "chan"),
        P("chan", None),
    )
    out_specs = (
        P("chan", "band"),
        P(None, None, "chan"),
        P(None, None, "chan"),
        P(None, "chan", None),
        P("chan", None),
        P("chan", "band", None, None),
        P(None, "chan"),
        P("chan", None),
    )
    return jax.shard_map(local, mesh=mesh, in_specs=in_specs, out_specs=out_specs, check_vma=False)
```

```python
import functools

import jax
import jax.numpy as jnp
from jax import lax
from jax.experimental import pallas as pl
from jax.experimental.pallas import tpu as pltpu
from jax.sharding import PartitionSpec as P

PTS = 128
LON = 1440
MESH = pl.DeviceIdType.MESH
F32 = jnp.float32
BF16 = jnp.bfloat16
VMEM = pltpu.VMEM
DMA = pltpu.SemaphoreType.DMA
ZLEN = 8
LIMIT = 56 * 1024 * 1024


def nn(a, b):
    return lax.dot_general(a, b, (((1,), (0,)), ((), ())), preferred_element_type=F32)


def tn(a, b):
    return lax.dot_general(a, b, (((0,), (0,)), ((), ())), preferred_element_type=F32)


def nt(a, b):
    return lax.dot_general(a, b, (((1,), (1,)), ((), ())), preferred_element_type=F32)


def sigmoid(v):
    return 0.5 * jnp.tanh(0.5 * v) + 0.5


def place():
    b, c = lax.axis_index("band"), lax.axis_index("chan")
    mate = (c // 2) * 2 + (1 - c % 2)
    return b, c, mate, (c + 2) % 4, (mate + 2) % 4


def send(src, dst, ssem, rsem, b, c):
    copy = pltpu.make_async_remote_copy(
        src_ref=src,
        dst_ref=dst,
        send_sem=ssem,
        recv_sem=rsem,
        device_id=(b, c),
        device_id_type=MESH,
    )
    copy.start()
    return copy


def drain(ref, sem):
    pltpu.make_async_copy(ref, ref, sem).wait()


def signal(b, c):
    pl.semaphore_signal(
        pltpu.get_barrier_semaphore(), inc=1, device_id=(b, c), device_id_type=MESH
    )


def shifted(ref, start, extra, width):
    wide = ref[:, start : start + width + 128].astype(F32)
    return pltpu.roll(wide, width + 128 - extra, axis=1)[:, :width]


def table_kernel(route, table):
    blocks = route.shape[0]
    col = route[...]
    k = lax.broadcasted_iota(jnp.int32, (blocks, blocks), 0)
    j = lax.broadcasted_iota(jnp.int32, (blocks, blocks), 1)
    row = jnp.sum(jnp.where(k == j, col, 0), axis=0, keepdims=True)
    rank = jnp.sum(jnp.where((row == col) & (j < k), 1, 0), axis=1, keepdims=True)
    slot = col * 2 + rank
    k = lax.broadcasted_iota(jnp.int32, (blocks, 128), 0)
    s = lax.broadcasted_iota(jnp.int32, (blocks, 128), 1)
    empty = 48
    inv = empty + jnp.sum(jnp.where(slot == s, k - empty, 0), axis=0, keepdims=True)
    back = jnp.sum(jnp.where(k == s, slot, 0), axis=0, keepdims=True)
    line = lax.broadcasted_iota(jnp.int32, (8, 128), 0)
    table[...] = jnp.where(line == 0, inv, back)


def finish_kernel(dat, dst, out, gk, datmos, dk, dw1, dw2, dwf, dstate, do1, do2):
    datmos[...] = dat[...]
    dstate[...] = dst[...]
    for j in range(2):
        dw1[:, j * 128 : j * 128 + 128] = out[j * 256 : j * 256 + 256].astype(F32)
        dw2[:, j * 128 : j * 128 + 128] = out[512 + j * 256 : 768 + j * 256].astype(F32)
    dwf[...] = out[1024:1088].astype(F32)
    do1[...] = out[1152:1408].astype(F32)
    do2[...] = out[1408:1536].astype(F32).T
    dk[...] = gk[:3, :64]


def main_kernel(
    table, atmos, taps, w_one, w_two, w_flux, sea, wo_one, wo_two, ct_all, state_all, cot_all,
    dat, dst, out, gkout,
    ext, a0, zc, zb, ab, alm, w1, w2, wf, fx, fm, mk, hid, slope,
    cts, ctb, sp, rf, bk, rb, st, ctv, ds, wa, wb, perm, go1, go2,
    dfp, dfb, gb, gc, dzb, dzc, dext, dzacc, dubuf, gwf,
    gs, ra, hx, rx, gso, rao, hxo, rxo, own, owno, t, r1, fs, r2, fr, ag, tb, gkt, gkr,
    lsem, hs, hr, ws, wr, as_, ar, zs, zr, fxs, fxr, cs, cr, ss, sr, rs, rr,
    os_, or_, dfs, dfr, gsd, grd, dzs, dzr, h2s, h2r, s0, q0, s1, q1, s2, q2, s3, q3, s4, q4, ks, kr,
):
    b, c, mate, across, diag = place()
    bands = lax.axis_size("band")
    up, down = (b + bands - 1) % bands, (b + 1) % bands
    q, z = b // ZLEN, b % ZLEN
    groups = bands // ZLEN
    flip = ((q // 2) * 2 + (1 - q % 2)) * ZLEN + z
    rows, points = atmos.shape
    share = zb.shape[1]
    own_blocks = share // PTS
    quarter = st.shape[0]
    blocks = dfp.shape[0]
    wide = wo_one.shape[1]
    peers = [(c + 2) % 4, (c + 1) % 4, (c + 3) % 4]
    ds_of = (2, 1, 3)

    def greet(i, _):
        signal((b + i) % bands, c)
        return 0

    lax.fori_loop(1, bands, greet, 0)
    for d in (1, 2, 3):
        signal(b, (c + d) % 4)
    signal(flip, across)
    loads = [
        pltpu.make_async_copy(ct_all, cts.at[:, :points], lsem.at[0]),
        pltpu.make_async_copy(
            state_all.at[pl.ds(pl.multiple_of(quarter * c, quarter), quarter), 0], st, lsem.at[1]
        ),
        pltpu.make_async_copy(
            cot_all.at[pl.ds(pl.multiple_of(quarter * c, quarter), quarter), 0], ctv, lsem.at[2]
        ),
    ]
    for load in loads:
        load.start()
    mine = pl.ds(pl.multiple_of(c * rows, rows), rows)
    lanes = pl.ds(pl.multiple_of(share * c, share), share)
    part = pl.ds(pl.multiple_of(quarter * c, quarter), quarter)
    a0[:, :points] = atmos[...]
    a0[:, points:] = jnp.zeros((rows, a0.shape[1] - points), BF16)
    pl.semaphore_wait(pltpu.get_barrier_semaphore(), bands - 1 + 4)

    halo = [
        send(atmos.at[:, points - share :], ext.at[:, :share], hs.at[0], hr.at[0], down, c),
        send(atmos.at[:, :share], ext.at[:, share + points :], hs.at[1], hr.at[1], up, c),
    ]
    acopies = []
    for d, to in zip(ds_of, peers):
        cols = pl.ds(pl.multiple_of(share * to, share), share)
        acopies.append(send(a0.at[:, cols], ab.at[mine, :], as_.at[d], ar.at[d], b, to))
    mine_wide = pl.ds(pl.multiple_of(c * wide, wide), wide)
    theirs = pl.ds(pl.multiple_of(across * rows, rows), rows)
    theirs_wide = pl.ds(pl.multiple_of(across * wide, wide), wide)
    sources = (w_one, w_two, w_flux, wo_one, wo_two)
    near = (w1.at[c], w2.at[c], wf.at[mine, :], wa.at[:, mine_wide], wb.at[mine_wide, :])
    far = (
        w1.at[across], w2.at[across], wf.at[theirs, :],
        wa.at[:, theirs_wide], wb.at[theirs_wide, :],
    )
    first, second, third = [], [], []
    for i in range(5):
        second.append(send(sources[i], near[i], ws.at[1, i], wr.at[1, i], flip, across))
        first.append(send(sources[i], near[i], ws.at[0, i], wr.at[0, i], b, mate))
    w1[c] = w_one[...]
    w2[c] = w_two[...]
    wf[mine, :] = w_flux[...]
    wa[:, mine_wide] = wo_one[...]
    wb[mine_wide, :] = wo_two[...]
    ext[:, share : share + points] = atmos[...]
    zc[:, points:] = jnp.zeros((rows, zc.shape[1] - points), BF16)
    cts[:, points:] = jnp.zeros((rows, cts.shape[1] - points), BF16)
    mk[:, :points] = sea[...].astype(F32)
    mk[:, points:] = jnp.zeros((1, mk.shape[1] - points), F32)
    ab[mine, :] = a0[:, lanes]
    eye = lax.broadcasted_iota(jnp.int32, (rows, rows), 0) == lax.broadcasted_iota(
        jnp.int32, (rows, rows), 1
    )
    t0, t1, t2 = [
        jnp.sum(jnp.where(eye, taps[i : i + 1, :], 0.0), axis=1, keepdims=True) for i in range(3)
    ]
    for copy in halo:
        copy.wait()

    @pl.when(b == 0)
    def _():
        ext[:, :share] = jnp.zeros((rows, share), BF16)

    @pl.when(b == bands - 1)
    def _():
        ext[:, share + points :] = jnp.zeros((rows, share), BF16)

    width = 384
    low = share - LON
    high = share + LON
    for at in range(0, points, width):
        zc[:, at : at + width] = (
            t0 * shifted(ext, at + low // 128 * 128, low % 128, width)
            + t1 * ext[:, at + share : at + share + width].astype(F32)
            + t2 * shifted(ext, at + high // 128 * 128, high % 128, width)
        ).astype(BF16)
    width = 512
    steps = share // width
    per = width // PTS
    zcopies = []
    for n in range(steps):
        for d, to in zip(ds_of, peers):
            cols = pl.ds(pl.multiple_of(share * to + n * width, width), width)
            zcopies.append(
                send(
                    zc.at[:, cols], zb.at[mine, n * width : (n + 1) * width],
                    zs.at[n, d], zr.at[n, d], b, to,
                )
            )
    zb[mine, :] = zc[:, lanes]
    for i in range(5):
        second[i].wait_recv()
        third.append(send(far[i], far[i], ws.at[2, i], wr.at[2, i], b, mate))
    for i in range(3):
        first[i].wait()
        second[i].wait_send()
        third[i].wait()
    own_mask = mk[:, lanes]
    fcopies = []
    for n in range(steps):
        cols = slice(n * width, (n + 1) * width)
        for copy in zcopies[3 * n : 3 * n + 3]:
            copy.wait()
        zcol = zb[:, cols]
        total = None
        for i in range(4):
            u = tn(w1[i], zcol)
            sig = sigmoid(u)
            act = u * sig
            h = act.astype(BF16)
            hid[i, :, cols] = h
            slope[i, :, cols] = (sig + act * (1.0 - sig)).astype(BF16)
            piece = tn(w2[i], h)
            total = piece if total is None else total + piece
        if n == 0:
            for copy in acopies:
                copy.wait()
        acol = (ab[:, cols].astype(F32) + total).astype(BF16)
        acol = (acol.astype(F32) * own_mask[:, cols]).astype(BF16)
        alm[:, cols] = acol
        fx[n * per : (n + 1) * per] = tn(acol, wf[...]).astype(BF16).reshape(per, PTS, PTS)
        for d, to in zip(ds_of, peers):
            piece = pl.ds(pl.multiple_of(quarter * to, quarter), quarter)
            fcopies.append(
                send(
                    fx.at[n * per : (n + 1) * per, piece, :],
                    fm.at[pl.ds(c * own_blocks + n * per, per)],
                    fxs.at[n, d], fxr.at[n, d], b, to,
                )
            )
    fm[pl.ds(c * own_blocks, own_blocks)] = fx[:, part, :]
    fm[blocks] = jnp.zeros(fm.shape[1:], BF16)
    span = 2 * ZLEN
    size = span * quarter
    r = lax.broadcasted_iota(jnp.int32, (size, size), 0)
    k = lax.broadcasted_iota(jnp.int32, (size, size), 1)
    perm[...] = jnp.where((r % span) * quarter + r // span == k, 1.0, 0.0).astype(BF16)
    go1[...] = jnp.zeros(go1.shape, F32)
    go2[...] = jnp.zeros(go2.shape, F32)
    for load in loads:
        load.wait()
    for i in range(3, 5):
        first[i].wait()
        second[i].wait_send()
        third[i].wait()
    for copy in fcopies:
        copy.wait()

    def pack(s, _):
        sp[s] = fm[table[0, s]]
        return 0

    lax.fori_loop(0, 2 * bands, pack, 0)

    def couple(i, _):
        d = i // ZLEN
        to = ((q + d) % groups) * ZLEN + (z + i % ZLEN) % ZLEN
        send(sp.at[pl.ds(2 * to, 2)], rf.at[pl.ds(2 * b, 2)], ss, sr.at[d], to, c)
        return 0

    lax.fori_loop(1, bands, couple, 0)
    ctcopies = []
    for d, to in zip(ds_of, peers):
        cols = pl.ds(pl.multiple_of(share * to, share), share)
        ctcopies.append(send(cts.at[:, cols], ctb.at[mine, :], cs.at[d], cr.at[d], b, to))
    ctb[mine, :] = cts[:, lanes]
    rf[pl.ds(2 * b, 2)] = sp[pl.ds(2 * b, 2)]
    drain(rf.at[pl.ds(0, span - 2)], sr.at[0])

    def step(d, _):
        @pl.when(d > 0)
        def _():
            drain(rf.at[pl.ds(0, span)], sr.at[d])

        src = (q + groups - d) % groups
        at = pl.ds(pl.multiple_of(src * span, span), span)
        force = nn(perm[...], rf[at].reshape(size, PTS)).astype(BF16)
        both = jnp.concatenate([st[:, at, :].reshape(size, PTS), force], axis=1)
        cot = ctv[:, at, :].reshape(size, PTS)
        pre = nn(both, wa[...])
        sig = sigmoid(pre)
        act = pre * sig
        grad = (nt(cot, wb[...]) * (sig + act * (1.0 - sig))).astype(BF16)
        back = nt(grad, wa[...])
        bk[at] = tn(perm[...], back[:, PTS:].astype(BF16)).astype(BF16).reshape(span, quarter, PTS)

        def give(i, _):
            @pl.when(d + i > 0)
            def _():
                to = src * ZLEN + (z + i) % ZLEN
                send(bk.at[pl.ds(2 * to, 2)], rb.at[pl.ds(2 * b, 2)], rs, rr, to, c)

            return 0

        lax.fori_loop(0, ZLEN, give, 0)
        ds[:, at, :] = (
            (cot.astype(F32) + back[:, :PTS]).astype(BF16).reshape(quarter, span, PTS)
        )
        go2[...] += tn(cot, act.astype(BF16))
        go1[...] += tn(both, grad)
        return 0

    lax.fori_loop(0, groups, step, 0)
    dstore = pltpu.make_async_copy(ds, dst, lsem.at[3])
    dstore.start()
    rb[pl.ds(2 * b, 2)] = bk[pl.ds(2 * b, 2)]
    for i in range(4):
        gso[i, :256] = go1[:, i * 128 : i * 128 + 128].astype(BF16)
        gso[i, 256:] = go2[:, i * 128 : i * 128 + 128].astype(BF16)
    ocopies = [
        send(gso.at[diag], rao.at[1], os_.at[1], or_.at[1], b, mate),
        send(gso.at[mate], rao.at[0], os_.at[0], or_.at[0], b, mate),
    ]
    for copy in ctcopies:
        copy.wait()
    drain(rb.at[pl.ds(0, 2 * bands - 2)], rr)

    def unpack(k, _):
        dfp[k] = rb[table[1, k]]
        return 0

    lax.fori_loop(0, blocks, unpack, 0)
    dcopies = []
    for d, to in zip(ds_of, peers):
        dcopies.append(
            send(
                dfp.at[pl.ds(own_blocks * to, own_blocks)], dfb.at[:, part, :],
                dfs.at[d], dfr.at[d], b, to,
            )
        )
    dfb[:, part, :] = dfp[pl.ds(own_blocks * c, own_blocks)]
    for copy in ocopies:
        copy.wait()
    hxo[...] = (gso[across].astype(F32) + rao[1].astype(F32)).astype(BF16)
    owno[...] = gso[c].astype(F32) + rao[0].astype(F32)
    ocopy = send(hxo, rxo, os_.at[2], or_.at[2], b, across)
    gs[:, 1088:] = jnp.zeros((4, 64, 128), BF16)
    for copy in dcopies:
        copy.wait()
    flux = dfb[...].reshape(share, PTS)
    gb[...] = (ctb[...].astype(F32) + nt(wf[...], flux) * own_mask).astype(BF16)
    gwf[...] = nn(alm[...], flux)
    wcopies = []
    for turn, i in enumerate((diag, mate, across, c)):
        for n in range(steps):
            cols = slice(n * width, (n + 1) * width)
            du = (nn(w2[i], gb[:, cols]) * slope[i, :, cols].astype(F32)).astype(BF16)
            dubuf[:, cols] = du
            piece = nn(w1[i], du)
            if turn == 0:
                dzacc[:, cols] = piece
            elif turn < 3:
                dzacc[:, cols] += piece
            else:
                dzb[:, cols] = (dzacc[:, cols] + piece).astype(BF16)
        g1 = nt(zb[...], dubuf[...])
        g2 = nt(hid[i], gb[...])
        for j in range(2):
            gs[i, j * 256 : j * 256 + 256] = g1[:, j * 128 : j * 128 + 128].astype(BF16)
            gs[i, 512 + j * 256 : 768 + j * 256] = g2[:, j * 128 : j * 128 + 128].astype(BF16)
        gs[i, 1024:1088] = gwf[pl.ds(pl.multiple_of(rows * i, rows), rows), :].astype(BF16)
        if turn == 0:
            wcopies.append(send(gs.at[diag], ra.at[1], s0.at[1], q0.at[1], b, mate))
        if turn == 1:
            wcopies.append(send(gs.at[mate], ra.at[0], s0.at[0], q0.at[0], b, mate))
        if turn == 2:
            wcopies[0].wait()
            hx[...] = (gs[across].astype(F32) + ra[1].astype(F32)).astype(BF16)
            wcopies.append(send(hx, rx, s0.at[2], q0.at[2], b, across))
    dzcopies, gcopies = [], []
    for d, to in zip(ds_of, peers):
        theirs = pl.ds(pl.multiple_of(rows * to, rows), rows)
        dzcopies.append(send(dzb.at[theirs, :], dzc.at[:, lanes], dzs.at[d], dzr.at[d], b, to))
    for d, to in zip(ds_of, peers):
        theirs = pl.ds(pl.multiple_of(rows * to, rows), rows)
        gcopies.append(send(gb.at[theirs, :], gc.at[:, lanes], gsd.at[d], grd.at[d], b, to))
    dzc[:, lanes] = dzb[mine, :]
    gc[:, lanes] = gb[mine, :]
    ocopy.wait()
    t[1152:] = (owno[...] + rxo[...].astype(F32)).astype(BF16)
    wcopies[1].wait()
    own[...] = gs[c].astype(F32) + ra[0].astype(F32)
    wcopies[2].wait()
    t[:1152] = (own[...] + rx[...].astype(F32)).astype(BF16)
    size = r1.shape[1]
    copies = []
    for d in range(1, groups):
        to = (q + d) % groups
        cut = pl.ds(pl.multiple_of(to * size, size), size)
        copies.append(send(t.at[cut], r1.at[q], s1.at[d], q1.at[d], to * ZLEN + z, c))
    r1[q] = t[pl.ds(pl.multiple_of(q * size, size), size)]
    for copy in copies:
        copy.wait()
    total = r1[0].astype(F32)
    for i in range(1, groups):
        total = total + r1[i].astype(F32)
    fs[...] = total.reshape(fs.shape)
    copies = []
    for d in range(1, ZLEN):
        to = (z + d) % ZLEN
        copies.append(send(fs.at[to], r2.at[z], s2.at[d], q2.at[d], q * ZLEN + to, c))
    r2[z] = fs[z]
    for copy in dzcopies:
        copy.wait()
    halo = [
        send(dzc.at[:, points - share : points], dext.at[:, :share], h2s.at[0], h2r.at[0], down, c),
        send(dzc.at[:, :share], dext.at[:, share + points :], h2s.at[1], h2r.at[1], up, c),
    ]
    for copy in copies:
        copy.wait()
    total = r2[0]
    for i in range(1, ZLEN):
        total = total + r2[i]
    fr[...] = total
    copies = []
    for d in range(1, ZLEN):
        to = (z + d) % ZLEN
        copies.append(send(fr, ag.at[z], s3.at[d], q3.at[d], q * ZLEN + to, c))
    ag[z] = total
    width = 384
    sums = [jnp.zeros((rows, 128), F32) for _ in range(3)]
    for at in range(0, points, width):
        grad = dzc[:, at : at + width].astype(F32)
        views = (
            shifted(ext, at + low // 128 * 128, low % 128, width),
            ext[:, at + share : at + share + width].astype(F32),
            shifted(ext, at + high // 128 * 128, high % 128, width),
        )
        for i in range(3):
            prod = views[i] * grad
            for o in range(0, width, 128):
                sums[i] = sums[i] + prod[:, o : o + 128]
    gkt[...] = jnp.zeros(gkt.shape, F32)
    for i in range(3):
        whole = jnp.sum(sums[i], axis=1, keepdims=True)
        gkt[i : i + 1, :rows] = jnp.sum(jnp.where(eye, whole, 0.0), axis=0, keepdims=True)

    def spread(i, _):
        send(gkt, gkr.at[b], ks, kr, (b + i) % bands, c)
        return 0

    lax.fori_loop(1, bands, spread, 0)
    gkr[b] = gkt[...]
    dext[:, share : share + points] = dzc[:, :points]
    for copy in copies:
        copy.wait()
    tb[...] = ag[...].reshape(size, 128).astype(BF16)
    copies = []
    for d in range(1, groups):
        to = (q + d) % groups
        cut = pl.ds(pl.multiple_of(q * size, size), size)
        copies.append(send(tb, out.at[cut], s4.at[d], q4.at[d], to * ZLEN + z, c))
    out[pl.ds(pl.multiple_of(q * size, size), size)] = tb[...]
    for copy in halo:
        copy.wait()

    @pl.when(b == 0)
    def _():
        dext[:, :share] = jnp.zeros((rows, share), BF16)

    @pl.when(b == bands - 1)
    def _():
        dext[:, share + points :] = jnp.zeros((rows, share), BF16)

    for copy in gcopies:
        copy.wait()
    for at in range(0, points, width):
        dat[:, at : at + width] = (
            gc[:, at : at + width].astype(F32)
            + t0 * shifted(dext, at + high // 128 * 128, high % 128, width)
            + t1 * dext[:, at + share : at + share + width].astype(F32)
            + t2 * shifted(dext, at + low // 128 * 128, low % 128, width)
        ).astype(BF16)
    drain(gkr.at[pl.ds(0, bands - 1)], kr)
    total = gkr[0]
    for i in range(1, bands):
        total = total + gkr[i]
    gkout[...] = total
    for copy in copies:
        copy.wait()
    drain(gkr.at[pl.ds(0, bands - 1)], ks)
    drain(sp.at[pl.ds(0, 2 * bands - 2)], ss)
    drain(bk.at[pl.ds(0, 2 * bands - 2)], rs)
    dstore.wait()


def local(
    atmos, kernels, w_one, w_two, w_flux, sea_mask, route,
    ocean_state, ct_atmos, ct_ocean, wo_one, wo_two,
):
    chans = lax.axis_size("chan")
    bands = lax.axis_size("band")
    rows, points = atmos.shape
    blocks = points // PTS
    own_blocks = -(-blocks // chans)
    share = own_blocks * PTS
    padded = own_blocks * chans
    quarter = PTS // chans
    slots = ocean_state.shape[2]
    hid = w_one.shape[2]
    full = rows * chans
    wide = wo_one.shape[1]
    total = wide * chans
    groups = bands // ZLEN
    flat = 1536
    big, little = 1152, 384
    size = flat // groups
    small = size // ZLEN
    vm = pl.BlockSpec(memory_space=VMEM)
    sm = pl.BlockSpec(memory_space=pltpu.SMEM)
    anywhere = pl.BlockSpec(memory_space=pl.ANY)

    table = pl.pallas_call(
        table_kernel,
        out_shape=jax.ShapeDtypeStruct((8, 128), jnp.int32),
        in_specs=[vm],
        out_specs=vm,
    )(route)
    ocean = VMEM((slots, quarter, PTS), BF16)
    points_first = VMEM((quarter, slots, PTS), BF16)
    wide_rows = VMEM((rows, padded * PTS), BF16)
    extended = VMEM((rows, points + 2 * share), BF16)
    square = VMEM((full, share), BF16)
    dat, dst, out, gk = pl.pallas_call(
        main_kernel,
        out_shape=[
            jax.ShapeDtypeStruct((rows, points), BF16),
            jax.ShapeDtypeStruct((quarter, slots, PTS), BF16),
            jax.ShapeDtypeStruct((flat, 128), BF16),
            jax.ShapeDtypeStruct((8, 128), F32),
        ],
        in_specs=[sm] + [vm] * 8 + [anywhere] * 3,
        out_specs=[vm, anywhere, vm, vm],
        scratch_shapes=[
            extended, wide_rows, wide_rows, square, square, square,
            VMEM((chans, full, hid), BF16),
            VMEM((chans, hid, full), BF16),
            VMEM((full, PTS), BF16),
            VMEM((own_blocks, PTS, PTS), BF16),
            VMEM((padded + 1, quarter, PTS), BF16),
            VMEM((1, padded * PTS), F32),
            VMEM((chans, hid, share), BF16),
            VMEM((chans, hid, share), BF16),
            wide_rows, square, ocean, ocean, ocean, ocean, points_first, points_first, points_first,
            VMEM((2 * PTS, total), BF16),
            VMEM((total, PTS), BF16),
            VMEM((2 * ZLEN * quarter, 2 * ZLEN * quarter), BF16),
            VMEM((2 * PTS, total), F32),
            VMEM((PTS, total), F32),
            VMEM((padded, quarter, PTS), BF16),
            VMEM((own_blocks, PTS, PTS), BF16),
            square, wide_rows, square, wide_rows, extended,
            VMEM((full, share), F32),
            VMEM((hid, share), BF16),
            VMEM((full, PTS), F32),
            VMEM((chans, big, 128), BF16),
            VMEM((2, big, 128), BF16),
            VMEM((big, 128), BF16),
            VMEM((big, 128), BF16),
            VMEM((chans, little, 128), BF16),
            VMEM((2, little, 128), BF16),
            VMEM((little, 128), BF16),
            VMEM((little, 128), BF16),
            VMEM((big, 128), F32),
            VMEM((little, 128), F32),
            VMEM((flat, 128), BF16),
            VMEM((groups, size, 128), BF16),
            VMEM((ZLEN, small, 128), F32),
            VMEM((ZLEN, small, 128), F32),
            VMEM((small, 128), F32),
            VMEM((ZLEN, small, 128), F32),
            VMEM((size, 128), BF16),
            VMEM((8, 128), F32),
            VMEM((bands, 8, 128), F32),
            DMA((4,)), DMA((2,)), DMA((2,)), DMA((3, 5)), DMA((3, 5)), DMA((4,)), DMA((4,)),
            DMA((3, 4)), DMA((3, 4)), DMA((3, 4)), DMA((3, 4)), DMA((4,)), DMA((4,)),
            DMA, DMA((groups,)), DMA, DMA,
            DMA((3,)), DMA((3,)), DMA((4,)), DMA((4,)), DMA((4,)), DMA((4,)), DMA((4,)), DMA((4,)),
            DMA((2,)), DMA((2,)), DMA((3,)), DMA((3,)),
            DMA((groups,)), DMA((groups,)), DMA((ZLEN,)), DMA((ZLEN,)),
            DMA((ZLEN,)), DMA((ZLEN,)), DMA((groups,)), DMA((groups,)), DMA, DMA,
        ],
        compiler_params=pltpu.CompilerParams(
            collective_id=0, has_side_effects=True, vmem_limit_bytes=LIMIT
        ),
    )(
        table, atmos, kernels[0], w_one[0], w_two[0], w_flux, sea_mask.reshape(1, points),
        wo_one, wo_two, ct_atmos, ocean_state, ct_ocean,
    )
    datmos, dk, dw1, dw2, dwf, dstate, do1, do2 = pl.pallas_call(
        finish_kernel,
        out_shape=[
            jax.ShapeDtypeStruct(dat.shape, BF16),
            jax.ShapeDtypeStruct((3, rows), F32),
            jax.ShapeDtypeStruct((full, hid), F32),
            jax.ShapeDtypeStruct((hid, full), F32),
            jax.ShapeDtypeStruct((rows, PTS), F32),
            jax.ShapeDtypeStruct(dst.shape, BF16),
            jax.ShapeDtypeStruct((2 * PTS, wide), F32),
            jax.ShapeDtypeStruct((wide, PTS), F32),
        ],
        in_specs=[vm] * 4,
        out_specs=[vm] * 8,
        compiler_params=pltpu.CompilerParams(vmem_limit_bytes=LIMIT // 2),
    )(dat, dst, out, gk)
    return datmos, dk[None], dw1[None], dw2[None], dwf, dstate[:, None], do1, do2


def solution(mesh):
    in_specs = (
        P("chan", "band"),
        P(None, None, "chan"),
        P(None, None, "chan"),
        P(None, "chan", None),
        P("chan", None),
        P("band"),
        P("band", None),
        P(None, "band", None, None),
        P("chan", "band"),
        P(None, "band", None, None),
        P(None, "chan"),
        P("chan", None),
    )
    out_specs = (
        P("chan", "band"),
        P(None, None, "chan"),
        P(None, None, "chan"),
        P(None, "chan", None),
        P("chan", None),
        P("chan", "band", None, None),
        P(None, "chan"),
        P("chan", None),
    )
    return jax.shard_map(local, mesh=mesh, in_specs=in_specs, out_specs=out_specs, check_vma=False)
```

```python
import functools

import jax
import jax.numpy as jnp
from jax import lax
from jax.experimental import pallas as pl
from jax.experimental.pallas import tpu as pltpu
from jax.sharding import PartitionSpec as P

PTS = 128
LON = 1440
MESH = pl.DeviceIdType.MESH
F32 = jnp.float32
BF16 = jnp.bfloat16
VMEM = pltpu.VMEM
DMA = pltpu.SemaphoreType.DMA
ZLEN = 8
LIMIT = 56 * 1024 * 1024


def nn(a, b):
    return lax.dot_general(a, b, (((1,), (0,)), ((), ())), preferred_element_type=F32)


def tn(a, b):
    return lax.dot_general(a, b, (((0,), (0,)), ((), ())), preferred_element_type=F32)


def nt(a, b):
    return lax.dot_general(a, b, (((1,), (1,)), ((), ())), preferred_element_type=F32)


def sigmoid(v):
    return 0.5 * jnp.tanh(0.5 * v) + 0.5


def place():
    b, c = lax.axis_index("band"), lax.axis_index("chan")
    mate = (c // 2) * 2 + (1 - c % 2)
    return b, c, mate, (c + 2) % 4, (mate + 2) % 4


def send(src, dst, ssem, rsem, b, c):
    copy = pltpu.make_async_remote_copy(
        src_ref=src,
        dst_ref=dst,
        send_sem=ssem,
        recv_sem=rsem,
        device_id=(b, c),
        device_id_type=MESH,
    )
    copy.start()
    return copy


def drain(ref, sem):
    pltpu.make_async_copy(ref, ref, sem).wait()


def signal(b, c):
    pl.semaphore_signal(
        pltpu.get_barrier_semaphore(), inc=1, device_id=(b, c), device_id_type=MESH
    )


def taken(ref, start, width):
    extra = start % 128
    if extra == 0:
        return ref[:, start : start + width].astype(F32)
    wide = ref[:, start - extra : start - extra + width + 128].astype(F32)
    return pltpu.roll(wide, width + 128 - extra, axis=1)[:, :width]


def table_kernel(route, table):
    blocks = route.shape[1]
    row = route[...]
    k = lax.broadcasted_iota(jnp.int32, (blocks, blocks), 0)
    j = lax.broadcasted_iota(jnp.int32, (blocks, blocks), 1)
    col = jnp.sum(jnp.where(k == j, row, 0), axis=1, keepdims=True)
    rank = jnp.sum(jnp.where((row == col) & (j < k), 1, 0), axis=1, keepdims=True)
    slot = col * 2 + rank
    k = lax.broadcasted_iota(jnp.int32, (blocks, 128), 0)
    s = lax.broadcasted_iota(jnp.int32, (blocks, 128), 1)
    empty = blocks
    inv = empty + jnp.sum(jnp.where(slot == s, k - empty, 0), axis=0, keepdims=True)
    back = jnp.sum(jnp.where(k == s, slot, 0), axis=0, keepdims=True)
    line = lax.broadcasted_iota(jnp.int32, (8, 128), 0)
    table[...] = jnp.where(line == 0, inv, back)


def finish_kernel(dat, dst, out, datmos, dk, dw1, dw2, dwf, dstate, do1, do2):
    datmos[...] = dat[...]
    dstate[...] = dst[...]
    for j in range(2):
        dw1[:, j * 128 : j * 128 + 128] = out[j * 256 : j * 256 + 256].astype(F32)
        dw2[:, j * 128 : j * 128 + 128] = out[512 + j * 256 : 768 + j * 256].astype(F32)
    dwf[...] = out[1024:1088].astype(F32)
    do1[...] = out[1152:1408].astype(F32)
    do2[...] = out[1408:1536].astype(F32).T
    tile = out[1088:1152].astype(F32).T
    for i in range(3):
        dk[i] = tile[i : i + 1, :]


def main_kernel(
    table, atmos, taps, w_one, w_two, w_flux, sea, wo_one, wo_two, ct_all, state_all, cot_all,
    dat, dst, out,
    al, cl, ext, zb, alm, tapt, tapr, tapf, w1, w2, wf, fx, fm, mk, mk4, hid, slope,
    ctv0, ctb, sp, rf, bk, rb, st, ctv, ds, wa, wb, perm, go1, go2,
    dfp, dfb, gb, dext, dl, dq, dzacc, dubuf, gwf, gkp, gkr,
    gs, ra, hx, rx, gso, rao, hxo, rxo, own, owno, t, r1, fs, r2, fr, ag, tb,
    lsem, hs, hr, ws, wr, ts, tr, as_, ar, fxs, fxr, cs, cr, ss, sr, rs, rr,
    os_, or_, dfs, dfr, h2s, h2r, gks, gkq, das, dar, s0, q0, s1, q1, s2, q2, s3, q3, s4, q4,
):
    b, c, mate, across, diag = place()
    bands = lax.axis_size("band")
    up, down = (b + bands - 1) % bands, (b + 1) % bands
    q, z = b // ZLEN, b % ZLEN
    groups = bands // ZLEN
    flip = ((q // 2) * 2 + (1 - q % 2)) * ZLEN + z
    rows, points = atmos.shape
    full, share = zb.shape
    lats = points // LON
    width = share // lats
    quarter = st.shape[0]
    blocks = dfp.shape[0]
    row_groups = LON // quarter
    few = row_groups // 4
    stride = few * quarter
    wide = wo_one.shape[1]
    peers = [(c + 2) % 4, (c + 1) % 4, (c + 3) % 4]
    order = (2, 1, 3)
    pairs = list(zip(order, peers))

    def greet(i, _):
        signal((b + i) % bands, c)
        return 0

    for d in (1, 2, 3):
        signal(b, (c + d) % 4)
    signal(flip, across)
    lax.fori_loop(1, bands, greet, 0)
    loads = [
        pltpu.make_async_copy(ct_all, ctv0, lsem.at[0]),
        pltpu.make_async_copy(
            state_all.at[pl.ds(pl.multiple_of(quarter * c, quarter), quarter), 0], st, lsem.at[1]
        ),
        pltpu.make_async_copy(
            cot_all.at[pl.ds(pl.multiple_of(quarter * c, quarter), quarter), 0], ctv, lsem.at[2]
        ),
    ]
    for load in loads:
        load.start()
    mine = pl.ds(pl.multiple_of(c * rows, rows), rows)
    eye = lax.broadcasted_iota(jnp.int32, (rows, rows), 0) == lax.broadcasted_iota(
        jnp.int32, (rows, rows), 1
    )
    for r in (0, lats - 1) + tuple(range(1, lats - 1)):
        for j in range(4):
            al[j, :, r * width : (r + 1) * width] = taken(
                atmos, r * LON + j * stride, width
            ).astype(BF16)
    tapt[...] = jnp.zeros(tapt.shape, F32)
    for i in range(3):
        tapt[i : i + 1, :rows] = taps[i]
    pl.semaphore_wait(pltpu.get_barrier_semaphore(), bands - 1 + 4)

    cuts = (
        slice(0, width), slice((lats - 1) * width, lats * width), slice(width, (lats - 1) * width)
    )
    acopies = [[], [], []]

    def send_state(k):
        lo, hi = cuts[k].start, cuts[k].stop
        for d, to in pairs:
            acopies[k].append(
                send(
                    al.at[to, :, lo:hi], ext.at[mine, width + lo : width + hi],
                    as_.at[k, d], ar.at[k, d], b, to,
                )
            )

    send_state(0)
    send_state(1)
    mine_wide = pl.ds(pl.multiple_of(c * wide, wide), wide)
    theirs = pl.ds(pl.multiple_of(across * rows, rows), rows)
    theirs_wide = pl.ds(pl.multiple_of(across * wide, wide), wide)
    sources = (w_one, w_two, w_flux, wo_one, wo_two)
    near = (w1.at[c], w2.at[c], wf.at[mine, :], wa.at[:, mine_wide], wb.at[mine_wide, :])
    far = (
        w1.at[across], w2.at[across], wf.at[theirs, :],
        wa.at[:, theirs_wide], wb.at[theirs_wide, :],
    )
    first, second, third, tcopies = [], [], [], []
    for i in range(5):
        second.append(send(sources[i], near[i], ws.at[1, i], wr.at[1, i], flip, across))
        first.append(send(sources[i], near[i], ws.at[0, i], wr.at[0, i], b, mate))
    for d, to in pairs:
        tcopies.append(send(tapt, tapr.at[c], ts.at[d], tr.at[d], b, to))
    send_state(2)
    w1[c] = w_one[...]
    w2[c] = w_two[...]
    wf[mine, :] = w_flux[...]
    wa[:, mine_wide] = wo_one[...]
    wb[mine_wide, :] = wo_two[...]
    ext[mine, width : width + share] = al[c]
    tapr[c] = tapt[...]
    for i in range(points // PTS):
        mk[:, i * PTS : (i + 1) * PTS] = sea[i : i + 1, :].astype(F32)
    for r in range(lats):
        for j in range(4):
            mk4[j, :, r * width : (r + 1) * width] = taken(mk, r * LON + j * stride, width)
    for k in (0, 1):
        for copy in acopies[k]:
            copy.wait()
    halo = [
        send(
            ext.at[:, lats * width : (lats + 1) * width], ext.at[:, :width],
            hs.at[0], hr.at[0], down, c,
        ),
        send(
            ext.at[:, width : 2 * width], ext.at[:, (lats + 1) * width :],
            hs.at[1], hr.at[1], up, c,
        ),
    ]
    for copy in tcopies:
        copy.wait()
    for j in range(4):
        for i in range(3):
            tapf[j * rows : (j + 1) * rows, i : i + 1] = jnp.sum(
                jnp.where(eye, tapr[j, i : i + 1, :rows], 0.0), axis=1, keepdims=True
            )
    t0, t1, t2 = tapf[:, 0:1], tapf[:, 1:2], tapf[:, 2:3]
    lane = lax.broadcasted_iota(jnp.int32, (1, share), 1) % width
    kept = jnp.where((lane < stride) | (c == 3), 1.0, 0.0)
    sea_kept = mk4[c] * kept
    for i in range(5):
        second[i].wait_recv()
        third.append(send(far[i], far[i], ws.at[2, i], wr.at[2, i], b, mate))
    for copy in acopies[2]:
        copy.wait()
    for i in range(3):
        first[i].wait()
        second[i].wait_send()
        third[i].wait()
    fcopies = []
    line = (1, 2, 0, 3)
    for r in line:
        if r == 0:
            for copy in halo:
                copy.wait()

            @pl.when(b == 0)
            def _():
                ext[:, :width] = jnp.zeros((full, width), BF16)

            @pl.when(b == bands - 1)
            def _():
                ext[:, (lats + 1) * width :] = jnp.zeros((full, width), BF16)

        cols = slice(r * width, (r + 1) * width)
        state = ext[:, (r + 1) * width : (r + 2) * width].astype(F32)
        zcol = (
            t0 * ext[:, r * width : (r + 1) * width].astype(F32)
            + t1 * state
            + t2 * ext[:, (r + 2) * width : (r + 3) * width].astype(F32)
        ).astype(BF16)
        zb[:, cols] = zcol
        total = None
        for i in range(4):
            u = tn(w1[i], zcol)
            sig = sigmoid(u)
            act = u * sig
            h = act.astype(BF16)
            hid[i, :, cols] = h
            slope[i, :, cols] = (sig + act * (1.0 - sig)).astype(BF16)
            piece = tn(w2[i], h)
            total = piece if total is None else total + piece
        acol = (state + total).astype(BF16)
        acol = (acol.astype(F32) * sea_kept[:, cols]).astype(BF16)
        alm[:, cols] = acol
        fx[r] = tn(acol, wf[...]).astype(BF16).reshape(fx.shape[1:])
        for d, to in pairs:
            i0 = (to + 3 * r + c) % 4
            k0 = (row_groups * r + few * c + i0) // 4
            twice = ((i0 + 1) // 4) * ((6 - c) // 4)
            k2 = k0 + 2 + twice * (blocks + 1 + 4 * c + r - k0 - 2)
            fcopies.append(
                send(
                    fx.at[r, 0:2, i0], fm.at[pl.ds(k0, 2)], fxs.at[r, d, 0], fxr.at[r, d, 0], b, to
                )
            )
            fcopies.append(
                send(
                    fx.at[r, 2:3, i0], fm.at[pl.ds(k2, 1)], fxs.at[r, d, 1], fxr.at[r, d, 1], b, to
                )
            )
        i0 = (2 * c + 3 * r) % 4
        k0 = (row_groups * r + few * c + i0) // 4
        twice = ((i0 + 1) // 4) * ((6 - c) // 4)
        k2 = k0 + 2 + twice * (blocks + 1 + 4 * c + r - k0 - 2)
        fm[pl.ds(k0, 2)] = fx[r, 0:2, i0]
        fm[k2] = fx[r, 2, i0]
    fm[blocks] = jnp.zeros(fm.shape[1:], BF16)
    span = 2 * ZLEN
    size = span * quarter
    r = lax.broadcasted_iota(jnp.int32, (size, size), 0)
    k = lax.broadcasted_iota(jnp.int32, (size, size), 1)
    perm[...] = jnp.where((r % span) * quarter + r // span == k, 1.0, 0.0).astype(BF16)
    go1[...] = jnp.zeros(go1.shape, F32)
    go2[...] = jnp.zeros(go2.shape, F32)
    for load in loads:
        load.wait()
    for i in range(3, 5):
        first[i].wait()
        second[i].wait_send()
        third[i].wait()
    for copy in fcopies:
        copy.wait()

    def pack(s, _):
        sp[s] = fm[table[0, s]]
        return 0

    lax.fori_loop(0, 2 * bands, pack, 0)
    turn = [(z + i) % ZLEN for i in range(ZLEN)]

    def couple(d, start):
        base = ((q + d) % groups) * ZLEN
        for i in range(start, ZLEN):
            to = base + turn[i]
            send(sp.at[pl.ds(2 * to, 2)], rf.at[pl.ds(2 * b, 2)], ss, sr.at[d], to, c)

    couple(0, 1)

    def couple_all(d, _):
        couple(d, 0)
        return 0

    lax.fori_loop(1, groups, couple_all, 0)
    rf[pl.ds(2 * b, 2)] = sp[pl.ds(2 * b, 2)]
    for r in range(lats):
        for j in range(4):
            cl[j, :, r * width : (r + 1) * width] = taken(
                ctv0, r * LON + j * stride, width
            ).astype(BF16)
    ctcopies = []
    for d, to in pairs:
        ctcopies.append(send(cl.at[to], ctb.at[mine, :], cs.at[d], cr.at[d], b, to))
    ctb[mine, :] = cl[c]
    drain(rf.at[pl.ds(0, span - 2)], sr.at[0])

    def step(d, _):
        @pl.when(d > 0)
        def _():
            drain(rf.at[pl.ds(0, span)], sr.at[d])

        src = (q + groups - d) % groups
        at = pl.ds(pl.multiple_of(src * span, span), span)
        force = nn(perm[...], rf[at].reshape(size, PTS)).astype(BF16)
        both = jnp.concatenate([st[:, at, :].reshape(size, PTS), force], axis=1)
        cot = ctv[:, at, :].reshape(size, PTS)
        pre = nn(both, wa[...])
        sig = sigmoid(pre)
        act = pre * sig
        grad = (nt(cot, wb[...]) * (sig + act * (1.0 - sig))).astype(BF16)
        back = nt(grad, wa[...])
        bk[at] = tn(perm[...], back[:, PTS:].astype(BF16)).astype(BF16).reshape(span, quarter, PTS)

        def give(i):
            to = src * ZLEN + turn[i]
            send(bk.at[pl.ds(2 * to, 2)], rb.at[pl.ds(2 * b, 2)], rs, rr, to, c)

        @pl.when(d > 0)
        def _():
            give(0)

        for i in range(1, ZLEN):
            give(i)
        ds[:, at, :] = (
            (cot.astype(F32) + back[:, :PTS]).astype(BF16).reshape(quarter, span, PTS)
        )
        go2[...] += tn(cot, act.astype(BF16))
        go1[...] += tn(both, grad)
        return 0

    lax.fori_loop(0, groups, step, 0)
    dstore = pltpu.make_async_copy(ds, dst, lsem.at[3])
    dstore.start()
    rb[pl.ds(2 * b, 2)] = bk[pl.ds(2 * b, 2)]
    for i in range(4):
        gso[i, :256] = go1[:, i * 128 : i * 128 + 128].astype(BF16)
        gso[i, 256:] = go2[:, i * 128 : i * 128 + 128].astype(BF16)
    ocopies = [
        send(gso.at[diag], rao.at[1], os_.at[1], or_.at[1], b, mate),
        send(gso.at[mate], rao.at[0], os_.at[0], or_.at[0], b, mate),
    ]
    for copy in ctcopies:
        copy.wait()
    drain(rb.at[pl.ds(0, 2 * bands - 2)], rr)

    def unpack(k, _):
        dfp[k] = rb[table[1, k]]
        return 0

    lax.fori_loop(0, blocks, unpack, 0)
    dcopies = []
    for r in range(lats):
        for d, to in pairs:
            i0 = (c + 3 * r + to) % 4
            k0 = (row_groups * r + few * to + i0) // 4
            dcopies.append(
                send(dfp.at[pl.ds(k0, 3)], dfb.at[r, :, i0], dfs.at[r, d], dfr.at[r, d], b, to)
            )
        i0 = (2 * c + 3 * r) % 4
        k0 = (row_groups * r + few * c + i0) // 4
        dfb[r, :, i0] = dfp[pl.ds(k0, 3)]
    for copy in ocopies:
        copy.wait()
    hxo[...] = (gso[across].astype(F32) + rao[1].astype(F32)).astype(BF16)
    owno[...] = gso[c].astype(F32) + rao[0].astype(F32)
    ocopy = send(hxo, rxo, os_.at[2], or_.at[2], b, across)
    gs[:, 1088:] = jnp.zeros((4, 64, 128), BF16)
    for copy in dcopies:
        copy.wait()
    flux = dfb[...].reshape(share, PTS)
    gb[...] = (ctb[...].astype(F32) * kept + nt(wf[...], flux) * sea_kept).astype(BF16)
    gwf[...] = nn(alm[...], flux)
    wcopies = []
    halo = []
    for turn, i in enumerate((diag, mate, across, c)):
        for r in (0, 3, 1, 2):
            cols = slice(r * width, (r + 1) * width)
            du = (nn(w2[i], gb[:, cols]) * slope[i, :, cols].astype(F32)).astype(BF16)
            dubuf[:, cols] = du
            piece = nn(w1[i], du)
            if turn == 0:
                dzacc[:, cols] = piece
            elif turn < 3:
                dzacc[:, cols] += piece
            else:
                at = (r + 1) * width
                dext[:, at : at + width] = (dzacc[:, cols] + piece).astype(BF16)
                if r == 0:
                    halo.append(
                        send(
                            dext.at[:, at : at + width], dext.at[:, (lats + 1) * width :],
                            h2s.at[1], h2r.at[1], up, c,
                        )
                    )
                if r == 3:
                    halo.append(
                        send(
                            dext.at[:, at : at + width], dext.at[:, :width],
                            h2s.at[0], h2r.at[0], down, c,
                        )
                    )
        g1 = nt(zb[...], dubuf[...])
        g2 = nt(hid[i], gb[...])
        for j in range(2):
            gs[i, j * 256 : j * 256 + 256] = g1[:, j * 128 : j * 128 + 128].astype(BF16)
            gs[i, 512 + j * 256 : 768 + j * 256] = g2[:, j * 128 : j * 128 + 128].astype(BF16)
        gs[i, 1024:1088] = gwf[pl.ds(pl.multiple_of(rows * i, rows), rows), :].astype(BF16)
        if turn == 0:
            wcopies.append(send(gs.at[diag], ra.at[1], s0.at[1], q0.at[1], b, mate))
        if turn == 1:
            wcopies.append(send(gs.at[mate], ra.at[0], s0.at[0], q0.at[0], b, mate))
        if turn == 2:
            wcopies[0].wait()
            hx[...] = (gs[across].astype(F32) + ra[1].astype(F32)).astype(BF16)
            wcopies.append(send(hx, rx, s0.at[2], q0.at[2], b, across))
    column = lax.broadcasted_iota(jnp.int32, (full, 128), 1)
    tile = jnp.zeros((full, 128), F32)
    for i in range(3):
        acc = jnp.zeros((full, 128), F32)
        for r in range(lats):
            prod = ext[:, (r + i) * width : (r + i + 1) * width].astype(F32) * dext[
                :, (r + 1) * width : (r + 2) * width
            ].astype(F32)
            for o in range(0, width, 128):
                acc = acc + prod[:, o : o + 128]
        tile = jnp.where(column == i, jnp.sum(acc, axis=1, keepdims=True), tile)
    gkp[...] = tile.reshape(gkp.shape)
    kcopies = []
    for d, to in pairs:
        kcopies.append(send(gkp.at[to], gkr.at[d], gks.at[d], gkq.at[d], b, to))
    dcopies = []

    def spread(r):
        cols = slice(r * width, (r + 1) * width)
        dl[:, cols] = (
            gb[:, cols].astype(F32)
            + t0 * dext[:, (r + 2) * width : (r + 3) * width].astype(F32)
            + t1 * dext[:, (r + 1) * width : (r + 2) * width].astype(F32)
            + t2 * dext[:, r * width : (r + 1) * width].astype(F32)
        ).astype(BF16)

    def send_back(k):
        lo, hi = cuts[k].start, cuts[k].stop
        for d, to in pairs:
            theirs = pl.ds(pl.multiple_of(rows * to, rows), rows)
            dcopies.append(
                send(dl.at[theirs, lo:hi], dq.at[c, :, lo:hi], das.at[k, d], dar.at[k, d], b, to)
            )

    spread(1)
    spread(2)
    send_back(2)
    wcopies[1].wait()
    own[...] = gs[c].astype(F32) + ra[0].astype(F32)
    ocopy.wait()
    t[1152:] = (owno[...] + rxo[...].astype(F32)).astype(BF16)
    for copy in kcopies:
        copy.wait()
    t[1088:1152] = (gkp[c] + gkr[1] + gkr[2] + gkr[3]).astype(BF16)
    wcopies[2].wait()
    t[:1088] = (own[:1088] + rx[:1088].astype(F32)).astype(BF16)
    size = r1.shape[1]
    copies = []
    for d in range(1, groups):
        to = (q + d) % groups
        cut = pl.ds(pl.multiple_of(to * size, size), size)
        copies.append(send(t.at[cut], r1.at[q], s1.at[d], q1.at[d], to * ZLEN + z, c))
    r1[q] = t[pl.ds(pl.multiple_of(q * size, size), size)]
    for copy in halo:
        copy.wait()

    @pl.when(b == 0)
    def _():
        dext[:, :width] = jnp.zeros((full, width), BF16)

    @pl.when(b == bands - 1)
    def _():
        dext[:, (lats + 1) * width :] = jnp.zeros((full, width), BF16)

    spread(0)
    send_back(0)
    spread(3)
    send_back(1)
    dq[c] = dl[mine, :]
    for copy in copies:
        copy.wait()
    total = r1[0].astype(F32)
    for i in range(1, groups):
        total = total + r1[i].astype(F32)
    fs[...] = total.reshape(fs.shape)
    copies = []
    for d in range(1, ZLEN):
        to = (z + d) % ZLEN
        copies.append(send(fs.at[to], r2.at[z], s2.at[d], q2.at[d], q * ZLEN + to, c))
    r2[z] = fs[z]
    for copy in copies:
        copy.wait()
    total = r2[0]
    for i in range(1, ZLEN):
        total = total + r2[i]
    fr[...] = total
    copies = []
    for d in range(1, ZLEN):
        to = (z + d) % ZLEN
        copies.append(send(fr, ag.at[z], s3.at[d], q3.at[d], q * ZLEN + to, c))
    ag[z] = total
    for copy in copies:
        copy.wait()
    tb[...] = ag[...].reshape(size, 128).astype(BF16)
    copies = []
    for d in range(1, groups):
        to = (q + d) % groups
        cut = pl.ds(pl.multiple_of(q * size, size), size)
        copies.append(send(tb, out.at[cut], s4.at[d], q4.at[d], to * ZLEN + z, c))
    out[pl.ds(pl.multiple_of(q * size, size), size)] = tb[...]
    for copy in dcopies:
        copy.wait()
    for r in range(lats):
        for j in range(4):
            start = r * LON + j * stride
            extra = start % 128
            piece = dq[j, :, r * width : (r + 1) * width]
            if extra == 0:
                dat[:, start : start + width] = piece
                continue
            base = start - extra
            moved = jnp.concatenate([piece.astype(F32), jnp.zeros((rows, 128), F32)], axis=1)
            moved = pltpu.roll(moved, extra, axis=1)
            lead = lax.broadcasted_iota(jnp.int32, (rows, 128), 1)
            dat[:, base : base + 128] = jnp.where(
                lead < extra, dat[:, base : base + 128].astype(F32), moved[:, :128]
            ).astype(BF16)
            dat[:, base + 128 : base + 128 + width] = moved[:, 128:].astype(BF16)
    for copy in copies:
        copy.wait()
    drain(sp.at[pl.ds(0, 2 * bands - 2)], ss)
    drain(bk.at[pl.ds(0, 2 * bands - 2)], rs)
    dstore.wait()


def local(
    atmos, kernels, w_one, w_two, w_flux, sea_mask, route,
    ocean_state, ct_atmos, ct_ocean, wo_one, wo_two,
):
    chans = lax.axis_size("chan")
    bands = lax.axis_size("band")
    rows, points = atmos.shape
    blocks = points // PTS
    quarter = PTS // chans
    lats = points // LON
    share = lats * (LON // quarter // chans + 1) * quarter
    width = share // lats
    slots = ocean_state.shape[2]
    hid = w_one.shape[2]
    full = rows * chans
    wide = wo_one.shape[1]
    total = wide * chans
    groups = bands // ZLEN
    flat = 1536
    big, little = 1152, 384
    size = flat // groups
    small = size // ZLEN
    vm = pl.BlockSpec(memory_space=VMEM)
    sm = pl.BlockSpec(memory_space=pltpu.SMEM)
    anywhere = pl.BlockSpec(memory_space=pl.ANY)

    table = pl.pallas_call(
        table_kernel,
        out_shape=jax.ShapeDtypeStruct((8, 128), jnp.int32),
        in_specs=[vm],
        out_specs=vm,
    )(route.T)
    ocean = VMEM((slots, quarter, PTS), BF16)
    points_first = VMEM((quarter, slots, PTS), BF16)
    split = VMEM((chans, rows, share), BF16)
    extended = VMEM((full, share + 2 * width), BF16)
    square = VMEM((full, share), BF16)
    grouped = VMEM((lats, width // PTS, chans, quarter, PTS), BF16)
    dat, dst, out = pl.pallas_call(
        main_kernel,
        out_shape=[
            jax.ShapeDtypeStruct((rows, points), BF16),
            jax.ShapeDtypeStruct((quarter, slots, PTS), BF16),
            jax.ShapeDtypeStruct((flat, 128), BF16),
        ],
        in_specs=[sm] + [vm] * 8 + [anywhere] * 3,
        out_specs=[vm, anywhere, vm],
        scratch_shapes=[
            split, split, extended, square, square,
            VMEM((8, 128), F32),
            VMEM((chans, 8, 128), F32),
            VMEM((full, 128), F32),
            VMEM((chans, full, hid), BF16),
            VMEM((chans, hid, full), BF16),
            VMEM((full, PTS), BF16),
            grouped,
            VMEM((blocks + 1 + 4 * lats, quarter, PTS), BF16),
            VMEM((1, points), F32),
            VMEM((chans, 1, share), F32),
            VMEM((chans, hid, share), BF16),
            VMEM((chans, hid, share), BF16),
            VMEM((rows, points), BF16),
            square, ocean, ocean, ocean, ocean, points_first, points_first, points_first,
            VMEM((2 * PTS, total), BF16),
            VMEM((total, PTS), BF16),
            VMEM((2 * ZLEN * quarter, 2 * ZLEN * quarter), BF16),
            VMEM((2 * PTS, total), F32),
            VMEM((PTS, total), F32),
            VMEM((blocks, quarter, PTS), BF16),
            grouped, square, extended, square, split,
            VMEM((full, share), F32),
            VMEM((hid, share), BF16),
            VMEM((full, PTS), F32),
            VMEM((chans, rows, 128), F32),
            VMEM((chans, rows, 128), F32),
            VMEM((chans, big, 128), BF16),
            VMEM((2, big, 128), BF16),
            VMEM((big, 128), BF16),
            VMEM((big, 128), BF16),
            VMEM((chans, little, 128), BF16),
            VMEM((2, little, 128), BF16),
            VMEM((little, 128), BF16),
            VMEM((little, 128), BF16),
            VMEM((big, 128), F32),
            VMEM((little, 128), F32),
            VMEM((flat, 128), BF16),
            VMEM((groups, size, 128), BF16),
            VMEM((ZLEN, small, 128), F32),
            VMEM((ZLEN, small, 128), F32),
            VMEM((small, 128), F32),
            VMEM((ZLEN, small, 128), F32),
            VMEM((size, 128), BF16),
            DMA((4,)), DMA((2,)), DMA((2,)), DMA((3, 5)), DMA((3, 5)), DMA((4,)), DMA((4,)),
            DMA((3, 4)), DMA((3, 4)), DMA((lats, 4, 2)), DMA((lats, 4, 2)), DMA((4,)), DMA((4,)),
            DMA, DMA((groups,)), DMA, DMA,
            DMA((3,)), DMA((3,)), DMA((lats, 4)), DMA((lats, 4)), DMA((2,)), DMA((2,)),
            DMA((4,)), DMA((4,)), DMA((3, 4)), DMA((3, 4)), DMA((3,)), DMA((3,)),
            DMA((groups,)), DMA((groups,)), DMA((ZLEN,)), DMA((ZLEN,)),
            DMA((ZLEN,)), DMA((ZLEN,)), DMA((groups,)), DMA((groups,)),
        ],
        compiler_params=pltpu.CompilerParams(
            collective_id=0, has_side_effects=True, vmem_limit_bytes=LIMIT
        ),
    )(
        table, atmos, kernels.transpose(1, 0, 2), w_one[0], w_two[0], w_flux, sea_mask.reshape(blocks, PTS),
        wo_one, wo_two, ct_atmos, ocean_state, ct_ocean,
    )
    datmos, dk, dw1, dw2, dwf, dstate, do1, do2 = pl.pallas_call(
        finish_kernel,
        out_shape=[
            jax.ShapeDtypeStruct(dat.shape, BF16),
            jax.ShapeDtypeStruct((3, 1, rows), F32),
            jax.ShapeDtypeStruct((full, hid), F32),
            jax.ShapeDtypeStruct((hid, full), F32),
            jax.ShapeDtypeStruct((rows, PTS), F32),
            jax.ShapeDtypeStruct(dst.shape, BF16),
            jax.ShapeDtypeStruct((2 * PTS, wide), F32),
            jax.ShapeDtypeStruct((wide, PTS), F32),
        ],
        in_specs=[vm] * 3,
        out_specs=[vm] * 8,
        compiler_params=pltpu.CompilerParams(vmem_limit_bytes=LIMIT + (4 << 20)),
    )(dat, dst, out)
    return datmos, dk.transpose(1, 0, 2), dw1[None], dw2[None], dwf, dstate[:, None], do1, do2


def solution(mesh):
    in_specs = (
        P("chan", "band"),
        P(None, None, "chan"),
        P(None, None, "chan"),
        P(None, "chan", None),
        P("chan", None),
        P("band"),
        P("band", None),
        P(None, "band", None, None),
        P("chan", "band"),
        P(None, "band", None, None),
        P(None, "chan"),
        P("chan", None),
    )
    out_specs = (
        P("chan", "band"),
        P(None, None, "chan"),
        P(None, None, "chan"),
        P(None, "chan", None),
        P("chan", None),
        P("chan", "band", None, None),
        P(None, "chan"),
        P("chan", None),
    )
    return jax.shard_map(local, mesh=mesh, in_specs=in_specs, out_specs=out_specs, check_vma=False)
```

```python
import functools

import jax
import jax.numpy as jnp
from jax import lax
from jax.experimental import pallas as pl
from jax.experimental.pallas import tpu as pltpu
from jax.sharding import PartitionSpec as P

PTS = 128
LON = 1440
MESH = pl.DeviceIdType.MESH
F32 = jnp.float32
BF16 = jnp.bfloat16
VMEM = pltpu.VMEM
DMA = pltpu.SemaphoreType.DMA
ZLEN = 8
LIMIT = 56 * 1024 * 1024


def nn(a, b):
    return lax.dot_general(a, b, (((1,), (0,)), ((), ())), preferred_element_type=F32)


def tn(a, b):
    return lax.dot_general(a, b, (((0,), (0,)), ((), ())), preferred_element_type=F32)


def nt(a, b):
    return lax.dot_general(a, b, (((1,), (1,)), ((), ())), preferred_element_type=F32)


def sigmoid(v):
    return 0.5 * jnp.tanh(0.5 * v) + 0.5


def place():
    b, c = lax.axis_index("band"), lax.axis_index("chan")
    mate = (c // 2) * 2 + (1 - c % 2)
    return b, c, mate, (c + 2) % 4, (mate + 2) % 4


def send(src, dst, ssem, rsem, b, c):
    copy = pltpu.make_async_remote_copy(
        src_ref=src,
        dst_ref=dst,
        send_sem=ssem,
        recv_sem=rsem,
        device_id=(b, c),
        device_id_type=MESH,
    )
    copy.start()
    return copy


def drain(ref, sem):
    pltpu.make_async_copy(ref, ref, sem).wait()


def signal(b, c):
    pl.semaphore_signal(
        pltpu.get_barrier_semaphore(), inc=1, device_id=(b, c), device_id_type=MESH
    )


def taken(ref, start, width):
    extra = start % 128
    if extra == 0:
        return ref[:, start : start + width].astype(F32)
    wide = ref[:, start - extra : start - extra + width + 128].astype(F32)
    return pltpu.roll(wide, width + 128 - extra, axis=1)[:, :width]


def table_kernel(route, table):
    blocks = route.shape[1]
    row = route[...]
    k = lax.broadcasted_iota(jnp.int32, (blocks, blocks), 0)
    j = lax.broadcasted_iota(jnp.int32, (blocks, blocks), 1)
    col = jnp.sum(jnp.where(k == j, row, 0), axis=1, keepdims=True)
    rank = jnp.sum(jnp.where((row == col) & (j < k), 1, 0), axis=1, keepdims=True)
    slot = col * 2 + rank
    k = lax.broadcasted_iota(jnp.int32, (blocks, 128), 0)
    s = lax.broadcasted_iota(jnp.int32, (blocks, 128), 1)
    empty = blocks
    inv = empty + jnp.sum(jnp.where(slot == s, k - empty, 0), axis=0, keepdims=True)
    back = jnp.sum(jnp.where(k == s, slot, 0), axis=0, keepdims=True)
    line = lax.broadcasted_iota(jnp.int32, (8, 128), 0)
    table[...] = jnp.where(line == 0, inv, back)


def finish_kernel(
    dat, dst, out_hbm, datmos, dk, dw1, dw2, dwf, dstate, do1, do2, dbuf, sbuf, out, isem, osem
):
    loads = [
        pltpu.make_async_copy(out_hbm, out, isem.at[0]),
        pltpu.make_async_copy(dst, sbuf, isem.at[1]),
        pltpu.make_async_copy(dat, dbuf, isem.at[2]),
    ]
    for load in loads:
        load.start()
    stores = [
        pltpu.make_async_copy(sbuf, dstate, osem.at[0]),
        pltpu.make_async_copy(dbuf, datmos, osem.at[1]),
    ]
    loads[0].wait()
    half = out.shape[0] // 2
    dw1[:, :128] = out[:256].astype(F32)
    dw1[:, 128:] = out[256:512].astype(F32)
    dw2[:32, :128] = out[512:544].astype(F32)
    dw2[32:, :128] = out[half : half + 224].astype(F32)
    dw2[:, 128:] = out[half + 224 : half + 480].astype(F32)
    loads[1].wait()
    stores[0].start()
    loads[2].wait()
    stores[1].start()
    dwf[...] = out[half + 480 : half + 544].astype(F32)
    tile = out[544:560].astype(F32) + out[half + 544 : half + 560].astype(F32)
    for i in range(3):
        dk[i] = tile[i : i + 1, :64]
    do1[:192] = out[576:768].astype(F32)
    do1[192:] = out[half + 576 : half + 640].astype(F32)
    do2[...] = out[half + 640 :].astype(F32).T
    for store in stores:
        store.wait()


def main_kernel(
    table, taps, sea, atmos_all, w_one, w_two, w_flux, wo_one, wo_two, ct_all, state_all, cot_all,
    dat_all, dst, out,
    atmos, dat, al, cl, ext, zb, alm, tapt, tapr, tapf, w1, w2, wf, fx, fm, mk, mk4, hid, slope,
    ctv0, ctb, sp, rf, bk, rb, st, ctv, ds, wa, wb, perm, go1, go2,
    dfp, dfb, gb, dext, dl, dq, dzacc, dubuf, gwf, gkp, gkr,
    gs, ra, hx, rw, gso, rao, hxo, rxo, own, owno, ownb, ownob, t, r1, fs, r2, fr, ag, tb,
    lsem, msem, hs, hr, ws, wr, ts, tr, as_, ar, fxs, fxr, cs, cr, ss, sr, rs, rr,
    os_, or_, dfs, dfr, h2s, h2r, gks, gkq, das, dar, s0, q0, s1, q1, s2, q2, s3, q3, s4, q4,
):
    b, c, mate, across, diag = place()
    bands = lax.axis_size("band")
    up, down = (b + bands - 1) % bands, (b + 1) % bands
    q, z = b // ZLEN, b % ZLEN
    groups = bands // ZLEN
    flip = ((q // 2) * 2 + (1 - q % 2)) * ZLEN + z
    rows, points = atmos.shape
    full, share = zb.shape
    lats = points // LON
    width = share // lats
    quarter = st.shape[0]
    blocks = dfp.shape[0]
    row_groups = LON // quarter
    few = row_groups // 4
    stride = few * quarter
    wide = wo_one.shape[1]
    peers = [(c + 2) % 4, (c + 1) % 4, (c + 3) % 4]
    order = (2, 1, 3)
    pairs = list(zip(order, peers))

    def greet(i, _):
        signal((b + i) % bands, c)
        return 0

    for d in (1, 2, 3):
        signal(b, (c + d) % 4)
    signal(flip, across)
    lax.fori_loop(1, bands, greet, 0)
    loads = [
        pltpu.make_async_copy(ct_all, ctv0, lsem.at[0]),
        pltpu.make_async_copy(
            state_all.at[pl.ds(pl.multiple_of(quarter * c, quarter), quarter), 0], st, lsem.at[1]
        ),
        pltpu.make_async_copy(
            cot_all.at[pl.ds(pl.multiple_of(quarter * c, quarter), quarter), 0], ctv, lsem.at[2]
        ),
    ]
    mine = pl.ds(pl.multiple_of(c * rows, rows), rows)
    mine_wide = pl.ds(pl.multiple_of(c * wide, wide), wide)
    sources = (w_one, w_two, w_flux, wo_one, wo_two)
    near = (w1.at[c], w2.at[c], wf.at[mine, :], wa.at[:, mine_wide], wb.at[mine_wide, :])
    early = [pltpu.make_async_copy(atmos_all, atmos, msem.at[5])]
    for i in range(5):
        early.append(pltpu.make_async_copy(sources[i], near[i], msem.at[i]))
    for load in early + loads:
        load.start()
    early[0].wait()
    eye = lax.broadcasted_iota(jnp.int32, (rows, rows), 0) == lax.broadcasted_iota(
        jnp.int32, (rows, rows), 1
    )
    for r in (0, lats - 1) + tuple(range(1, lats - 1)):
        for j in range(4):
            al[j, :, r * width : (r + 1) * width] = taken(
                atmos, r * LON + j * stride, width
            ).astype(BF16)
    tapt[...] = jnp.zeros(tapt.shape, F32)
    for i in range(3):
        tapt[i : i + 1, :rows] = taps[i]
    pl.semaphore_wait(pltpu.get_barrier_semaphore(), bands - 1 + 4)

    cuts = (
        slice(0, width), slice((lats - 1) * width, lats * width), slice(width, (lats - 1) * width)
    )
    acopies = [[], [], []]

    def send_state(k):
        lo, hi = cuts[k].start, cuts[k].stop
        for d, to in pairs:
            acopies[k].append(
                send(
                    al.at[to, :, lo:hi], ext.at[mine, width + lo : width + hi],
                    as_.at[k, d], ar.at[k, d], b, to,
                )
            )

    send_state(0)
    send_state(1)
    theirs = pl.ds(pl.multiple_of(across * rows, rows), rows)
    theirs_wide = pl.ds(pl.multiple_of(across * wide, wide), wide)
    far = (
        w1.at[across], w2.at[across], wf.at[theirs, :],
        wa.at[:, theirs_wide], wb.at[theirs_wide, :],
    )
    first, second, third, tcopies = [], [], [], []
    for i in range(5):
        early[i + 1].wait()
        second.append(send(near[i], near[i], ws.at[1, i], wr.at[1, i], flip, across))
        first.append(send(near[i], near[i], ws.at[0, i], wr.at[0, i], b, mate))
    for d, to in pairs:
        tcopies.append(send(tapt, tapr.at[c], ts.at[d], tr.at[d], b, to))
    send_state(2)
    ext[mine, width : width + share] = al[c]
    tapr[c] = tapt[...]
    for i in range(points // PTS):
        mk[:, i * PTS : (i + 1) * PTS] = sea[i : i + 1, :].astype(F32)
    for r in range(lats):
        for j in range(4):
            mk4[j, :, r * width : (r + 1) * width] = taken(mk, r * LON + j * stride, width)
    for k in (0, 1):
        for copy in acopies[k]:
            copy.wait()
    halo = [
        send(
            ext.at[:, lats * width : (lats + 1) * width], ext.at[:, :width],
            hs.at[0], hr.at[0], down, c,
        ),
        send(
            ext.at[:, width : 2 * width], ext.at[:, (lats + 1) * width :],
            hs.at[1], hr.at[1], up, c,
        ),
    ]
    for copy in tcopies:
        copy.wait()
    for j in range(4):
        for i in range(3):
            tapf[j * rows : (j + 1) * rows, i : i + 1] = jnp.sum(
                jnp.where(eye, tapr[j, i : i + 1, :rows], 0.0), axis=1, keepdims=True
            )
    t0, t1, t2 = tapf[:, 0:1], tapf[:, 1:2], tapf[:, 2:3]
    lane = lax.broadcasted_iota(jnp.int32, (1, share), 1) % width
    kept = jnp.where((lane < stride) | (c == 3), 1.0, 0.0)
    sea_kept = mk4[c] * kept
    for i in range(5):
        second[i].wait_recv()
        third.append(send(far[i], far[i], ws.at[2, i], wr.at[2, i], b, mate))
    for copy in acopies[2]:
        copy.wait()
    for i in range(3):
        first[i].wait()
        second[i].wait_send()
        third[i].wait()
    fcopies = []
    line = (1, 2, 0, 3)
    for r in line:
        if r == 0:
            for copy in halo:
                copy.wait()

            @pl.when(b == 0)
            def _():
                ext[:, :width] = jnp.zeros((full, width), BF16)

            @pl.when(b == bands - 1)
            def _():
                ext[:, (lats + 1) * width :] = jnp.zeros((full, width), BF16)

        cols = slice(r * width, (r + 1) * width)
        state = ext[:, (r + 1) * width : (r + 2) * width].astype(F32)
        zcol = (
            t0 * ext[:, r * width : (r + 1) * width].astype(F32)
            + t1 * state
            + t2 * ext[:, (r + 2) * width : (r + 3) * width].astype(F32)
        ).astype(BF16)
        zb[:, cols] = zcol
        total = None
        for i in range(4):
            u = tn(w1[i], zcol)
            sig = sigmoid(u)
            act = u * sig
            h = act.astype(BF16)
            hid[i, :, cols] = h
            slope[i, :, cols] = (sig + act * (1.0 - sig)).astype(BF16)
            piece = tn(w2[i], h)
            total = piece if total is None else total + piece
        acol = (state + total).astype(BF16)
        acol = (acol.astype(F32) * sea_kept[:, cols]).astype(BF16)
        alm[:, cols] = acol
        fx[r] = tn(acol, wf[...]).astype(BF16).reshape(fx.shape[1:])
        for d, to in pairs:
            i0 = (to + 3 * r + c) % 4
            k0 = (row_groups * r + few * c + i0) // 4
            twice = ((i0 + 1) // 4) * ((6 - c) // 4)
            k2 = k0 + 2 + twice * (blocks + 1 + 4 * c + r - k0 - 2)
            fcopies.append(
                send(
                    fx.at[r, 0:2, i0], fm.at[pl.ds(k0, 2)], fxs.at[r, d, 0], fxr.at[r, d, 0], b, to
                )
            )
            fcopies.append(
                send(
                    fx.at[r, 2:3, i0], fm.at[pl.ds(k2, 1)], fxs.at[r, d, 1], fxr.at[r, d, 1], b, to
                )
            )
        i0 = (2 * c + 3 * r) % 4
        k0 = (row_groups * r + few * c + i0) // 4
        twice = ((i0 + 1) // 4) * ((6 - c) // 4)
        k2 = k0 + 2 + twice * (blocks + 1 + 4 * c + r - k0 - 2)
        fm[pl.ds(k0, 2)] = fx[r, 0:2, i0]
        fm[k2] = fx[r, 2, i0]
    fm[blocks] = jnp.zeros(fm.shape[1:], BF16)
    span = 2 * ZLEN
    size = span * quarter
    r = lax.broadcasted_iota(jnp.int32, (size, size), 0)
    k = lax.broadcasted_iota(jnp.int32, (size, size), 1)
    perm[...] = jnp.where((r % span) * quarter + r // span == k, 1.0, 0.0).astype(BF16)
    go1[...] = jnp.zeros(go1.shape, F32)
    go2[...] = jnp.zeros(go2.shape, F32)
    for load in loads:
        load.wait()
    for i in range(3, 5):
        first[i].wait()
        second[i].wait_send()
        third[i].wait()
    for copy in fcopies:
        copy.wait()

    def pack(s, _):
        sp[s] = fm[table[0, s]]
        return 0

    lax.fori_loop(0, 2 * bands, pack, 0)
    turn = [(z + i) % ZLEN for i in range(ZLEN)]

    def couple(d, start):
        base = ((q + d) % groups) * ZLEN
        for i in range(start, ZLEN):
            to = base + turn[i]
            send(sp.at[pl.ds(2 * to, 2)], rf.at[pl.ds(2 * b, 2)], ss, sr.at[d], to, c)

    couple(0, 1)

    def couple_all(d, _):
        couple(d, 0)
        return 0

    lax.fori_loop(1, groups, couple_all, 0)
    rf[pl.ds(2 * b, 2)] = sp[pl.ds(2 * b, 2)]
    for r in range(lats):
        for j in range(4):
            cl[j, :, r * width : (r + 1) * width] = taken(
                ctv0, r * LON + j * stride, width
            ).astype(BF16)
    ctcopies = []
    for d, to in pairs:
        ctcopies.append(send(cl.at[to], ctb.at[mine, :], cs.at[d], cr.at[d], b, to))
    ctb[mine, :] = cl[c]
    drain(rf.at[pl.ds(0, span - 2)], sr.at[0])

    def step(d, _):
        @pl.when(d > 0)
        def _():
            drain(rf.at[pl.ds(0, span)], sr.at[d])

        src = (q + groups - d) % groups
        at = pl.ds(pl.multiple_of(src * span, span), span)
        force = nn(perm[...], rf[at].reshape(size, PTS)).astype(BF16)
        both = jnp.concatenate([st[:, at, :].reshape(size, PTS), force], axis=1)
        cot = ctv[:, at, :].reshape(size, PTS)
        pre = nn(both, wa[...])
        sig = sigmoid(pre)
        act = pre * sig
        grad = (nt(cot, wb[...]) * (sig + act * (1.0 - sig))).astype(BF16)
        back = nt(grad, wa[...])
        bk[at] = tn(perm[...], back[:, PTS:].astype(BF16)).astype(BF16).reshape(span, quarter, PTS)

        def give(i):
            to = src * ZLEN + turn[i]
            send(bk.at[pl.ds(2 * to, 2)], rb.at[pl.ds(2 * b, 2)], rs, rr, to, c)

        @pl.when(d > 0)
        def _():
            give(0)

        for i in range(1, ZLEN):
            give(i)
        ds[:, at, :] = (
            (cot.astype(F32) + back[:, :PTS]).astype(BF16).reshape(quarter, span, PTS)
        )
        go2[...] += tn(cot, act.astype(BF16))
        go1[...] += tn(both, grad)
        return 0

    lax.fori_loop(0, groups, step, 0)
    dstore = pltpu.make_async_copy(ds, dst, lsem.at[3])
    dstore.start()
    rb[pl.ds(2 * b, 2)] = bk[pl.ds(2 * b, 2)]
    for i in range(4):
        gso[i, :256] = go1[:, i * 128 : i * 128 + 128].astype(BF16)
        gso[i, 256:] = go2[:, i * 128 : i * 128 + 128].astype(BF16)
    ocopies = [
        send(gso.at[diag], rao.at[1], os_.at[1], or_.at[1], b, mate),
        send(gso.at[mate], rao.at[0], os_.at[0], or_.at[0], b, mate),
    ]
    for copy in ctcopies:
        copy.wait()
    drain(rb.at[pl.ds(0, 2 * bands - 2)], rr)

    def unpack(k, _):
        dfp[k] = rb[table[1, k]]
        return 0

    lax.fori_loop(0, blocks, unpack, 0)
    dcopies = []
    for r in range(lats):
        for d, to in pairs:
            i0 = (c + 3 * r + to) % 4
            k0 = (row_groups * r + few * to + i0) // 4
            dcopies.append(
                send(dfp.at[pl.ds(k0, 3)], dfb.at[r, :, i0], dfs.at[r, d], dfr.at[r, d], b, to)
            )
        i0 = (2 * c + 3 * r) % 4
        k0 = (row_groups * r + few * c + i0) // 4
        dfb[r, :, i0] = dfp[pl.ds(k0, 3)]
    for copy in ocopies:
        copy.wait()
    side = q % 2
    little, big = rxo.shape[1], rw.shape[1]
    kept_little = pl.ds(pl.multiple_of(little * side, little), little)
    sent_little = pl.ds(pl.multiple_of(little * (1 - side), little), little)
    kept_big = pl.ds(pl.multiple_of(big * side, big), big)
    sent_big = pl.ds(pl.multiple_of(big * (1 - side), big), big)
    hxo[...] = (gso[across].astype(F32) + rao[1].astype(F32)).astype(BF16)
    owno[...] = gso[c].astype(F32) + rao[0].astype(F32)
    ownob[...] = owno[sent_little].astype(BF16)
    for copy in dcopies:
        copy.wait()
    ocopies = [
        send(ownob, rxo.at[2], os_.at[4], or_.at[4], flip, c),
        send(hxo.at[kept_little], rxo.at[0], os_.at[2], or_.at[2], b, across),
        send(hxo.at[sent_little], rxo.at[1], os_.at[3], or_.at[3], flip, across),
    ]
    flux = dfb[...].reshape(share, PTS)
    gb[...] = (ctb[...].astype(F32) * kept + nt(wf[...], flux) * sea_kept).astype(BF16)
    gwf[...] = nn(alm[...], flux)
    wcopies = []
    halo = []
    for turn, i in enumerate((mate, c, diag, across)):
        for r in (0, 3, 1, 2):
            cols = slice(r * width, (r + 1) * width)
            du = (nn(w2[i], gb[:, cols]) * slope[i, :, cols].astype(F32)).astype(BF16)
            dubuf[:, cols] = du
            piece = nn(w1[i], du)
            if turn == 0:
                dzacc[:, cols] = piece
            elif turn < 3:
                dzacc[:, cols] += piece
            else:
                at = (r + 1) * width
                dext[:, at : at + width] = (dzacc[:, cols] + piece).astype(BF16)
                if r == 0:
                    halo.append(
                        send(
                            dext.at[:, at : at + width], dext.at[:, (lats + 1) * width :],
                            h2s.at[1], h2r.at[1], up, c,
                        )
                    )
                if r == 3:
                    halo.append(
                        send(
                            dext.at[:, at : at + width], dext.at[:, :width],
                            h2s.at[0], h2r.at[0], down, c,
                        )
                    )
        g1 = nt(zb[...], dubuf[...])
        g2 = nt(hid[i], gb[...])
        for j in range(2):
            gs[i, j * 256 : j * 256 + 256] = g1[:, j * 128 : j * 128 + 128].astype(BF16)
            gs[i, 512 + j * 256 : 768 + j * 256] = g2[:, j * 128 : j * 128 + 128].astype(BF16)
        gs[i, 1024:1088] = gwf[pl.ds(pl.multiple_of(rows * i, rows), rows), :].astype(BF16)
        if turn == 0:
            mcopies = [send(gs.at[mate], ra.at[0], s0.at[0], q0.at[0], b, mate)]
        if turn == 1:
            mcopies[0].wait()
            own[...] = gs[c].astype(F32) + ra[0].astype(F32)
            ownb[...] = own[sent_big].astype(BF16)
            wcopies.append(send(ownb, rw.at[2], s0.at[4], q0.at[4], flip, c))
        if turn == 2:
            mcopies.append(send(gs.at[diag], ra.at[1], s0.at[1], q0.at[1], b, mate))
        if turn == 3:
            mcopies[1].wait()
            hx[...] = (gs[across].astype(F32) + ra[1].astype(F32)).astype(BF16)
            wcopies.append(send(hx.at[kept_big], rw.at[0], s0.at[2], q0.at[2], b, across))
            wcopies.append(send(hx.at[sent_big], rw.at[1], s0.at[3], q0.at[3], flip, across))
    gkp[...] = jnp.zeros(gkp.shape, F32)
    for i in range(3):
        acc = jnp.zeros((full, 128), F32)
        for r in range(lats):
            prod = ext[:, (r + i) * width : (r + i + 1) * width].astype(F32) * dext[
                :, (r + 1) * width : (r + 2) * width
            ].astype(F32)
            for o in range(0, width, 128):
                acc = acc + prod[:, o : o + 128]
        acc = jnp.sum(acc, axis=1, keepdims=True)
        for j in range(4):
            gkp[j, i : i + 1, :rows] = jnp.sum(
                jnp.where(eye, acc[j * rows : (j + 1) * rows], 0.0), axis=0, keepdims=True
            )
    kcopies = []
    for d, to in pairs:
        kcopies.append(send(gkp.at[to], gkr.at[d], gks.at[d], gkq.at[d], b, to))
    dcopies = []

    def spread(r):
        cols = slice(r * width, (r + 1) * width)
        dl[:, cols] = (
            gb[:, cols].astype(F32)
            + t0 * dext[:, (r + 2) * width : (r + 3) * width].astype(F32)
            + t1 * dext[:, (r + 1) * width : (r + 2) * width].astype(F32)
            + t2 * dext[:, r * width : (r + 1) * width].astype(F32)
        ).astype(BF16)

    def send_back(k):
        lo, hi = cuts[k].start, cuts[k].stop
        for d, to in pairs:
            theirs = pl.ds(pl.multiple_of(rows * to, rows), rows)
            dcopies.append(
                send(dl.at[theirs, lo:hi], dq.at[c, :, lo:hi], das.at[k, d], dar.at[k, d], b, to)
            )

    spread(1)
    spread(2)
    for copy in ocopies:
        copy.wait()
    t[big + 32 :] = (
        owno[kept_little]
        + rxo[0].astype(F32)
        + rxo[1].astype(F32)
        + rxo[2].astype(F32)
    ).astype(BF16)
    for copy in kcopies:
        copy.wait()
    t[big : big + 16] = (gkp[c] + gkr[1] + gkr[2] + gkr[3]).astype(BF16)
    t[big + 16 : big + 32] = jnp.zeros((16, 128), BF16)
    for copy in wcopies:
        copy.wait()
    t[:big] = (
        own[kept_big] + rw[0].astype(F32) + rw[1].astype(F32) + rw[2].astype(F32)
    ).astype(BF16)
    size = r1.shape[1]
    x, xs = q // 2, groups // 2
    copies = []
    for d in range(1, xs):
        to = (x + d) % xs
        cut = pl.ds(pl.multiple_of(to * size, size), size)
        copies.append(
            send(t.at[cut], r1.at[x], s1.at[d], q1.at[d], (2 * to + side) * ZLEN + z, c)
        )
    r1[x] = t[pl.ds(pl.multiple_of(x * size, size), size)]
    for copy in halo:
        copy.wait()

    @pl.when(b == 0)
    def _():
        dext[:, :width] = jnp.zeros((full, width), BF16)

    @pl.when(b == bands - 1)
    def _():
        dext[:, (lats + 1) * width :] = jnp.zeros((full, width), BF16)

    spread(0)
    spread(3)
    dq[c] = dl[mine, :]
    for copy in copies:
        copy.wait()
    total = r1[0].astype(F32)
    for i in range(1, xs):
        total = total + r1[i].astype(F32)
    fs[...] = total.reshape(fs.shape)
    copies = []
    for d in range(1, ZLEN):
        to = (z + d) % ZLEN
        copies.append(send(fs.at[to], r2.at[z], s2.at[d], q2.at[d], q * ZLEN + to, c))
    for k in range(3):
        send_back(k)
    r2[z] = fs[z]
    for copy in copies:
        copy.wait()
    total = r2[0]
    for i in range(1, ZLEN):
        total = total + r2[i]
    fr[...] = total
    copies = []
    for d in range(1, ZLEN):
        to = (z + d) % ZLEN
        copies.append(send(fr, ag.at[z], s3.at[d], q3.at[d], q * ZLEN + to, c))
    ag[z] = total
    for copy in copies:
        copy.wait()
    tb[...] = ag[...].reshape(size, 128).astype(BF16)
    copies = []
    cut = pl.ds(pl.multiple_of((side * xs + x) * size, size), size)
    for d in range(1, groups):
        to = (q + d) % groups
        copies.append(send(tb, out.at[cut], s4.at[d], q4.at[d], to * ZLEN + z, c))
    out[cut] = tb[...]
    for copy in dcopies:
        copy.wait()
    for r in range(lats):
        for j in range(4):
            start = r * LON + j * stride
            extra = start % 128
            piece = dq[j, :, r * width : (r + 1) * width]
            if extra == 0:
                dat[:, start : start + width] = piece
                continue
            base = start - extra
            moved = jnp.concatenate([piece.astype(F32), jnp.zeros((rows, 128), F32)], axis=1)
            moved = pltpu.roll(moved, extra, axis=1)
            lead = lax.broadcasted_iota(jnp.int32, (rows, 128), 1)
            dat[:, base : base + 128] = jnp.where(
                lead < extra, dat[:, base : base + 128].astype(F32), moved[:, :128]
            ).astype(BF16)
            dat[:, base + 128 : base + 128 + width] = moved[:, 128:].astype(BF16)
    astore = pltpu.make_async_copy(dat, dat_all, lsem.at[4])
    astore.start()
    for copy in copies:
        copy.wait()
    drain(sp.at[pl.ds(0, 2 * bands - 2)], ss)
    drain(bk.at[pl.ds(0, 2 * bands - 2)], rs)
    dstore.wait()
    astore.wait()


def local(
    atmos, kernels, w_one, w_two, w_flux, sea_mask, route,
    ocean_state, ct_atmos, ct_ocean, wo_one, wo_two,
):
    chans = lax.axis_size("chan")
    bands = lax.axis_size("band")
    rows, points = atmos.shape
    blocks = points // PTS
    quarter = PTS // chans
    lats = points // LON
    share = lats * (LON // quarter // chans + 1) * quarter
    width = share // lats
    slots = ocean_state.shape[2]
    hid = w_one.shape[2]
    full = rows * chans
    wide = wo_one.shape[1]
    total = wide * chans
    groups = bands // ZLEN
    flat = 1536
    big, little = 1088, 384
    size = flat // groups
    small = size // ZLEN
    vm = pl.BlockSpec(memory_space=VMEM)
    sm = pl.BlockSpec(memory_space=pltpu.SMEM)
    anywhere = pl.BlockSpec(memory_space=pl.ANY)

    table = pl.pallas_call(
        table_kernel,
        out_shape=jax.ShapeDtypeStruct((8, 128), jnp.int32),
        in_specs=[vm],
        out_specs=vm,
    )(route.T)
    ocean = VMEM((slots, quarter, PTS), BF16)
    points_first = VMEM((quarter, slots, PTS), BF16)
    split = VMEM((chans, rows, share), BF16)
    extended = VMEM((full, share + 2 * width), BF16)
    square = VMEM((full, share), BF16)
    grouped = VMEM((lats, width // PTS, chans, quarter, PTS), BF16)
    dat, dst, out = pl.pallas_call(
        main_kernel,
        out_shape=[
            jax.ShapeDtypeStruct((rows, points), BF16),
            jax.ShapeDtypeStruct((quarter, slots, PTS), BF16),
            jax.ShapeDtypeStruct((flat, 128), BF16),
        ],
        in_specs=[sm, vm, vm] + [anywhere] * 9,
        out_specs=[anywhere, anywhere, vm],
        scratch_shapes=[
            VMEM((rows, points), BF16),
            VMEM((rows, points), BF16),
            split, split, extended, square, square,
            VMEM((8, 128), F32),
            VMEM((chans, 8, 128), F32),
            VMEM((full, 128), F32),
            VMEM((chans, full, hid), BF16),
            VMEM((chans, hid, full), BF16),
            VMEM((full, PTS), BF16),
            grouped,
            VMEM((blocks + 1 + 4 * lats, quarter, PTS), BF16),
            VMEM((1, points), F32),
            VMEM((chans, 1, share), F32),
            VMEM((chans, hid, share), BF16),
            VMEM((chans, hid, share), BF16),
            VMEM((rows, points), BF16),
            square, ocean, ocean, ocean, ocean, points_first, points_first, points_first,
            VMEM((2 * PTS, total), BF16),
            VMEM((total, PTS), BF16),
            VMEM((2 * ZLEN * quarter, 2 * ZLEN * quarter), BF16),
            VMEM((2 * PTS, total), F32),
            VMEM((PTS, total), F32),
            VMEM((blocks, quarter, PTS), BF16),
            grouped, square, extended, square, split,
            VMEM((full, share), F32),
            VMEM((hid, share), BF16),
            VMEM((full, PTS), F32),
            VMEM((chans, 16, 128), F32),
            VMEM((chans, 16, 128), F32),
            VMEM((chans, big, 128), BF16),
            VMEM((2, big, 128), BF16),
            VMEM((big, 128), BF16),
            VMEM((3, big // 2, 128), BF16),
            VMEM((chans, little, 128), BF16),
            VMEM((2, little, 128), BF16),
            VMEM((little, 128), BF16),
            VMEM((3, little // 2, 128), BF16),
            VMEM((big, 128), F32),
            VMEM((little, 128), F32),
            VMEM((big // 2, 128), BF16),
            VMEM((little // 2, 128), BF16),
            VMEM((flat // 2, 128), BF16),
            VMEM((groups // 2, size, 128), BF16),
            VMEM((ZLEN, small, 128), F32),
            VMEM((ZLEN, small, 128), F32),
            VMEM((small, 128), F32),
            VMEM((ZLEN, small, 128), F32),
            VMEM((size, 128), BF16),
            DMA((5,)), DMA((6,)), DMA((2,)), DMA((2,)), DMA((3, 5)), DMA((3, 5)), DMA((4,)), DMA((4,)),
            DMA((3, 4)), DMA((3, 4)), DMA((lats, 4, 2)), DMA((lats, 4, 2)), DMA((4,)), DMA((4,)),
            DMA, DMA((groups,)), DMA, DMA,
            DMA((5,)), DMA((5,)), DMA((lats, 4)), DMA((lats, 4)), DMA((2,)), DMA((2,)),
            DMA((4,)), DMA((4,)), DMA((3, 4)), DMA((3, 4)), DMA((5,)), DMA((5,)),
            DMA((groups,)), DMA((groups,)), DMA((ZLEN,)), DMA((ZLEN,)),
            DMA((ZLEN,)), DMA((ZLEN,)), DMA((groups,)), DMA((groups,)),
        ],
        compiler_params=pltpu.CompilerParams(
            collective_id=0, has_side_effects=True, vmem_limit_bytes=LIMIT
        ),
    )(
        table, kernels.transpose(1, 0, 2), sea_mask.reshape(blocks, PTS), atmos, w_one[0], w_two[0],
        w_flux, wo_one, wo_two, ct_atmos, ocean_state, ct_ocean,
    )
    datmos, dk, dw1, dw2, dwf, dstate, do1, do2 = pl.pallas_call(
        finish_kernel,
        out_shape=[
            jax.ShapeDtypeStruct(dat.shape, BF16),
            jax.ShapeDtypeStruct((3, 1, rows), F32),
            jax.ShapeDtypeStruct((full, hid), F32),
            jax.ShapeDtypeStruct((hid, full), F32),
            jax.ShapeDtypeStruct((rows, PTS), F32),
            jax.ShapeDtypeStruct(dst.shape, BF16),
            jax.ShapeDtypeStruct((2 * PTS, wide), F32),
            jax.ShapeDtypeStruct((wide, PTS), F32),
        ],
        in_specs=[anywhere] * 3,
        out_specs=[anywhere, vm, vm, vm, vm, anywhere, vm, vm],
        scratch_shapes=[
            VMEM(dat.shape, BF16), VMEM(dst.shape, BF16), VMEM(out.shape, BF16), DMA((3,)), DMA((2,)),
        ],
        compiler_params=pltpu.CompilerParams(vmem_limit_bytes=LIMIT + (4 << 20)),
    )(dat, dst, out)
    return datmos, dk.transpose(1, 0, 2), dw1[None], dw2[None], dwf, dstate[:, None], do1, do2


def solution(mesh):
    in_specs = (
        P("chan", "band"),
        P(None, None, "chan"),
        P(None, None, "chan"),
        P(None, "chan", None),
        P("chan", None),
        P("band"),
        P("band", None),
        P(None, "band", None, None),
        P("chan", "band"),
        P(None, "band", None, None),
        P(None, "chan"),
        P("chan", None),
    )
    out_specs = (
        P("chan", "band"),
        P(None, None, "chan"),
        P(None, None, "chan"),
        P(None, "chan", None),
        P("chan", None),
        P("chan", "band", None, None),
        P(None, "chan"),
        P("chan", None),
    )
    return jax.shard_map(local, mesh=mesh, in_specs=in_specs, out_specs=out_specs, check_vma=False)
```

```python
import functools

import jax
import jax.numpy as jnp
from jax import lax
from jax.experimental import pallas as pl
from jax.experimental.pallas import tpu as pltpu
from jax.sharding import PartitionSpec as P

PTS = 128
LON = 1440
MESH = pl.DeviceIdType.MESH
F32 = jnp.float32
BF16 = jnp.bfloat16
VMEM = pltpu.VMEM
DMA = pltpu.SemaphoreType.DMA
ZLEN = 8
LIMIT = 56 * 1024 * 1024


def nn(a, b):
    return lax.dot_general(a, b, (((1,), (0,)), ((), ())), preferred_element_type=F32)


def tn(a, b):
    return lax.dot_general(a, b, (((0,), (0,)), ((), ())), preferred_element_type=F32)


def nt(a, b):
    return lax.dot_general(a, b, (((1,), (1,)), ((), ())), preferred_element_type=F32)


def sigmoid(v):
    return 0.5 * jnp.tanh(0.5 * v) + 0.5


def place():
    b, c = lax.axis_index("band"), lax.axis_index("chan")
    mate = (c // 2) * 2 + (1 - c % 2)
    return b, c, mate, (c + 2) % 4, (mate + 2) % 4


def send(src, dst, ssem, rsem, b, c):
    copy = pltpu.make_async_remote_copy(
        src_ref=src,
        dst_ref=dst,
        send_sem=ssem,
        recv_sem=rsem,
        device_id=(b, c),
        device_id_type=MESH,
    )
    copy.start()
    return copy


def drain(ref, sem):
    pltpu.make_async_copy(ref, ref, sem).wait()


def signal(b, c):
    pl.semaphore_signal(
        pltpu.get_barrier_semaphore(), inc=1, device_id=(b, c), device_id_type=MESH
    )


def taken(ref, start, width):
    extra = start % 128
    if extra == 0:
        return ref[:, start : start + width].astype(F32)
    wide = ref[:, start - extra : start - extra + width + 128].astype(F32)
    return pltpu.roll(wide, width + 128 - extra, axis=1)[:, :width]


def tables(row):
    blocks = row.shape[1]
    k = lax.broadcasted_iota(jnp.int32, (blocks, blocks), 0)
    j = lax.broadcasted_iota(jnp.int32, (blocks, blocks), 1)
    col = jnp.sum(jnp.where(k == j, row, 0), axis=1, keepdims=True)
    rank = jnp.sum(jnp.where((row == col) & (j < k), 1, 0), axis=1, keepdims=True)
    slot = col * 2 + rank
    k = lax.broadcasted_iota(jnp.int32, (blocks, 128), 0)
    s = lax.broadcasted_iota(jnp.int32, (blocks, 128), 1)
    inv = blocks + jnp.sum(jnp.where(slot == s, k - blocks, 0), axis=0, keepdims=True)
    back = jnp.sum(jnp.where(k == s, slot, 0), axis=0, keepdims=True)
    line = lax.broadcasted_iota(jnp.int32, (8, 128), 0)
    return jnp.where(line == 0, inv, back)


def finish_kernel(dat, dst, out, datmos, dk, dw1, dw2, dwf, dstate, do1, do2):
    half = out.shape[0] // 2
    datmos[...] = dat[...]
    dstate[...] = dst[...]
    dw1[:, :128] = out[:256].astype(F32)
    dw1[:, 128:] = out[256:512].astype(F32)
    dw2[:32, :128] = out[512:544].astype(F32)
    dw2[32:, :128] = out[half : half + 224].astype(F32)
    dw2[:, 128:] = out[half + 224 : half + 480].astype(F32)
    dwf[...] = out[half + 480 : half + 544].astype(F32)
    tile = out[544:560].astype(F32) + out[half + 544 : half + 560].astype(F32)
    for i in range(3):
        dk[i] = tile[i : i + 1, :64]
    do1[:192] = out[576:768].astype(F32)
    do1[192:] = out[half + 576 : half + 640].astype(F32)
    do2[...] = out[half + 640 :].astype(F32).T


def main_kernel(
    route, taps, sea, atmos_all, w_one, w_two, w_flux, wo_one, wo_two, ct_all, state_all, cot_all,
    dat_all, dst, out,
    tabv, table, atmos, dat, al, cl, ext, zb, alm, tapt, tapr, tapf, w1, w2, wf, fx, fm, mk, mk4, hid, slope,
    ctv0, ctb, sp, rf, bk, rb, st, ctv, ds, wa, wb, perm, go1, go2,
    dfp, dfb, gb, dext, dl, dq, dzacc, dubuf, gwf, gkp, gkr,
    gs, ra, hx, rw, gso, rao, hxo, rxo, own, owno, ownb, ownob, t, r1, fs, r2, fr, ag, tb,
    lsem, msem, hs, hr, ws, wr, ts, tr, as_, ar, fxs, fxr, cs, cr, ss, sr, rs, rr,
    os_, or_, dfs, dfr, h2s, h2r, gks, gkq, das, dar, s0, q0, s1, q1, s2, q2, s3, q3, s4, q4,
):
    b, c, mate, across, diag = place()
    bands = lax.axis_size("band")
    up, down = (b + bands - 1) % bands, (b + 1) % bands
    q, z = b // ZLEN, b % ZLEN
    groups = bands // ZLEN
    flip = ((q // 2) * 2 + (1 - q % 2)) * ZLEN + z
    rows, points = atmos.shape
    full, share = zb.shape
    lats = points // LON
    width = share // lats
    quarter = st.shape[0]
    blocks = dfp.shape[0]
    row_groups = LON // quarter
    few = row_groups // 4
    stride = few * quarter
    wide = wo_one.shape[1]
    peers = [(c + 2) % 4, (c + 1) % 4, (c + 3) % 4]
    order = (2, 1, 3)
    pairs = list(zip(order, peers))

    turn = [(z + i) % ZLEN for i in range(ZLEN)]
    for d in (1, 2, 3):
        signal(b, (c + d) % 4)
    signal(flip, across)
    for i in range(1, ZLEN):
        signal(q * ZLEN + turn[i], c)

    def greet(d, _):
        base = ((q + d) % groups) * ZLEN
        for i in range(ZLEN):
            signal(base + turn[i], c)
        return 0

    lax.fori_loop(1, groups, greet, 0)
    loads = [
        pltpu.make_async_copy(ct_all, ctv0, lsem.at[0]),
        pltpu.make_async_copy(
            state_all.at[pl.ds(pl.multiple_of(quarter * c, quarter), quarter), 0], st, lsem.at[1]
        ),
        pltpu.make_async_copy(
            cot_all.at[pl.ds(pl.multiple_of(quarter * c, quarter), quarter), 0], ctv, lsem.at[2]
        ),
    ]
    mine = pl.ds(pl.multiple_of(c * rows, rows), rows)
    mine_wide = pl.ds(pl.multiple_of(c * wide, wide), wide)
    sources = (w_one, w_two, w_flux, wo_one, wo_two)
    near = (w1.at[c], w2.at[c], wf.at[mine, :], wa.at[:, mine_wide], wb.at[mine_wide, :])
    early = [pltpu.make_async_copy(atmos_all, atmos, msem.at[5])]
    for i in range(5):
        early.append(pltpu.make_async_copy(sources[i], near[i], msem.at[i]))
    for load in early + loads:
        load.start()
    tabv[...] = tables(route[...])
    tcopy = pltpu.make_async_copy(tabv, table, msem.at[6])
    tcopy.start()
    early[0].wait()
    eye = lax.broadcasted_iota(jnp.int32, (rows, rows), 0) == lax.broadcasted_iota(
        jnp.int32, (rows, rows), 1
    )
    for r in (0, lats - 1) + tuple(range(1, lats - 1)):
        for j in range(4):
            al[j, :, r * width : (r + 1) * width] = taken(
                atmos, r * LON + j * stride, width
            ).astype(BF16)
    tapt[...] = jnp.zeros(tapt.shape, F32)
    for i in range(3):
        tapt[i : i + 1, :rows] = taps[i]
    tcopy.wait()
    pl.semaphore_wait(pltpu.get_barrier_semaphore(), bands - 1 + 4)

    cuts = (
        slice(0, width), slice((lats - 1) * width, lats * width), slice(width, (lats - 1) * width)
    )
    acopies = [[], [], []]

    def send_state(k):
        lo, hi = cuts[k].start, cuts[k].stop
        for d, to in pairs:
            acopies[k].append(
                send(
                    al.at[to, :, lo:hi], ext.at[mine, width + lo : width + hi],
                    as_.at[k, d], ar.at[k, d], b, to,
                )
            )

    send_state(0)
    send_state(1)
    theirs = pl.ds(pl.multiple_of(across * rows, rows), rows)
    theirs_wide = pl.ds(pl.multiple_of(across * wide, wide), wide)
    far = (
        w1.at[across], w2.at[across], wf.at[theirs, :],
        wa.at[:, theirs_wide], wb.at[theirs_wide, :],
    )
    first, second, third, tcopies = [], [], [], []
    for i in range(5):
        early[i + 1].wait()
        second.append(send(near[i], near[i], ws.at[1, i], wr.at[1, i], flip, across))
        first.append(send(near[i], near[i], ws.at[0, i], wr.at[0, i], b, mate))
    for d, to in pairs:
        tcopies.append(send(tapt, tapr.at[c], ts.at[d], tr.at[d], b, to))
    ext[mine, width : width + share] = al[c]
    tapr[c] = tapt[...]
    for copy in acopies[0]:
        copy.wait()
    halo = [
        send(
            ext.at[:, width : 2 * width], ext.at[:, (lats + 1) * width :],
            hs.at[1], hr.at[1], up, c,
        )
    ]
    for copy in acopies[1]:
        copy.wait()
    halo.append(
        send(
            ext.at[:, lats * width : (lats + 1) * width], ext.at[:, :width],
            hs.at[0], hr.at[0], down, c,
        )
    )
    send_state(2)
    for i in range(points // PTS):
        mk[:, i * PTS : (i + 1) * PTS] = sea[i : i + 1, :].astype(F32)
    for r in range(lats):
        for j in range(4):
            mk4[j, :, r * width : (r + 1) * width] = taken(mk, r * LON + j * stride, width)
    for copy in tcopies:
        copy.wait()
    for j in range(4):
        for i in range(3):
            tapf[j * rows : (j + 1) * rows, i : i + 1] = jnp.sum(
                jnp.where(eye, tapr[j, i : i + 1, :rows], 0.0), axis=1, keepdims=True
            )
    t0, t1, t2 = tapf[:, 0:1], tapf[:, 1:2], tapf[:, 2:3]
    lane = lax.broadcasted_iota(jnp.int32, (1, share), 1) % width
    kept = jnp.where((lane < stride) | (c == 3), 1.0, 0.0)
    sea_kept = mk4[c] * kept
    for i in range(5):
        second[i].wait_recv()
        third.append(send(far[i], far[i], ws.at[2, i], wr.at[2, i], b, mate))
    for copy in acopies[2]:
        copy.wait()
    for i in range(3):
        first[i].wait()
        second[i].wait_send()
        third[i].wait()
    fcopies = []
    line = (1, 2, 0, 3)
    for r in line:
        if r == 0:
            for copy in halo:
                copy.wait()

            @pl.when(b == 0)
            def _():
                ext[:, :width] = jnp.zeros((full, width), BF16)

            @pl.when(b == bands - 1)
            def _():
                ext[:, (lats + 1) * width :] = jnp.zeros((full, width), BF16)

        cols = slice(r * width, (r + 1) * width)
        state = ext[:, (r + 1) * width : (r + 2) * width].astype(F32)
        zcol = (
            t0 * ext[:, r * width : (r + 1) * width].astype(F32)
            + t1 * state
            + t2 * ext[:, (r + 2) * width : (r + 3) * width].astype(F32)
        ).astype(BF16)
        zb[:, cols] = zcol
        total = None
        for i in range(4):
            u = tn(w1[i], zcol)
            sig = sigmoid(u)
            act = u * sig
            h = act.astype(BF16)
            hid[i, :, cols] = h
            slope[i, :, cols] = (sig + act * (1.0 - sig)).astype(BF16)
            piece = tn(w2[i], h)
            total = piece if total is None else total + piece
        acol = (state + total).astype(BF16)
        acol = (acol.astype(F32) * sea_kept[:, cols]).astype(BF16)
        alm[:, cols] = acol
        fx[r] = tn(acol, wf[...]).astype(BF16).reshape(fx.shape[1:])
        for d, to in pairs:
            i0 = (to + 3 * r + c) % 4
            k0 = (row_groups * r + few * c + i0) // 4
            twice = ((i0 + 1) // 4) * ((6 - c) // 4)
            k2 = k0 + 2 + twice * (blocks + 1 + 4 * c + r - k0 - 2)
            fcopies.append(
                send(
                    fx.at[r, 0:2, i0], fm.at[pl.ds(k0, 2)], fxs.at[r, d, 0], fxr.at[r, d, 0], b, to
                )
            )
            fcopies.append(
                send(
                    fx.at[r, 2:3, i0], fm.at[pl.ds(k2, 1)], fxs.at[r, d, 1], fxr.at[r, d, 1], b, to
                )
            )
        i0 = (2 * c + 3 * r) % 4
        k0 = (row_groups * r + few * c + i0) // 4
        twice = ((i0 + 1) // 4) * ((6 - c) // 4)
        k2 = k0 + 2 + twice * (blocks + 1 + 4 * c + r - k0 - 2)
        fm[pl.ds(k0, 2)] = fx[r, 0:2, i0]
        fm[k2] = fx[r, 2, i0]
    fm[blocks] = jnp.zeros(fm.shape[1:], BF16)
    span = 2 * ZLEN
    size = span * quarter
    r = lax.broadcasted_iota(jnp.int32, (size, size), 0)
    k = lax.broadcasted_iota(jnp.int32, (size, size), 1)
    perm[...] = jnp.where((r % span) * quarter + r // span == k, 1.0, 0.0).astype(BF16)
    go1[...] = jnp.zeros(go1.shape, F32)
    go2[...] = jnp.zeros(go2.shape, F32)
    for load in loads:
        load.wait()
    for i in range(3, 5):
        first[i].wait()
        second[i].wait_send()
        third[i].wait()
    for copy in fcopies:
        copy.wait()

    def pack(s, _):
        sp[s] = fm[table[0, s]]
        return 0

    lax.fori_loop(0, 2 * bands, pack, 0)

    def couple(d, start):
        base = ((q + d) % groups) * ZLEN
        for i in range(start, ZLEN):
            to = base + turn[i]
            send(sp.at[pl.ds(2 * to, 2)], rf.at[pl.ds(2 * b, 2)], ss, sr.at[d], to, c)

    couple(0, 1)

    def couple_all(d, _):
        couple(d, 0)
        return 0

    lax.fori_loop(1, groups, couple_all, 0)
    rf[pl.ds(2 * b, 2)] = sp[pl.ds(2 * b, 2)]
    for r in range(lats):
        for j in range(4):
            cl[j, :, r * width : (r + 1) * width] = taken(
                ctv0, r * LON + j * stride, width
            ).astype(BF16)
    ctcopies = []
    for d, to in pairs:
        ctcopies.append(send(cl.at[to], ctb.at[mine, :], cs.at[d], cr.at[d], b, to))
    ctb[mine, :] = cl[c]
    drain(rf.at[pl.ds(0, span - 2)], sr.at[0])

    def step(d, _):
        @pl.when(d > 0)
        def _():
            drain(rf.at[pl.ds(0, span)], sr.at[d])

        src = (q + groups - d) % groups
        at = pl.ds(pl.multiple_of(src * span, span), span)
        force = nn(perm[...], rf[at].reshape(size, PTS)).astype(BF16)
        both = jnp.concatenate([st[:, at, :].reshape(size, PTS), force], axis=1)
        cot = ctv[:, at, :].reshape(size, PTS)
        pre = nn(both, wa[...])
        sig = sigmoid(pre)
        act = pre * sig
        grad = (nt(cot, wb[...]) * (sig + act * (1.0 - sig))).astype(BF16)
        back = nt(grad, wa[...])
        bk[at] = tn(perm[...], back[:, PTS:].astype(BF16)).astype(BF16).reshape(span, quarter, PTS)

        def give(i):
            to = src * ZLEN + turn[i]
            send(bk.at[pl.ds(2 * to, 2)], rb.at[pl.ds(2 * b, 2)], rs, rr, to, c)

        @pl.when(d > 0)
        def _():
            give(0)

        for i in range(1, ZLEN):
            give(i)
        ds[:, at, :] = (
            (cot.astype(F32) + back[:, :PTS]).astype(BF16).reshape(quarter, span, PTS)
        )
        go2[...] += tn(cot, act.astype(BF16))
        go1[...] += tn(both, grad)
        return 0

    lax.fori_loop(0, groups, step, 0)
    dstore = pltpu.make_async_copy(ds, dst, lsem.at[3])
    dstore.start()
    rb[pl.ds(2 * b, 2)] = bk[pl.ds(2 * b, 2)]
    for i in range(4):
        gso[i, :256] = go1[:, i * 128 : i * 128 + 128].astype(BF16)
        gso[i, 256:] = go2[:, i * 128 : i * 128 + 128].astype(BF16)
    ocopies = [
        send(gso.at[diag], rao.at[1], os_.at[1], or_.at[1], b, mate),
        send(gso.at[mate], rao.at[0], os_.at[0], or_.at[0], b, mate),
    ]
    for copy in ctcopies:
        copy.wait()
    drain(rb.at[pl.ds(0, 2 * bands - 2)], rr)

    def unpack(k, _):
        dfp[k] = rb[table[1, k]]
        return 0

    lax.fori_loop(0, blocks, unpack, 0)
    dcopies = []
    for r in (0, 3, 1, 2):
        for d, to in pairs:
            i0 = (c + 3 * r + to) % 4
            k0 = (row_groups * r + few * to + i0) // 4
            dcopies.append(
                send(dfp.at[pl.ds(k0, 3)], dfb.at[r, :, i0], dfs.at[r, d], dfr.at[r, d], b, to)
            )
        i0 = (2 * c + 3 * r) % 4
        k0 = (row_groups * r + few * c + i0) // 4
        dfb[r, :, i0] = dfp[pl.ds(k0, 3)]
    for copy in ocopies:
        copy.wait()
    side = q % 2
    little, big = rxo.shape[1], rw.shape[1]
    kept_little = pl.ds(pl.multiple_of(little * side, little), little)
    sent_little = pl.ds(pl.multiple_of(little * (1 - side), little), little)
    kept_big = pl.ds(pl.multiple_of(big * side, big), big)
    sent_big = pl.ds(pl.multiple_of(big * (1 - side), big), big)
    hxo[...] = (gso[across].astype(F32) + rao[1].astype(F32)).astype(BF16)
    owno[...] = gso[c].astype(F32) + rao[0].astype(F32)
    ownob[...] = owno[sent_little].astype(BF16)
    for n, r in enumerate((0, 3, 1, 2)):
        for copy in dcopies[3 * n : 3 * n + 3]:
            copy.wait()
        cols = slice(r * width, (r + 1) * width)
        flux = dfb[r].reshape(width, PTS)
        gb[:, cols] = (
            ctb[:, cols].astype(F32) * kept[:, cols] + nt(wf[...], flux) * sea_kept[:, cols]
        ).astype(BF16)
    ocopies = [
        send(ownob, rxo.at[2], os_.at[4], or_.at[4], flip, c),
        send(hxo.at[kept_little], rxo.at[0], os_.at[2], or_.at[2], b, across),
        send(hxo.at[sent_little], rxo.at[1], os_.at[3], or_.at[3], flip, across),
    ]
    gwf[...] = nn(alm[...], dfb[...].reshape(share, PTS))
    wcopies = []
    halo = []
    for turn, i in enumerate((mate, c, diag, across)):
        for r in (0, 3, 1, 2):
            cols = slice(r * width, (r + 1) * width)
            du = (nn(w2[i], gb[:, cols]) * slope[i, :, cols].astype(F32)).astype(BF16)
            dubuf[:, cols] = du
            piece = nn(w1[i], du)
            if turn == 0:
                dzacc[:, cols] = piece
            elif turn < 3:
                dzacc[:, cols] += piece
            else:
                at = (r + 1) * width
                dext[:, at : at + width] = (dzacc[:, cols] + piece).astype(BF16)
                if r == 0:
                    halo.append(
                        send(
                            dext.at[:, at : at + width], dext.at[:, (lats + 1) * width :],
                            h2s.at[1], h2r.at[1], up, c,
                        )
                    )
                if r == 3:
                    halo.append(
                        send(
                            dext.at[:, at : at + width], dext.at[:, :width],
                            h2s.at[0], h2r.at[0], down, c,
                        )
                    )
        g1 = nt(zb[...], dubuf[...])
        g2 = nt(hid[i], gb[...])
        for j in range(2):
            gs[i, j * 256 : j * 256 + 256] = g1[:, j * 128 : j * 128 + 128].astype(BF16)
            gs[i, 512 + j * 256 : 768 + j * 256] = g2[:, j * 128 : j * 128 + 128].astype(BF16)
        gs[i, 1024:1088] = gwf[pl.ds(pl.multiple_of(rows * i, rows), rows), :].astype(BF16)
        if turn == 0:
            mcopies = [send(gs.at[mate], ra.at[0], s0.at[0], q0.at[0], b, mate)]
        if turn == 1:
            mcopies[0].wait()
            own[...] = gs[c].astype(F32) + ra[0].astype(F32)
            ownb[...] = own[sent_big].astype(BF16)
            wcopies.append(send(ownb, rw.at[2], s0.at[4], q0.at[4], flip, c))
        if turn == 2:
            mcopies.append(send(gs.at[diag], ra.at[1], s0.at[1], q0.at[1], b, mate))
        if turn == 3:
            mcopies[1].wait()
            hx[...] = (gs[across].astype(F32) + ra[1].astype(F32)).astype(BF16)
            wcopies.append(send(hx.at[kept_big], rw.at[0], s0.at[2], q0.at[2], b, across))
            wcopies.append(send(hx.at[sent_big], rw.at[1], s0.at[3], q0.at[3], flip, across))
    gkp[...] = jnp.zeros(gkp.shape, F32)
    for i in range(3):
        acc = jnp.zeros((full, 128), F32)
        for r in range(lats):
            prod = ext[:, (r + i) * width : (r + i + 1) * width].astype(F32) * dext[
                :, (r + 1) * width : (r + 2) * width
            ].astype(F32)
            for o in range(0, width, 128):
                acc = acc + prod[:, o : o + 128]
        acc = jnp.sum(acc, axis=1, keepdims=True)
        for j in range(4):
            gkp[j, i : i + 1, :rows] = jnp.sum(
                jnp.where(eye, acc[j * rows : (j + 1) * rows], 0.0), axis=0, keepdims=True
            )
    kcopies = []
    for d, to in pairs:
        kcopies.append(send(gkp.at[to], gkr.at[d], gks.at[d], gkq.at[d], b, to))
    dcopies = []

    def spread(r):
        cols = slice(r * width, (r + 1) * width)
        dl[:, cols] = (
            gb[:, cols].astype(F32)
            + t0 * dext[:, (r + 2) * width : (r + 3) * width].astype(F32)
            + t1 * dext[:, (r + 1) * width : (r + 2) * width].astype(F32)
            + t2 * dext[:, r * width : (r + 1) * width].astype(F32)
        ).astype(BF16)

    def send_back(k):
        lo, hi = cuts[k].start, cuts[k].stop
        for d, to in pairs:
            theirs = pl.ds(pl.multiple_of(rows * to, rows), rows)
            dcopies.append(
                send(dl.at[theirs, lo:hi], dq.at[c, :, lo:hi], das.at[k, d], dar.at[k, d], b, to)
            )

    spread(1)
    spread(2)
    for copy in ocopies:
        copy.wait()
    t[big + 32 :] = (
        owno[kept_little]
        + rxo[0].astype(F32)
        + rxo[1].astype(F32)
        + rxo[2].astype(F32)
    ).astype(BF16)
    for copy in kcopies:
        copy.wait()
    t[big : big + 16] = (gkp[c] + gkr[1] + gkr[2] + gkr[3]).astype(BF16)
    t[big + 16 : big + 32] = jnp.zeros((16, 128), BF16)
    for copy in wcopies:
        copy.wait()
    t[:big] = (
        own[kept_big] + rw[0].astype(F32) + rw[1].astype(F32) + rw[2].astype(F32)
    ).astype(BF16)
    size = r1.shape[1]
    x, xs = q // 2, groups // 2
    copies = []
    for d in range(1, xs):
        to = (x + d) % xs
        cut = pl.ds(pl.multiple_of(to * size, size), size)
        copies.append(
            send(t.at[cut], r1.at[x], s1.at[d], q1.at[d], (2 * to + side) * ZLEN + z, c)
        )
    send_back(2)
    r1[x] = t[pl.ds(pl.multiple_of(x * size, size), size)]
    for copy in halo:
        copy.wait()

    @pl.when(b == 0)
    def _():
        dext[:, :width] = jnp.zeros((full, width), BF16)

    @pl.when(b == bands - 1)
    def _():
        dext[:, (lats + 1) * width :] = jnp.zeros((full, width), BF16)

    spread(0)
    send_back(0)
    spread(3)
    send_back(1)
    dq[c] = dl[mine, :]
    for copy in copies:
        copy.wait()
    total = r1[0].astype(F32)
    for i in range(1, xs):
        total = total + r1[i].astype(F32)
    fs[...] = total.reshape(fs.shape)
    copies = []
    for d in range(1, ZLEN):
        to = (z + d) % ZLEN
        copies.append(send(fs.at[to], r2.at[z], s2.at[d], q2.at[d], q * ZLEN + to, c))
    r2[z] = fs[z]
    for copy in copies:
        copy.wait()
    total = r2[0]
    for i in range(1, ZLEN):
        total = total + r2[i]
    fr[...] = total
    copies = []
    for d in range(1, ZLEN):
        to = (z + d) % ZLEN
        copies.append(send(fr, ag.at[z], s3.at[d], q3.at[d], q * ZLEN + to, c))
    ag[z] = total
    for copy in copies:
        copy.wait()
    tb[...] = ag[...].reshape(size, 128).astype(BF16)
    copies = []
    cut = pl.ds(pl.multiple_of((side * xs + x) * size, size), size)
    for d in range(1, groups):
        to = (q + d) % groups
        copies.append(send(tb, out.at[cut], s4.at[d], q4.at[d], to * ZLEN + z, c))
    out[cut] = tb[...]
    for copy in dcopies:
        copy.wait()
    for r in range(lats):
        for j in range(4):
            start = r * LON + j * stride
            extra = start % 128
            piece = dq[j, :, r * width : (r + 1) * width]
            if extra == 0:
                dat[:, start : start + width] = piece
                continue
            base = start - extra
            moved = jnp.concatenate([piece.astype(F32), jnp.zeros((rows, 128), F32)], axis=1)
            moved = pltpu.roll(moved, extra, axis=1)
            lead = lax.broadcasted_iota(jnp.int32, (rows, 128), 1)
            dat[:, base : base + 128] = jnp.where(
                lead < extra, dat[:, base : base + 128].astype(F32), moved[:, :128]
            ).astype(BF16)
            dat[:, base + 128 : base + 128 + width] = moved[:, 128:].astype(BF16)
    astore = pltpu.make_async_copy(dat, dat_all, lsem.at[4])
    astore.start()
    for copy in copies:
        copy.wait()
    drain(sp.at[pl.ds(0, 2 * bands - 2)], ss)
    drain(bk.at[pl.ds(0, 2 * bands - 2)], rs)
    dstore.wait()
    astore.wait()


def local(
    atmos, kernels, w_one, w_two, w_flux, sea_mask, route,
    ocean_state, ct_atmos, ct_ocean, wo_one, wo_two,
):
    chans = lax.axis_size("chan")
    bands = lax.axis_size("band")
    rows, points = atmos.shape
    blocks = points // PTS
    quarter = PTS // chans
    lats = points // LON
    share = lats * (LON // quarter // chans + 1) * quarter
    width = share // lats
    slots = ocean_state.shape[2]
    hid = w_one.shape[2]
    full = rows * chans
    wide = wo_one.shape[1]
    total = wide * chans
    groups = bands // ZLEN
    flat = 1536
    big, little = 1088, 384
    size = flat // groups
    small = size // ZLEN
    vm = pl.BlockSpec(memory_space=VMEM)
    anywhere = pl.BlockSpec(memory_space=pl.ANY)

    ocean = VMEM((slots, quarter, PTS), BF16)
    points_first = VMEM((quarter, slots, PTS), BF16)
    split = VMEM((chans, rows, share), BF16)
    extended = VMEM((full, share + 2 * width), BF16)
    square = VMEM((full, share), BF16)
    grouped = VMEM((lats, width // PTS, chans, quarter, PTS), BF16)
    dat, dst, out = pl.pallas_call(
        main_kernel,
        out_shape=[
            jax.ShapeDtypeStruct((rows, points), BF16),
            jax.ShapeDtypeStruct((quarter, slots, PTS), BF16),
            jax.ShapeDtypeStruct((flat, 128), BF16),
        ],
        in_specs=[vm, vm, vm] + [anywhere] * 9,
        out_specs=[anywhere, anywhere, vm],
        scratch_shapes=[
            VMEM((8, 128), jnp.int32),
            pltpu.SMEM((8, 128), jnp.int32),
            VMEM((rows, points), BF16),
            VMEM((rows, points), BF16),
            split, split, extended, square, square,
            VMEM((8, 128), F32),
            VMEM((chans, 8, 128), F32),
            VMEM((full, 128), F32),
            VMEM((chans, full, hid), BF16),
            VMEM((chans, hid, full), BF16),
            VMEM((full, PTS), BF16),
            grouped,
            VMEM((blocks + 1 + 4 * lats, quarter, PTS), BF16),
            VMEM((1, points), F32),
            VMEM((chans, 1, share), F32),
            VMEM((chans, hid, share), BF16),
            VMEM((chans, hid, share), BF16),
            VMEM((rows, points), BF16),
            square, ocean, ocean, ocean, ocean, points_first, points_first, points_first,
            VMEM((2 * PTS, total), BF16),
            VMEM((total, PTS), BF16),
            VMEM((2 * ZLEN * quarter, 2 * ZLEN * quarter), BF16),
            VMEM((2 * PTS, total), F32),
            VMEM((PTS, total), F32),
            VMEM((blocks, quarter, PTS), BF16),
            grouped, square, extended, square, split,
            VMEM((full, share), F32),
            VMEM((hid, share), BF16),
            VMEM((full, PTS), F32),
            VMEM((chans, 16, 128), F32),
            VMEM((chans, 16, 128), F32),
            VMEM((chans, big, 128), BF16),
            VMEM((2, big, 128), BF16),
            VMEM((big, 128), BF16),
            VMEM((3, big // 2, 128), BF16),
            VMEM((chans, little, 128), BF16),
            VMEM((2, little, 128), BF16),
            VMEM((little, 128), BF16),
            VMEM((3, little // 2, 128), BF16),
            VMEM((big, 128), F32),
            VMEM((little, 128), F32),
            VMEM((big // 2, 128), BF16),
            VMEM((little // 2, 128), BF16),
            VMEM((flat // 2, 128), BF16),
            VMEM((groups // 2, size, 128), BF16),
            VMEM((ZLEN, small, 128), F32),
            VMEM((ZLEN, small, 128), F32),
            VMEM((small, 128), F32),
            VMEM((ZLEN, small, 128), F32),
            VMEM((size, 128), BF16),
            DMA((5,)), DMA((7,)), DMA((2,)), DMA((2,)), DMA((3, 5)), DMA((3, 5)), DMA((4,)), DMA((4,)),
            DMA((3, 4)), DMA((3, 4)), DMA((lats, 4, 2)), DMA((lats, 4, 2)), DMA((4,)), DMA((4,)),
            DMA, DMA((groups,)), DMA, DMA,
            DMA((5,)), DMA((5,)), DMA((lats, 4)), DMA((lats, 4)), DMA((2,)), DMA((2,)),
            DMA((4,)), DMA((4,)), DMA((3, 4)), DMA((3, 4)), DMA((5,)), DMA((5,)),
            DMA((groups,)), DMA((groups,)), DMA((ZLEN,)), DMA((ZLEN,)),
            DMA((ZLEN,)), DMA((ZLEN,)), DMA((groups,)), DMA((groups,)),
        ],
        compiler_params=pltpu.CompilerParams(
            collective_id=0, has_side_effects=True, vmem_limit_bytes=LIMIT
        ),
    )(
        route.T, kernels.transpose(1, 0, 2), sea_mask.reshape(blocks, PTS), atmos, w_one[0], w_two[0],
        w_flux, wo_one, wo_two, ct_atmos, ocean_state, ct_ocean,
    )
    datmos, dk, dw1, dw2, dwf, dstate, do1, do2 = pl.pallas_call(
        finish_kernel,
        out_shape=[
            jax.ShapeDtypeStruct(dat.shape, BF16),
            jax.ShapeDtypeStruct((3, 1, rows), F32),
            jax.ShapeDtypeStruct((full, hid), F32),
            jax.ShapeDtypeStruct((hid, full), F32),
            jax.ShapeDtypeStruct((rows, PTS), F32),
            jax.ShapeDtypeStruct(dst.shape, BF16),
            jax.ShapeDtypeStruct((2 * PTS, wide), F32),
            jax.ShapeDtypeStruct((wide, PTS), F32),
        ],
        in_specs=[vm] * 3,
        out_specs=[vm] * 8,
        compiler_params=pltpu.CompilerParams(vmem_limit_bytes=LIMIT + (4 << 20)),
    )(dat, dst, out)
    return datmos, dk.transpose(1, 0, 2), dw1[None], dw2[None], dwf, dstate[:, None], do1, do2


def solution(mesh):
    in_specs = (
        P("chan", "band"),
        P(None, None, "chan"),
        P(None, None, "chan"),
        P(None, "chan", None),
        P("chan", None),
        P("band"),
        P("band", None),
        P(None, "band", None, None),
        P("chan", "band"),
        P(None, "band", None, None),
        P(None, "chan"),
        P("chan", None),
    )
    out_specs = (
        P("chan", "band"),
        P(None, None, "chan"),
        P(None, None, "chan"),
        P(None, "chan", None),
        P("chan", None),
        P("chan", "band", None, None),
        P(None, "chan"),
        P("chan", None),
    )
    return jax.shard_map(local, mesh=mesh, in_specs=in_specs, out_specs=out_specs, check_vma=False)
```

```python
import functools

import jax
import jax.numpy as jnp
from jax import lax
from jax.experimental import pallas as pl
from jax.experimental.pallas import tpu as pltpu
from jax.sharding import PartitionSpec as P

PTS = 128
LON = 1440
MESH = pl.DeviceIdType.MESH
F32 = jnp.float32
BF16 = jnp.bfloat16
VMEM = pltpu.VMEM
DMA = pltpu.SemaphoreType.DMA
ZLEN = 8
LIMIT = 56 * 1024 * 1024


def nn(a, b):
    return lax.dot_general(a, b, (((1,), (0,)), ((), ())), preferred_element_type=F32)


def tn(a, b):
    return lax.dot_general(a, b, (((0,), (0,)), ((), ())), preferred_element_type=F32)


def nt(a, b):
    return lax.dot_general(a, b, (((1,), (1,)), ((), ())), preferred_element_type=F32)


def sigmoid(v):
    return 0.5 * jnp.tanh(0.5 * v) + 0.5


def place():
    b, c = lax.axis_index("band"), lax.axis_index("chan")
    mate = (c // 2) * 2 + (1 - c % 2)
    return b, c, mate, (c + 2) % 4, (mate + 2) % 4


def send(src, dst, ssem, rsem, b, c):
    copy = pltpu.make_async_remote_copy(
        src_ref=src,
        dst_ref=dst,
        send_sem=ssem,
        recv_sem=rsem,
        device_id=(b, c),
        device_id_type=MESH,
    )
    copy.start()
    return copy


def drain(ref, sem):
    pltpu.make_async_copy(ref, ref, sem).wait()


def signal(b, c):
    pl.semaphore_signal(
        pltpu.get_barrier_semaphore(), inc=1, device_id=(b, c), device_id_type=MESH
    )


def taken(ref, start, width):
    extra = start % 128
    if extra == 0:
        return ref[:, start : start + width].astype(F32)
    wide = ref[:, start - extra : start - extra + width + 128].astype(F32)
    return pltpu.roll(wide, width + 128 - extra, axis=1)[:, :width]


def tables(row):
    blocks = row.shape[1]
    k = lax.broadcasted_iota(jnp.int32, (blocks, blocks), 0)
    j = lax.broadcasted_iota(jnp.int32, (blocks, blocks), 1)
    col = jnp.sum(jnp.where(k == j, row, 0), axis=1, keepdims=True)
    rank = jnp.sum(jnp.where((row == col) & (j < k), 1, 0), axis=1, keepdims=True)
    slot = col * 2 + rank
    k = lax.broadcasted_iota(jnp.int32, (blocks, 128), 0)
    s = lax.broadcasted_iota(jnp.int32, (blocks, 128), 1)
    inv = blocks + jnp.sum(jnp.where(slot == s, k - blocks, 0), axis=0, keepdims=True)
    back = jnp.sum(jnp.where(k == s, slot, 0), axis=0, keepdims=True)
    line = lax.broadcasted_iota(jnp.int32, (8, 128), 0)
    return jnp.where(line == 0, inv, back)


def finish_kernel(dat, dst, out, datmos, dk, dw1, dw2, dwf, dstate, do1, do2):
    half = out.shape[0] // 2
    datmos[...] = dat[...]
    dstate[...] = dst[...]
    dw1[:, :128] = out[:256].astype(F32)
    dw1[:, 128:] = out[256:512].astype(F32)
    dw2[:32, :128] = out[512:544].astype(F32)
    dw2[32:, :128] = out[half : half + 224].astype(F32)
    dw2[:, 128:] = out[half + 224 : half + 480].astype(F32)
    dwf[...] = out[half + 480 : half + 544].astype(F32)
    tile = out[544:560].astype(F32) + out[half + 544 : half + 560].astype(F32)
    for i in range(3):
        dk[i] = tile[i : i + 1, :64]
    do1[:192] = out[576:768].astype(F32)
    do1[192:] = out[half + 576 : half + 640].astype(F32)
    do2[...] = out[half + 640 :].astype(F32).T


def main_kernel(
    route, taps, sea, atmos_all, w_one, w_two, w_flux, wo_one, wo_two, ct_all, state_all, cot_all,
    dat_all, dst, out,
    tabv, table, atmos, dat, al, cl, ext, zb, alm, tapt, tapr, tapf, w1, w2, wf, fx, fm, mk, mk4, hid, slope,
    ctv0, ctb, sp, rf, bk, rb, st, ctv, ds, wa, wb, perm, go1, go2,
    dfp, dfb, gb, dext, dl, dq, dzacc, dubuf, gwf, gkp, gkr,
    gs, ra, hx, rw, gso, rao, hxo, rxo, own, owno, ownb, ownob, t, r1, fs, r2, fr, ag, tb,
    lsem, msem, hs, hr, ws, wr, ts, tr, as_, ar, fxs, fxr, cs, cr, ss, sr, rs, rr,
    os_, or_, dfs, dfr, h2s, h2r, gks, gkq, das, dar, s0, q0, s1, q1, s2, q2, s3, q3, s4, q4,
):
    b, c, mate, across, diag = place()
    bands = lax.axis_size("band")
    up, down = (b + bands - 1) % bands, (b + 1) % bands
    q, z = b // ZLEN, b % ZLEN
    groups = bands // ZLEN
    flip = ((q // 2) * 2 + (1 - q % 2)) * ZLEN + z
    rows, points = atmos.shape
    full, share = zb.shape
    lats = points // LON
    width = share // lats
    quarter = st.shape[0]
    blocks = dfp.shape[0]
    row_groups = LON // quarter
    few = row_groups // 4
    stride = few * quarter
    wide = wo_one.shape[1]
    peers = [(c + 2) % 4, (c + 1) % 4, (c + 3) % 4]
    order = (2, 1, 3)
    pairs = list(zip(order, peers))

    z_far = (4, 3, 5, 2, 6, 1, 7)
    turn = [(z + i) % ZLEN for i in z_far + (0,)]
    x, xs, side = q // 2, groups // 2, q % 2

    def column(n, way):
        m = n % 4
        dx = (2 + m + m // 2 + 2 * (m // 3)) % 4
        dy = 1 - n // 4
        return ((x + way * dx + xs) % xs) * 2 + (side + dy) % 2

    def greet(n, _):
        base = column(n, 1) * ZLEN
        for to in turn:
            signal(base + to, c)
        return 0

    lax.fori_loop(0, groups - 1, greet, 0)
    for to in turn[:-1]:
        signal(q * ZLEN + to, c)
    signal(flip, across)
    for d in (2, 1, 3):
        signal(b, (c + d) % 4)
    loads = [
        pltpu.make_async_copy(ct_all, ctv0, lsem.at[0]),
        pltpu.make_async_copy(
            state_all.at[pl.ds(pl.multiple_of(quarter * c, quarter), quarter), 0], st, lsem.at[1]
        ),
        pltpu.make_async_copy(
            cot_all.at[pl.ds(pl.multiple_of(quarter * c, quarter), quarter), 0], ctv, lsem.at[2]
        ),
    ]
    mine = pl.ds(pl.multiple_of(c * rows, rows), rows)
    mine_wide = pl.ds(pl.multiple_of(c * wide, wide), wide)
    sources = (w_one, w_two, w_flux, wo_one, wo_two)
    near = (w1.at[c], w2.at[c], wf.at[mine, :], wa.at[:, mine_wide], wb.at[mine_wide, :])
    early = [pltpu.make_async_copy(atmos_all, atmos, msem.at[5])]
    for i in range(5):
        early.append(pltpu.make_async_copy(sources[i], near[i], msem.at[i]))
    for load in early + loads:
        load.start()
    tabv[...] = tables(route[...])
    tcopy = pltpu.make_async_copy(tabv, table, msem.at[6])
    tcopy.start()
    early[0].wait()
    eye = lax.broadcasted_iota(jnp.int32, (rows, rows), 0) == lax.broadcasted_iota(
        jnp.int32, (rows, rows), 1
    )
    for r in (0, lats - 1) + tuple(range(1, lats - 1)):
        for j in range(4):
            al[j, :, r * width : (r + 1) * width] = taken(
                atmos, r * LON + j * stride, width
            ).astype(BF16)
    tapt[...] = jnp.zeros(tapt.shape, F32)
    for i in range(3):
        tapt[i : i + 1, :rows] = taps[i]
    tcopy.wait()
    pl.semaphore_wait(pltpu.get_barrier_semaphore(), bands - 1 + 4)

    cuts = (
        slice(0, width), slice((lats - 1) * width, lats * width), slice(width, (lats - 1) * width)
    )
    acopies = [[], [], []]

    def send_state(k):
        lo, hi = cuts[k].start, cuts[k].stop
        for d, to in pairs:
            acopies[k].append(
                send(
                    al.at[to, :, lo:hi], ext.at[mine, width + lo : width + hi],
                    as_.at[k, d], ar.at[k, d], b, to,
                )
            )

    send_state(0)
    send_state(1)
    theirs = pl.ds(pl.multiple_of(across * rows, rows), rows)
    theirs_wide = pl.ds(pl.multiple_of(across * wide, wide), wide)
    far = (
        w1.at[across], w2.at[across], wf.at[theirs, :],
        wa.at[:, theirs_wide], wb.at[theirs_wide, :],
    )
    first, second, third, tcopies = [], [], [], []
    for i in range(5):
        early[i + 1].wait()
        second.append(send(near[i], near[i], ws.at[1, i], wr.at[1, i], flip, across))
        first.append(send(near[i], near[i], ws.at[0, i], wr.at[0, i], b, mate))
    for d, to in pairs:
        tcopies.append(send(tapt, tapr.at[c], ts.at[d], tr.at[d], b, to))
    send_state(2)
    ext[mine, width : width + share] = al[c]
    tapr[c] = tapt[...]
    halo = []

    def send_halo(k, d):
        at = pl.ds(pl.multiple_of(rows * ((c + 4 - d) % 4), rows), rows)
        if k == 0:
            src, dst, to = (1, 2), (lats + 1, lats + 2), up
        else:
            src, dst, to = (lats, lats + 1), (0, 1), down
        halo.append(
            send(
                ext.at[at, src[0] * width : src[1] * width],
                ext.at[at, dst[0] * width : dst[1] * width],
                hs.at[k, d], hr.at[k, d], to, c,
            )
        )

    send_halo(0, 0)
    send_halo(1, 0)
    for k in (0, 1):
        for n, d in ((1, 1), (2, 3), (0, 2)):
            acopies[k][n].wait()
            send_halo(k, d)
    for i in range(points // PTS):
        mk[:, i * PTS : (i + 1) * PTS] = sea[i : i + 1, :].astype(F32)
    for r in range(lats):
        for j in range(4):
            mk4[j, :, r * width : (r + 1) * width] = taken(mk, r * LON + j * stride, width)
    for copy in tcopies:
        copy.wait()
    for j in range(4):
        for i in range(3):
            tapf[j * rows : (j + 1) * rows, i : i + 1] = jnp.sum(
                jnp.where(eye, tapr[j, i : i + 1, :rows], 0.0), axis=1, keepdims=True
            )
    t0, t1, t2 = tapf[:, 0:1], tapf[:, 1:2], tapf[:, 2:3]
    lane = lax.broadcasted_iota(jnp.int32, (1, share), 1) % width
    kept = jnp.where((lane < stride) | (c == 3), 1.0, 0.0)
    sea_kept = mk4[c] * kept
    for i in range(5):
        second[i].wait_recv()
        third.append(send(far[i], far[i], ws.at[2, i], wr.at[2, i], b, mate))
    for copy in acopies[2]:
        copy.wait()
    for i in range(3):
        first[i].wait()
        second[i].wait_send()
        third[i].wait()
    fcopies = []
    line = (1, 2, 0, 3)
    for r in line:
        if r == 0:
            for copy in halo:
                copy.wait()

            @pl.when(b == 0)
            def _():
                ext[:, :width] = jnp.zeros((full, width), BF16)

            @pl.when(b == bands - 1)
            def _():
                ext[:, (lats + 1) * width :] = jnp.zeros((full, width), BF16)

        cols = slice(r * width, (r + 1) * width)
        state = ext[:, (r + 1) * width : (r + 2) * width].astype(F32)
        zcol = (
            t0 * ext[:, r * width : (r + 1) * width].astype(F32)
            + t1 * state
            + t2 * ext[:, (r + 2) * width : (r + 3) * width].astype(F32)
        ).astype(BF16)
        zb[:, cols] = zcol
        total = None
        for i in range(4):
            u = tn(w1[i], zcol)
            sig = sigmoid(u)
            act = u * sig
            h = act.astype(BF16)
            hid[i, :, cols] = h
            slope[i, :, cols] = (sig + act * (1.0 - sig)).astype(BF16)
            piece = tn(w2[i], h)
            total = piece if total is None else total + piece
        acol = (state + total).astype(BF16)
        acol = (acol.astype(F32) * sea_kept[:, cols]).astype(BF16)
        alm[:, cols] = acol
        fx[r] = tn(acol, wf[...]).astype(BF16).reshape(fx.shape[1:])
        for d, to in pairs:
            i0 = (to + 3 * r + c) % 4
            k0 = (row_groups * r + few * c + i0) // 4
            twice = ((i0 + 1) // 4) * ((6 - c) // 4)
            k2 = k0 + 2 + twice * (blocks + 1 + 4 * c + r - k0 - 2)
            fcopies.append(
                send(
                    fx.at[r, 0:2, i0], fm.at[pl.ds(k0, 2)], fxs.at[r, d, 0], fxr.at[r, d, 0], b, to
                )
            )
            fcopies.append(
                send(
                    fx.at[r, 2:3, i0], fm.at[pl.ds(k2, 1)], fxs.at[r, d, 1], fxr.at[r, d, 1], b, to
                )
            )
        i0 = (2 * c + 3 * r) % 4
        k0 = (row_groups * r + few * c + i0) // 4
        twice = ((i0 + 1) // 4) * ((6 - c) // 4)
        k2 = k0 + 2 + twice * (blocks + 1 + 4 * c + r - k0 - 2)
        fm[pl.ds(k0, 2)] = fx[r, 0:2, i0]
        fm[k2] = fx[r, 2, i0]
    fm[blocks] = jnp.zeros(fm.shape[1:], BF16)
    span = 2 * ZLEN
    size = span * quarter
    r = lax.broadcasted_iota(jnp.int32, (size, size), 0)
    k = lax.broadcasted_iota(jnp.int32, (size, size), 1)
    perm[...] = jnp.where((r % span) * quarter + r // span == k, 1.0, 0.0).astype(BF16)
    go1[...] = jnp.zeros(go1.shape, F32)
    go2[...] = jnp.zeros(go2.shape, F32)
    for load in loads:
        load.wait()
    for i in range(3, 5):
        first[i].wait()
        second[i].wait_send()
        third[i].wait()
    for copy in fcopies:
        copy.wait()

    def pack(s, _):
        sp[s] = fm[table[0, s]]
        return 0

    lax.fori_loop(0, 2 * bands, pack, 0)

    def couple(n, ways):
        base = column(n, 1) * ZLEN
        for way in ways:
            to = base + way
            send(sp.at[pl.ds(2 * to, 2)], rf.at[pl.ds(2 * b, 2)], ss, sr.at[n], to, c)

    def couple_all(n, _):
        couple(n, turn)
        return 0

    lax.fori_loop(0, groups - 1, couple_all, 0)
    couple(groups - 1, turn[:-1])
    rf[pl.ds(2 * b, 2)] = sp[pl.ds(2 * b, 2)]
    for r in range(lats):
        for j in range(4):
            cl[j, :, r * width : (r + 1) * width] = taken(
                ctv0, r * LON + j * stride, width
            ).astype(BF16)
    ctcopies = []
    for d, to in pairs:
        ctcopies.append(send(cl.at[to], ctb.at[mine, :], cs.at[d], cr.at[d], b, to))
    ctb[mine, :] = cl[c]

    def step(n, _):
        @pl.when(n < groups - 1)
        def _():
            drain(rf.at[pl.ds(0, span)], sr.at[n])

        @pl.when(n == groups - 1)
        def _():
            drain(rf.at[pl.ds(0, span - 2)], sr.at[n])

        src = column(n, -1)
        at = pl.ds(pl.multiple_of(src * span, span), span)
        force = nn(perm[...], rf[at].reshape(size, PTS)).astype(BF16)
        both = jnp.concatenate([st[:, at, :].reshape(size, PTS), force], axis=1)
        cot = ctv[:, at, :].reshape(size, PTS)
        pre = nn(both, wa[...])
        sig = sigmoid(pre)
        act = pre * sig
        grad = (nt(cot, wb[...]) * (sig + act * (1.0 - sig))).astype(BF16)
        back = nt(grad, wa[...])
        bk[at] = tn(perm[...], back[:, PTS:].astype(BF16)).astype(BF16).reshape(span, quarter, PTS)

        def give(way):
            to = src * ZLEN + way
            send(bk.at[pl.ds(2 * to, 2)], rb.at[pl.ds(2 * b, 2)], rs, rr, to, c)

        for way in turn[:-1]:
            give(way)

        @pl.when(n < groups - 1)
        def _():
            give(turn[-1])

        ds[:, at, :] = (
            (cot.astype(F32) + back[:, :PTS]).astype(BF16).reshape(quarter, span, PTS)
        )
        go2[...] += tn(cot, act.astype(BF16))
        go1[...] += tn(both, grad)
        return 0

    lax.fori_loop(0, groups, step, 0)
    dstore = pltpu.make_async_copy(ds, dst, lsem.at[3])
    dstore.start()
    rb[pl.ds(2 * b, 2)] = bk[pl.ds(2 * b, 2)]
    for i in range(4):
        gso[i, :256] = go1[:, i * 128 : i * 128 + 128].astype(BF16)
        gso[i, 256:] = go2[:, i * 128 : i * 128 + 128].astype(BF16)
    ocopies = [
        send(gso.at[diag], rao.at[1], os_.at[1], or_.at[1], b, mate),
        send(gso.at[mate], rao.at[0], os_.at[0], or_.at[0], b, mate),
    ]
    for copy in ctcopies:
        copy.wait()
    drain(rb.at[pl.ds(0, 2 * bands - 2)], rr)

    def unpack(k, _):
        dfp[k] = rb[table[1, k]]
        return 0

    lax.fori_loop(0, blocks, unpack, 0)
    dcopies = []
    for r in (0, 3, 1, 2):
        for d, to in pairs:
            i0 = (c + 3 * r + to) % 4
            k0 = (row_groups * r + few * to + i0) // 4
            dcopies.append(
                send(dfp.at[pl.ds(k0, 3)], dfb.at[r, :, i0], dfs.at[r, d], dfr.at[r, d], b, to)
            )
        i0 = (2 * c + 3 * r) % 4
        k0 = (row_groups * r + few * c + i0) // 4
        dfb[r, :, i0] = dfp[pl.ds(k0, 3)]
    for copy in ocopies:
        copy.wait()
    little, big = rxo.shape[1], rw.shape[1]
    kept_little = pl.ds(pl.multiple_of(little * side, little), little)
    sent_little = pl.ds(pl.multiple_of(little * (1 - side), little), little)
    kept_big = pl.ds(pl.multiple_of(big * side, big), big)
    sent_big = pl.ds(pl.multiple_of(big * (1 - side), big), big)
    hxo[...] = (gso[across].astype(F32) + rao[1].astype(F32)).astype(BF16)
    owno[...] = gso[c].astype(F32) + rao[0].astype(F32)
    ownob[...] = owno[sent_little].astype(BF16)
    for n, r in enumerate((0, 3, 1, 2)):
        for copy in dcopies[3 * n : 3 * n + 3]:
            copy.wait()
        cols = slice(r * width, (r + 1) * width)
        flux = dfb[r].reshape(width, PTS)
        gb[:, cols] = (
            ctb[:, cols].astype(F32) * kept[:, cols] + nt(wf[...], flux) * sea_kept[:, cols]
        ).astype(BF16)
    ocopies = [
        send(ownob, rxo.at[2], os_.at[4], or_.at[4], flip, c),
        send(hxo.at[kept_little], rxo.at[0], os_.at[2], or_.at[2], b, across),
        send(hxo.at[sent_little], rxo.at[1], os_.at[3], or_.at[3], flip, across),
    ]
    gwf[...] = nn(alm[...], dfb[...].reshape(share, PTS))
    wcopies = []
    halo = []
    for turn, i in enumerate((mate, c, diag, across)):
        for r in (0, 3, 1, 2):
            cols = slice(r * width, (r + 1) * width)
            du = (nn(w2[i], gb[:, cols]) * slope[i, :, cols].astype(F32)).astype(BF16)
            dubuf[:, cols] = du
            piece = nn(w1[i], du)
            if turn == 0:
                dzacc[:, cols] = piece
            elif turn < 3:
                dzacc[:, cols] += piece
            else:
                at = (r + 1) * width
                dext[:, at : at + width] = (dzacc[:, cols] + piece).astype(BF16)
                if r == 0:
                    halo.append(
                        send(
                            dext.at[:, at : at + width], dext.at[:, (lats + 1) * width :],
                            h2s.at[1], h2r.at[1], up, c,
                        )
                    )
                if r == 3:
                    halo.append(
                        send(
                            dext.at[:, at : at + width], dext.at[:, :width],
                            h2s.at[0], h2r.at[0], down, c,
                        )
                    )
        g1 = nt(zb[...], dubuf[...])
        g2 = nt(hid[i], gb[...])
        for j in range(2):
            gs[i, j * 256 : j * 256 + 256] = g1[:, j * 128 : j * 128 + 128].astype(BF16)
            gs[i, 512 + j * 256 : 768 + j * 256] = g2[:, j * 128 : j * 128 + 128].astype(BF16)
        gs[i, 1024:1088] = gwf[pl.ds(pl.multiple_of(rows * i, rows), rows), :].astype(BF16)
        if turn == 0:
            mcopies = [send(gs.at[mate], ra.at[0], s0.at[0], q0.at[0], b, mate)]
        if turn == 1:
            mcopies[0].wait()
            own[...] = gs[c].astype(F32) + ra[0].astype(F32)
            ownb[...] = own[sent_big].astype(BF16)
            wcopies.append(send(ownb, rw.at[2], s0.at[4], q0.at[4], flip, c))
        if turn == 2:
            mcopies.append(send(gs.at[diag], ra.at[1], s0.at[1], q0.at[1], b, mate))
        if turn == 3:
            mcopies[1].wait()
            hx[...] = (gs[across].astype(F32) + ra[1].astype(F32)).astype(BF16)
            wcopies.append(send(hx.at[kept_big], rw.at[0], s0.at[2], q0.at[2], b, across))
            wcopies.append(send(hx.at[sent_big], rw.at[1], s0.at[3], q0.at[3], flip, across))
    gkp[...] = jnp.zeros(gkp.shape, F32)
    for i in range(3):
        acc = jnp.zeros((full, 128), F32)
        for r in range(lats):
            prod = ext[:, (r + i) * width : (r + i + 1) * width].astype(F32) * dext[
                :, (r + 1) * width : (r + 2) * width
            ].astype(F32)
            for o in range(0, width, 128):
                acc = acc + prod[:, o : o + 128]
        acc = jnp.sum(acc, axis=1, keepdims=True)
        for j in range(4):
            gkp[j, i : i + 1, :rows] = jnp.sum(
                jnp.where(eye, acc[j * rows : (j + 1) * rows], 0.0), axis=0, keepdims=True
            )
    kcopies = []
    for d, to in pairs:
        kcopies.append(send(gkp.at[to], gkr.at[d], gks.at[d], gkq.at[d], b, to))
    dcopies = []

    def spread(r):
        cols = slice(r * width, (r + 1) * width)
        dl[:, cols] = (
            gb[:, cols].astype(F32)
            + t0 * dext[:, (r + 2) * width : (r + 3) * width].astype(F32)
            + t1 * dext[:, (r + 1) * width : (r + 2) * width].astype(F32)
            + t2 * dext[:, r * width : (r + 1) * width].astype(F32)
        ).astype(BF16)

    def send_back(k):
        lo, hi = cuts[k].start, cuts[k].stop
        for d, to in pairs:
            theirs = pl.ds(pl.multiple_of(rows * to, rows), rows)
            dcopies.append(
                send(dl.at[theirs, lo:hi], dq.at[c, :, lo:hi], das.at[k, d], dar.at[k, d], b, to)
            )

    spread(1)
    spread(2)
    for copy in ocopies:
        copy.wait()
    t[big + 32 :] = (
        owno[kept_little]
        + rxo[0].astype(F32)
        + rxo[1].astype(F32)
        + rxo[2].astype(F32)
    ).astype(BF16)
    for copy in kcopies:
        copy.wait()
    t[big : big + 16] = (gkp[c] + gkr[1] + gkr[2] + gkr[3]).astype(BF16)
    t[big + 16 : big + 32] = jnp.zeros((16, 128), BF16)
    for copy in wcopies:
        copy.wait()
    t[:big] = (
        own[kept_big] + rw[0].astype(F32) + rw[1].astype(F32) + rw[2].astype(F32)
    ).astype(BF16)
    size = r1.shape[1]
    copies = []
    for d in (2, 1, 3):
        to = (x + d) % xs
        cut = pl.ds(pl.multiple_of(to * size, size), size)
        copies.append(
            send(t.at[cut], r1.at[x], s1.at[d], q1.at[d], (2 * to + side) * ZLEN + z, c)
        )
    send_back(2)
    r1[x] = t[pl.ds(pl.multiple_of(x * size, size), size)]
    for copy in halo:
        copy.wait()

    @pl.when(b == 0)
    def _():
        dext[:, :width] = jnp.zeros((full, width), BF16)

    @pl.when(b == bands - 1)
    def _():
        dext[:, (lats + 1) * width :] = jnp.zeros((full, width), BF16)

    spread(0)
    send_back(0)
    spread(3)
    send_back(1)
    dq[c] = dl[mine, :]
    for copy in copies:
        copy.wait()
    total = r1[0].astype(F32)
    for i in range(1, xs):
        total = total + r1[i].astype(F32)
    fs[...] = total.reshape(fs.shape)
    copies = []
    for d in z_far:
        to = (z + d) % ZLEN
        copies.append(send(fs.at[to], r2.at[z], s2.at[d], q2.at[d], q * ZLEN + to, c))
    r2[z] = fs[z]
    for copy in copies:
        copy.wait()
    total = r2[0]
    for i in range(1, ZLEN):
        total = total + r2[i]
    fr[...] = total
    copies = []
    for d in z_far:
        to = (z + d) % ZLEN
        copies.append(send(fr, ag.at[z], s3.at[d], q3.at[d], q * ZLEN + to, c))
    ag[z] = total
    for copy in copies:
        copy.wait()
    tb[...] = ag[...].reshape(size, 128).astype(BF16)
    copies = []
    cut = pl.ds(pl.multiple_of((side * xs + x) * size, size), size)
    for n in range(groups - 1):
        copies.append(send(tb, out.at[cut], s4.at[n], q4.at[n], column(n, 1) * ZLEN + z, c))
    out[cut] = tb[...]
    for copy in dcopies:
        copy.wait()
    for r in range(lats):
        for j in range(4):
            start = r * LON + j * stride
            extra = start % 128
            piece = dq[j, :, r * width : (r + 1) * width]
            if extra == 0:
                dat[:, start : start + width] = piece
                continue
            base = start - extra
            moved = jnp.concatenate([piece.astype(F32), jnp.zeros((rows, 128), F32)], axis=1)
            moved = pltpu.roll(moved, extra, axis=1)
            lead = lax.broadcasted_iota(jnp.int32, (rows, 128), 1)
            dat[:, base : base + 128] = jnp.where(
                lead < extra, dat[:, base : base + 128].astype(F32), moved[:, :128]
            ).astype(BF16)
            dat[:, base + 128 : base + 128 + width] = moved[:, 128:].astype(BF16)
    astore = pltpu.make_async_copy(dat, dat_all, lsem.at[4])
    astore.start()
    for copy in copies:
        copy.wait()
    drain(sp.at[pl.ds(0, 2 * bands - 2)], ss)
    drain(bk.at[pl.ds(0, 2 * bands - 2)], rs)
    dstore.wait()
    astore.wait()


def local(
    atmos, kernels, w_one, w_two, w_flux, sea_mask, route,
    ocean_state, ct_atmos, ct_ocean, wo_one, wo_two,
):
    chans = lax.axis_size("chan")
    bands = lax.axis_size("band")
    rows, points = atmos.shape
    blocks = points // PTS
    quarter = PTS // chans
    lats = points // LON
    share = lats * (LON // quarter // chans + 1) * quarter
    width = share // lats
    slots = ocean_state.shape[2]
    hid = w_one.shape[2]
    full = rows * chans
    wide = wo_one.shape[1]
    total = wide * chans
    groups = bands // ZLEN
    flat = 1536
    big, little = 1088, 384
    size = flat // groups
    small = size // ZLEN
    vm = pl.BlockSpec(memory_space=VMEM)
    anywhere = pl.BlockSpec(memory_space=pl.ANY)

    ocean = VMEM((slots, quarter, PTS), BF16)
    points_first = VMEM((quarter, slots, PTS), BF16)
    split = VMEM((chans, rows, share), BF16)
    extended = VMEM((full, share + 2 * width), BF16)
    square = VMEM((full, share), BF16)
    grouped = VMEM((lats, width // PTS, chans, quarter, PTS), BF16)
    dat, dst, out = pl.pallas_call(
        main_kernel,
        out_shape=[
            jax.ShapeDtypeStruct((rows, points), BF16),
            jax.ShapeDtypeStruct((quarter, slots, PTS), BF16),
            jax.ShapeDtypeStruct((flat, 128), BF16),
        ],
        in_specs=[vm, vm, vm] + [anywhere] * 9,
        out_specs=[anywhere, anywhere, vm],
        scratch_shapes=[
            VMEM((8, 128), jnp.int32),
            pltpu.SMEM((8, 128), jnp.int32),
            VMEM((rows, points), BF16),
            VMEM((rows, points), BF16),
            split, split, extended, square, square,
            VMEM((8, 128), F32),
            VMEM((chans, 8, 128), F32),
            VMEM((full, 128), F32),
            VMEM((chans, full, hid), BF16),
            VMEM((chans, hid, full), BF16),
            VMEM((full, PTS), BF16),
            grouped,
            VMEM((blocks + 1 + 4 * lats, quarter, PTS), BF16),
            VMEM((1, points), F32),
            VMEM((chans, 1, share), F32),
            VMEM((chans, hid, share), BF16),
            VMEM((chans, hid, share), BF16),
            VMEM((rows, points), BF16),
            square, ocean, ocean, ocean, ocean, points_first, points_first, points_first,
            VMEM((2 * PTS, total), BF16),
            VMEM((total, PTS), BF16),
            VMEM((2 * ZLEN * quarter, 2 * ZLEN * quarter), BF16),
            VMEM((2 * PTS, total), F32),
            VMEM((PTS, total), F32),
            VMEM((blocks, quarter, PTS), BF16),
            grouped, square, extended, square, split,
            VMEM((full, share), F32),
            VMEM((hid, share), BF16),
            VMEM((full, PTS), F32),
            VMEM((chans, 16, 128), F32),
            VMEM((chans, 16, 128), F32),
            VMEM((chans, big, 128), BF16),
            VMEM((2, big, 128), BF16),
            VMEM((big, 128), BF16),
            VMEM((3, big // 2, 128), BF16),
            VMEM((chans, little, 128), BF16),
            VMEM((2, little, 128), BF16),
            VMEM((little, 128), BF16),
            VMEM((3, little // 2, 128), BF16),
            VMEM((big, 128), F32),
            VMEM((little, 128), F32),
            VMEM((big // 2, 128), BF16),
            VMEM((little // 2, 128), BF16),
            VMEM((flat // 2, 128), BF16),
            VMEM((groups // 2, size, 128), BF16),
            VMEM((ZLEN, small, 128), F32),
            VMEM((ZLEN, small, 128), F32),
            VMEM((small, 128), F32),
            VMEM((ZLEN, small, 128), F32),
            VMEM((size, 128), BF16),
            DMA((5,)), DMA((7,)), DMA((2, 4)), DMA((2, 4)), DMA((3, 5)), DMA((3, 5)), DMA((4,)), DMA((4,)),
            DMA((3, 4)), DMA((3, 4)), DMA((lats, 4, 2)), DMA((lats, 4, 2)), DMA((4,)), DMA((4,)),
            DMA, DMA((groups,)), DMA, DMA,
            DMA((5,)), DMA((5,)), DMA((lats, 4)), DMA((lats, 4)), DMA((2,)), DMA((2,)),
            DMA((4,)), DMA((4,)), DMA((3, 4)), DMA((3, 4)), DMA((5,)), DMA((5,)),
            DMA((groups,)), DMA((groups,)), DMA((ZLEN,)), DMA((ZLEN,)),
            DMA((ZLEN,)), DMA((ZLEN,)), DMA((groups,)), DMA((groups,)),
        ],
        compiler_params=pltpu.CompilerParams(
            collective_id=0, has_side_effects=True, vmem_limit_bytes=LIMIT
        ),
    )(
        route.T, kernels.transpose(1, 0, 2), sea_mask.reshape(blocks, PTS), atmos, w_one[0], w_two[0],
        w_flux, wo_one, wo_two, ct_atmos, ocean_state, ct_ocean,
    )
    datmos, dk, dw1, dw2, dwf, dstate, do1, do2 = pl.pallas_call(
        finish_kernel,
        out_shape=[
            jax.ShapeDtypeStruct(dat.shape, BF16),
            jax.ShapeDtypeStruct((3, 1, rows), F32),
            jax.ShapeDtypeStruct((full, hid), F32),
            jax.ShapeDtypeStruct((hid, full), F32),
            jax.ShapeDtypeStruct((rows, PTS), F32),
            jax.ShapeDtypeStruct(dst.shape, BF16),
            jax.ShapeDtypeStruct((2 * PTS, wide), F32),
            jax.ShapeDtypeStruct((wide, PTS), F32),
        ],
        in_specs=[vm] * 3,
        out_specs=[vm] * 8,
        compiler_params=pltpu.CompilerParams(vmem_limit_bytes=LIMIT + (4 << 20)),
    )(dat, dst, out)
    return datmos, dk.transpose(1, 0, 2), dw1[None], dw2[None], dwf, dstate[:, None], do1, do2


def solution(mesh):
    in_specs = (
        P("chan", "band"),
        P(None, None, "chan"),
        P(None, None, "chan"),
        P(None, "chan", None),
        P("chan", None),
        P("band"),
        P("band", None),
        P(None, "band", None, None),
        P("chan", "band"),
        P(None, "band", None, None),
        P(None, "chan"),
        P("chan", None),
    )
    out_specs = (
        P("chan", "band"),
        P(None, None, "chan"),
        P(None, None, "chan"),
        P(None, "chan", None),
        P("chan", None),
        P("chan", "band", None, None),
        P(None, "chan"),
        P("chan", None),
    )
    return jax.shard_map(local, mesh=mesh, in_specs=in_specs, out_specs=out_specs, check_vma=False)
```

```python
import functools

import jax
import jax.numpy as jnp
from jax import lax
from jax.experimental import pallas as pl
from jax.experimental.pallas import tpu as pltpu
from jax.sharding import PartitionSpec as P

PTS = 128
LON = 1440
MESH = pl.DeviceIdType.MESH
F32 = jnp.float32
BF16 = jnp.bfloat16
VMEM = pltpu.VMEM
DMA = pltpu.SemaphoreType.DMA
ZLEN = 8
LIMIT = 56 * 1024 * 1024


def nn(a, b):
    return lax.dot_general(a, b, (((1,), (0,)), ((), ())), preferred_element_type=F32)


def tn(a, b):
    return lax.dot_general(a, b, (((0,), (0,)), ((), ())), preferred_element_type=F32)


def nt(a, b):
    return lax.dot_general(a, b, (((1,), (1,)), ((), ())), preferred_element_type=F32)


def sigmoid(v):
    return 0.5 * jnp.tanh(0.5 * v) + 0.5


def place():
    b, c = lax.axis_index("band"), lax.axis_index("chan")
    mate = (c // 2) * 2 + (1 - c % 2)
    return b, c, mate, (c + 2) % 4, (mate + 2) % 4


def send(src, dst, ssem, rsem, b, c):
    copy = pltpu.make_async_remote_copy(
        src_ref=src,
        dst_ref=dst,
        send_sem=ssem,
        recv_sem=rsem,
        device_id=(b, c),
        device_id_type=MESH,
    )
    copy.start()
    return copy


def drain(ref, sem):
    pltpu.make_async_copy(ref, ref, sem).wait()


def signal(b, c):
    pl.semaphore_signal(
        pltpu.get_barrier_semaphore(), inc=1, device_id=(b, c), device_id_type=MESH
    )


def taken(ref, start, width):
    extra = start % 128
    if extra == 0:
        return ref[:, start : start + width].astype(F32)
    wide = ref[:, start - extra : start - extra + width + 128].astype(F32)
    return pltpu.roll(wide, width + 128 - extra, axis=1)[:, :width]


def tables(row):
    blocks = row.shape[1]
    k = lax.broadcasted_iota(jnp.int32, (blocks, blocks), 0)
    j = lax.broadcasted_iota(jnp.int32, (blocks, blocks), 1)
    col = jnp.sum(jnp.where(k == j, row, 0), axis=1, keepdims=True)
    rank = jnp.sum(jnp.where((row == col) & (j < k), 1, 0), axis=1, keepdims=True)
    slot = col * 2 + rank
    k = lax.broadcasted_iota(jnp.int32, (blocks, 128), 0)
    s = lax.broadcasted_iota(jnp.int32, (blocks, 128), 1)
    inv = blocks + jnp.sum(jnp.where(slot == s, k - blocks, 0), axis=0, keepdims=True)
    back = jnp.sum(jnp.where(k == s, slot, 0), axis=0, keepdims=True)
    line = lax.broadcasted_iota(jnp.int32, (8, 128), 0)
    return jnp.where(line == 0, inv, back)


def finish_kernel(dat, dst, out, datmos, dk, dw1, dw2, dwf, dstate, do1, do2):
    half = out.shape[0] // 2
    datmos[...] = dat[...]
    dstate[...] = dst[...]
    dw1[:, :128] = out[:256].astype(F32)
    dw1[:, 128:] = out[256:512].astype(F32)
    dw2[:32, :128] = out[512:544].astype(F32)
    dw2[32:, :128] = out[half : half + 224].astype(F32)
    dw2[:, 128:] = out[half + 224 : half + 480].astype(F32)
    dwf[...] = out[half + 480 : half + 544].astype(F32)
    tile = out[544:560].astype(F32) + out[half + 544 : half + 560].astype(F32)
    for i in range(3):
        dk[i] = tile[i : i + 1, :64]
    do1[:192] = out[576:768].astype(F32)
    do1[192:] = out[half + 576 : half + 640].astype(F32)
    do2[...] = out[half + 640 :].astype(F32).T


def main_kernel(
    route, taps, sea, atmos_all, w_one, w_two, w_flux, wo_one, wo_two, ct_all, state_all, cot_all,
    dat_all, dst, out,
    tabv, table, atmos, dat, al, cl, ext, zb, alm, tapt, tapr, tapf, w1, w2, wf, fx, fm, mk, mk4, hid, slope,
    ctv0, ctb, sp, rf, bk, rb, st, ctv, ds, wa, wb, perm, go1, go2,
    dfp, dfb, gb, dext, dl, dq, dubuf, gwf, gkp, gkr,
    gs, ra, hx, rw, gso, rao, hxo, rxo, own, owno, ownb, ownob, t, r1, fs, r2, fr, ag, tb,
    lsem, msem, hs, hr, ws, wr, ts, tr, as_, ar, fxs, fxr, cs, cr, ss, sr, rs, rr,
    os_, or_, dfs, dfr, h2s, h2r, gks, gkq, das, dar, s0, q0, s1, q1, s2, q2, s3, q3, s4, q4,
):
    b, c, mate, across, diag = place()
    bands = lax.axis_size("band")
    up, down = (b + bands - 1) % bands, (b + 1) % bands
    q, z = b // ZLEN, b % ZLEN
    groups = bands // ZLEN
    flip = ((q // 2) * 2 + (1 - q % 2)) * ZLEN + z
    rows, points = atmos.shape
    full, share = zb.shape
    lats = points // LON
    width = share // lats
    quarter = st.shape[0]
    blocks = dfp.shape[0]
    row_groups = LON // quarter
    few = row_groups // 4
    stride = few * quarter
    wide = wo_one.shape[1]
    peers = [(c + 2) % 4, (c + 1) % 4, (c + 3) % 4]
    order = (2, 1, 3)
    pairs = list(zip(order, peers))

    z_far = (4, 3, 5, 2, 6, 1, 7)
    turn = [(z + i) % ZLEN for i in z_far + (0,)]
    x, xs, side = q // 2, groups // 2, q % 2

    def column(n, way):
        m = n % 4
        dx = (2 + m + m // 2 + 2 * (m // 3)) % 4
        dy = 1 - n // 4
        return ((x + way * dx + xs) % xs) * 2 + (side + dy) % 2

    def greet(n, _):
        base = column(n, 1) * ZLEN
        for to in turn:
            signal(base + to, c)
        return 0

    lax.fori_loop(0, groups - 1, greet, 0)
    for to in turn[:-1]:
        signal(q * ZLEN + to, c)
    signal(flip, across)
    for d in (2, 1, 3):
        signal(b, (c + d) % 4)
    loads = [
        pltpu.make_async_copy(ct_all, ctv0, lsem.at[0]),
        pltpu.make_async_copy(
            state_all.at[pl.ds(pl.multiple_of(quarter * c, quarter), quarter), 0], st, lsem.at[1]
        ),
        pltpu.make_async_copy(
            cot_all.at[pl.ds(pl.multiple_of(quarter * c, quarter), quarter), 0], ctv, lsem.at[2]
        ),
    ]
    mine = pl.ds(pl.multiple_of(c * rows, rows), rows)
    mine_wide = pl.ds(pl.multiple_of(c * wide, wide), wide)
    sources = (w_one, w_two, w_flux, wo_one, wo_two)
    near = (w1.at[c], w2.at[c], wf.at[mine, :], wa.at[:, mine_wide], wb.at[mine_wide, :])
    early = [pltpu.make_async_copy(atmos_all, atmos, msem.at[5])]
    for i in range(5):
        early.append(pltpu.make_async_copy(sources[i], near[i], msem.at[i]))
    for load in early + loads:
        load.start()
    tabv[...] = tables(route[...])
    tcopy = pltpu.make_async_copy(tabv, table, msem.at[6])
    tcopy.start()
    early[0].wait()
    eye = lax.broadcasted_iota(jnp.int32, (rows, rows), 0) == lax.broadcasted_iota(
        jnp.int32, (rows, rows), 1
    )
    for r in (0, lats - 1) + tuple(range(1, lats - 1)):
        for j in range(4):
            al[j, :, r * width : (r + 1) * width] = taken(
                atmos, r * LON + j * stride, width
            ).astype(BF16)
    tapt[...] = jnp.zeros(tapt.shape, F32)
    for i in range(3):
        tapt[i : i + 1, :rows] = taps[i]
    tcopy.wait()
    pl.semaphore_wait(pltpu.get_barrier_semaphore(), bands - 1 + 4)

    cuts = (
        slice(0, width), slice((lats - 1) * width, lats * width), slice(width, (lats - 1) * width)
    )
    acopies = [[], [], []]

    def send_state(k):
        lo, hi = cuts[k].start, cuts[k].stop
        for d, to in pairs:
            acopies[k].append(
                send(
                    al.at[to, :, lo:hi], ext.at[mine, width + lo : width + hi],
                    as_.at[k, d], ar.at[k, d], b, to,
                )
            )

    send_state(0)
    send_state(1)
    theirs = pl.ds(pl.multiple_of(across * rows, rows), rows)
    theirs_wide = pl.ds(pl.multiple_of(across * wide, wide), wide)
    far = (
        w1.at[across], w2.at[across], wf.at[theirs, :],
        wa.at[:, theirs_wide], wb.at[theirs_wide, :],
    )
    first, second, third, tcopies = [], [], [], []
    for i in range(5):
        early[i + 1].wait()
        second.append(send(near[i], near[i], ws.at[1, i], wr.at[1, i], flip, across))
        first.append(send(near[i], near[i], ws.at[0, i], wr.at[0, i], b, mate))
    for d, to in pairs:
        tcopies.append(send(tapt, tapr.at[c], ts.at[d], tr.at[d], b, to))
    send_state(2)
    ext[mine, width : width + share] = al[c]
    tapr[c] = tapt[...]
    halo = []

    def send_halo(k, d):
        at = pl.ds(pl.multiple_of(rows * ((c + 4 - d) % 4), rows), rows)
        if k == 0:
            src, dst, to = (1, 2), (lats + 1, lats + 2), up
        else:
            src, dst, to = (lats, lats + 1), (0, 1), down
        halo.append(
            send(
                ext.at[at, src[0] * width : src[1] * width],
                ext.at[at, dst[0] * width : dst[1] * width],
                hs.at[k, d], hr.at[k, d], to, c,
            )
        )

    send_halo(0, 0)
    send_halo(1, 0)
    for k in (0, 1):
        for n, d in ((1, 1), (2, 3), (0, 2)):
            acopies[k][n].wait()
            send_halo(k, d)
    for i in range(points // PTS):
        mk[:, i * PTS : (i + 1) * PTS] = sea[i : i + 1, :].astype(F32)
    for r in range(lats):
        for j in range(4):
            mk4[j, :, r * width : (r + 1) * width] = taken(mk, r * LON + j * stride, width)
    for copy in tcopies:
        copy.wait()
    for j in range(4):
        for i in range(3):
            tapf[j * rows : (j + 1) * rows, i : i + 1] = jnp.sum(
                jnp.where(eye, tapr[j, i : i + 1, :rows], 0.0), axis=1, keepdims=True
            )
    t0, t1, t2 = tapf[:, 0:1], tapf[:, 1:2], tapf[:, 2:3]
    lane = lax.broadcasted_iota(jnp.int32, (1, share), 1) % width
    kept = jnp.where((lane < stride) | (c == 3), 1.0, 0.0)
    sea_kept = mk4[c] * kept
    for i in range(5):
        second[i].wait_recv()
        third.append(send(far[i], far[i], ws.at[2, i], wr.at[2, i], b, mate))
    for copy in acopies[2]:
        copy.wait()
    for i in range(3):
        first[i].wait()
        second[i].wait_send()
        third[i].wait()
    fcopies = []
    line = (1, 2, 0, 3)
    for r in line:
        if r == 0:
            for copy in halo:
                copy.wait()

            @pl.when(b == 0)
            def _():
                ext[:, :width] = jnp.zeros((full, width), BF16)

            @pl.when(b == bands - 1)
            def _():
                ext[:, (lats + 1) * width :] = jnp.zeros((full, width), BF16)

        cols = slice(r * width, (r + 1) * width)
        state = ext[:, (r + 1) * width : (r + 2) * width].astype(F32)
        zcol = (
            t0 * ext[:, r * width : (r + 1) * width].astype(F32)
            + t1 * state
            + t2 * ext[:, (r + 2) * width : (r + 3) * width].astype(F32)
        ).astype(BF16)
        zb[:, cols] = zcol
        total = None
        for i in range(4):
            u = tn(w1[i], zcol)
            sig = sigmoid(u)
            act = u * sig
            h = act.astype(BF16)
            hid[i, :, cols] = h
            slope[i, :, cols] = (sig + act * (1.0 - sig)).astype(BF16)
            piece = tn(w2[i], h)
            total = piece if total is None else total + piece
        acol = (state + total).astype(BF16)
        acol = (acol.astype(F32) * sea_kept[:, cols]).astype(BF16)
        alm[:, cols] = acol
        fx[r] = tn(acol, wf[...]).astype(BF16).reshape(fx.shape[1:])
        for d, to in pairs:
            i0 = (to + 3 * r + c) % 4
            k0 = (row_groups * r + few * c + i0) // 4
            twice = ((i0 + 1) // 4) * ((6 - c) // 4)
            k2 = k0 + 2 + twice * (blocks + 1 + 4 * c + r - k0 - 2)
            fcopies.append(
                send(
                    fx.at[r, 0:2, i0], fm.at[pl.ds(k0, 2)], fxs.at[r, d, 0], fxr.at[r, d, 0], b, to
                )
            )
            fcopies.append(
                send(
                    fx.at[r, 2:3, i0], fm.at[pl.ds(k2, 1)], fxs.at[r, d, 1], fxr.at[r, d, 1], b, to
                )
            )
        i0 = (2 * c + 3 * r) % 4
        k0 = (row_groups * r + few * c + i0) // 4
        twice = ((i0 + 1) // 4) * ((6 - c) // 4)
        k2 = k0 + 2 + twice * (blocks + 1 + 4 * c + r - k0 - 2)
        fm[pl.ds(k0, 2)] = fx[r, 0:2, i0]
        fm[k2] = fx[r, 2, i0]
    fm[blocks] = jnp.zeros(fm.shape[1:], BF16)
    span = 2 * ZLEN
    size = span * quarter
    r = lax.broadcasted_iota(jnp.int32, (size, size), 0)
    k = lax.broadcasted_iota(jnp.int32, (size, size), 1)
    perm[...] = jnp.where((r % span) * quarter + r // span == k, 1.0, 0.0).astype(BF16)
    go1[...] = jnp.zeros(go1.shape, F32)
    go2[...] = jnp.zeros(go2.shape, F32)
    for load in loads:
        load.wait()
    for i in range(3, 5):
        first[i].wait()
        second[i].wait_send()
        third[i].wait()
    for copy in fcopies:
        copy.wait()


    def couple(n, ways):
        base = column(n, 1) * ZLEN
        for i in range(span):
            sp[2 * base + i] = fm[table[0, 2 * base + i]]
        for way in ways:
            to = base + way
            send(sp.at[pl.ds(2 * to, 2)], rf.at[pl.ds(2 * b, 2)], ss, sr.at[n], to, c)

    def couple_all(n, _):
        couple(n, turn)
        return 0

    lax.fori_loop(0, groups - 1, couple_all, 0)
    couple(groups - 1, turn[:-1])
    rf[pl.ds(2 * b, 2)] = sp[pl.ds(2 * b, 2)]
    for r in range(lats):
        for j in range(4):
            cl[j, :, r * width : (r + 1) * width] = taken(
                ctv0, r * LON + j * stride, width
            ).astype(BF16)
    ctcopies = []
    for d, to in pairs:
        ctcopies.append(send(cl.at[to], ctb.at[mine, :], cs.at[d], cr.at[d], b, to))
    ctb[mine, :] = cl[c]

    def step(n, _):
        @pl.when(n < groups - 1)
        def _():
            drain(rf.at[pl.ds(0, span)], sr.at[n])

        @pl.when(n == groups - 1)
        def _():
            drain(rf.at[pl.ds(0, span - 2)], sr.at[n])

        src = column(n, -1)
        at = pl.ds(pl.multiple_of(src * span, span), span)
        force = nn(perm[...], rf[at].reshape(size, PTS)).astype(BF16)
        both = jnp.concatenate([st[:, at, :].reshape(size, PTS), force], axis=1)
        cot = ctv[:, at, :].reshape(size, PTS)
        pre = nn(both, wa[...])
        sig = sigmoid(pre)
        act = pre * sig
        grad = (nt(cot, wb[...]) * (sig + act * (1.0 - sig))).astype(BF16)
        back = nt(grad, wa[...])
        bk[at] = tn(perm[...], back[:, PTS:].astype(BF16)).astype(BF16).reshape(span, quarter, PTS)

        def give(way):
            to = src * ZLEN + way
            send(bk.at[pl.ds(2 * to, 2)], rb.at[pl.ds(2 * b, 2)], rs, rr, to, c)

        for way in turn[:-1]:
            give(way)

        @pl.when(n < groups - 1)
        def _():
            give(turn[-1])

        ds[:, at, :] = (
            (cot.astype(F32) + back[:, :PTS]).astype(BF16).reshape(quarter, span, PTS)
        )
        go2[...] += tn(cot, act.astype(BF16))
        go1[...] += tn(both, grad)
        return 0

    lax.fori_loop(0, groups, step, 0)
    dstore = pltpu.make_async_copy(ds, dst, lsem.at[3])
    dstore.start()
    rb[pl.ds(2 * b, 2)] = bk[pl.ds(2 * b, 2)]
    for i in range(4):
        gso[i, :256] = go1[:, i * 128 : i * 128 + 128].astype(BF16)
        gso[i, 256:] = go2[:, i * 128 : i * 128 + 128].astype(BF16)
    ocopies = [
        send(gso.at[diag], rao.at[1], os_.at[1], or_.at[1], b, mate),
        send(gso.at[mate], rao.at[0], os_.at[0], or_.at[0], b, mate),
    ]
    for copy in ctcopies:
        copy.wait()
    drain(rb.at[pl.ds(0, 2 * bands - 2)], rr)

    def unpack(k, _):
        dfp[k] = rb[table[1, k]]
        return 0

    lax.fori_loop(0, blocks, unpack, 0)
    dcopies = []
    for r in (0, 3, 1, 2):
        for d, to in pairs:
            i0 = (c + 3 * r + to) % 4
            k0 = (row_groups * r + few * to + i0) // 4
            dcopies.append(
                send(dfp.at[pl.ds(k0, 3)], dfb.at[r, :, i0], dfs.at[r, d], dfr.at[r, d], b, to)
            )
        i0 = (2 * c + 3 * r) % 4
        k0 = (row_groups * r + few * c + i0) // 4
        dfb[r, :, i0] = dfp[pl.ds(k0, 3)]
    for copy in ocopies:
        copy.wait()
    little, big = rxo.shape[1], rw.shape[1]
    kept_little = pl.ds(pl.multiple_of(little * side, little), little)
    sent_little = pl.ds(pl.multiple_of(little * (1 - side), little), little)
    kept_big = pl.ds(pl.multiple_of(big * side, big), big)
    sent_big = pl.ds(pl.multiple_of(big * (1 - side), big), big)
    hxo[...] = (gso[across].astype(F32) + rao[1].astype(F32)).astype(BF16)
    owno[...] = gso[c].astype(F32) + rao[0].astype(F32)
    ownob[...] = owno[sent_little].astype(BF16)
    for n, r in enumerate((0, 3, 1, 2)):
        for copy in dcopies[3 * n : 3 * n + 3]:
            copy.wait()
        cols = slice(r * width, (r + 1) * width)
        flux = dfb[r].reshape(width, PTS)
        gb[:, cols] = (
            ctb[:, cols].astype(F32) * kept[:, cols] + nt(wf[...], flux) * sea_kept[:, cols]
        ).astype(BF16)
    ocopies = [
        send(ownob, rxo.at[2], os_.at[4], or_.at[4], flip, c),
        send(hxo.at[kept_little], rxo.at[0], os_.at[2], or_.at[2], b, across),
        send(hxo.at[sent_little], rxo.at[1], os_.at[3], or_.at[3], flip, across),
    ]
    gwf[...] = nn(alm[...], dfb[...].reshape(share, PTS))
    wcopies = []
    halo = []
    for turn, i in enumerate((mate, diag, c, across)):
        for r in range(lats):
            cols = slice(r * width, (r + 1) * width)
            dubuf[i, :, cols] = (
                nn(w2[i], gb[:, cols]) * slope[i, :, cols].astype(F32)
            ).astype(BF16)
        g1 = nt(zb[...], dubuf[i])
        g2 = nt(hid[i], gb[...])
        for j in range(2):
            gs[i, j * 256 : j * 256 + 256] = g1[:, j * 128 : j * 128 + 128].astype(BF16)
            gs[i, 512 + j * 256 : 768 + j * 256] = g2[:, j * 128 : j * 128 + 128].astype(BF16)
        gs[i, 1024:1088] = gwf[pl.ds(pl.multiple_of(rows * i, rows), rows), :].astype(BF16)
        if turn == 0:
            mcopies = [send(gs.at[mate], ra.at[0], s0.at[0], q0.at[0], b, mate)]
        if turn == 1:
            mcopies.append(send(gs.at[diag], ra.at[1], s0.at[1], q0.at[1], b, mate))
        if turn == 2:
            mcopies[0].wait()
            own[...] = gs[c].astype(F32) + ra[0].astype(F32)
            ownb[...] = own[sent_big].astype(BF16)
            wcopies.append(send(ownb, rw.at[2], s0.at[4], q0.at[4], flip, c))
        if turn == 3:
            mcopies[1].wait()
            hx[...] = (gs[across].astype(F32) + ra[1].astype(F32)).astype(BF16)
            wcopies.append(send(hx.at[kept_big], rw.at[0], s0.at[2], q0.at[2], b, across))
            wcopies.append(send(hx.at[sent_big], rw.at[1], s0.at[3], q0.at[3], flip, across))
    for r in (0, 3, 1, 2):
        cols = slice(r * width, (r + 1) * width)
        total = None
        for i in range(4):
            piece = nn(w1[i], dubuf[i, :, cols])
            total = piece if total is None else total + piece
        at = (r + 1) * width
        dext[:, at : at + width] = total.astype(BF16)
        if r == 0:
            halo.append(
                send(
                    dext.at[:, at : at + width], dext.at[:, (lats + 1) * width :],
                    h2s.at[1], h2r.at[1], up, c,
                )
            )
        if r == 3:
            halo.append(
                send(
                    dext.at[:, at : at + width], dext.at[:, :width],
                    h2s.at[0], h2r.at[0], down, c,
                )
            )
    gkp[...] = jnp.zeros(gkp.shape, F32)
    for i in range(3):
        acc = jnp.zeros((full, 128), F32)
        for r in range(lats):
            prod = ext[:, (r + i) * width : (r + i + 1) * width].astype(F32) * dext[
                :, (r + 1) * width : (r + 2) * width
            ].astype(F32)
            for o in range(0, width, 128):
                acc = acc + prod[:, o : o + 128]
        acc = jnp.sum(acc, axis=1, keepdims=True)
        for j in range(4):
            gkp[j, i : i + 1, :rows] = jnp.sum(
                jnp.where(eye, acc[j * rows : (j + 1) * rows], 0.0), axis=0, keepdims=True
            )
    kcopies = []
    for d, to in pairs:
        kcopies.append(send(gkp.at[to], gkr.at[d], gks.at[d], gkq.at[d], b, to))
    dcopies = []

    def spread(r):
        cols = slice(r * width, (r + 1) * width)
        dl[:, cols] = (
            gb[:, cols].astype(F32)
            + t0 * dext[:, (r + 2) * width : (r + 3) * width].astype(F32)
            + t1 * dext[:, (r + 1) * width : (r + 2) * width].astype(F32)
            + t2 * dext[:, r * width : (r + 1) * width].astype(F32)
        ).astype(BF16)

    def send_back(k):
        lo, hi = cuts[k].start, cuts[k].stop
        for d, to in pairs:
            theirs = pl.ds(pl.multiple_of(rows * to, rows), rows)
            dcopies.append(
                send(dl.at[theirs, lo:hi], dq.at[c, :, lo:hi], das.at[k, d], dar.at[k, d], b, to)
            )

    spread(1)
    spread(2)
    for copy in ocopies:
        copy.wait()
    t[big + 32 :] = (
        owno[kept_little]
        + rxo[0].astype(F32)
        + rxo[1].astype(F32)
        + rxo[2].astype(F32)
    ).astype(BF16)
    for copy in kcopies:
        copy.wait()
    t[big : big + 16] = (gkp[c] + gkr[1] + gkr[2] + gkr[3]).astype(BF16)
    t[big + 16 : big + 32] = jnp.zeros((16, 128), BF16)
    for copy in wcopies:
        copy.wait()
    t[:big] = (
        own[kept_big] + rw[0].astype(F32) + rw[1].astype(F32) + rw[2].astype(F32)
    ).astype(BF16)
    size = r1.shape[1]
    copies = []
    for d in (2, 1, 3):
        to = (x + d) % xs
        cut = pl.ds(pl.multiple_of(to * size, size), size)
        copies.append(
            send(t.at[cut], r1.at[x], s1.at[d], q1.at[d], (2 * to + side) * ZLEN + z, c)
        )
    send_back(2)
    r1[x] = t[pl.ds(pl.multiple_of(x * size, size), size)]
    for copy in halo:
        copy.wait()

    @pl.when(b == 0)
    def _():
        dext[:, :width] = jnp.zeros((full, width), BF16)

    @pl.when(b == bands - 1)
    def _():
        dext[:, (lats + 1) * width :] = jnp.zeros((full, width), BF16)

    spread(0)
    send_back(0)
    spread(3)
    send_back(1)
    dq[c] = dl[mine, :]
    for copy in copies:
        copy.wait()
    total = r1[0].astype(F32)
    for i in range(1, xs):
        total = total + r1[i].astype(F32)
    fs[...] = total.reshape(fs.shape)
    copies = []
    for d in z_far:
        to = (z + d) % ZLEN
        copies.append(send(fs.at[to], r2.at[z], s2.at[d], q2.at[d], q * ZLEN + to, c))
    r2[z] = fs[z]
    for copy in copies:
        copy.wait()
    total = r2[0]
    for i in range(1, ZLEN):
        total = total + r2[i]
    fr[...] = total
    copies = []
    for d in z_far:
        to = (z + d) % ZLEN
        copies.append(send(fr, ag.at[z], s3.at[d], q3.at[d], q * ZLEN + to, c))
    ag[z] = total
    for copy in copies:
        copy.wait()
    tb[...] = ag[...].reshape(size, 128).astype(BF16)
    copies = []
    cut = pl.ds(pl.multiple_of((side * xs + x) * size, size), size)
    for n in range(groups - 1):
        copies.append(send(tb, out.at[cut], s4.at[n], q4.at[n], column(n, 1) * ZLEN + z, c))
    out[cut] = tb[...]
    for copy in dcopies:
        copy.wait()
    for r in range(lats):
        for j in range(4):
            start = r * LON + j * stride
            extra = start % 128
            piece = dq[j, :, r * width : (r + 1) * width]
            if extra == 0:
                dat[:, start : start + width] = piece
                continue
            base = start - extra
            moved = jnp.concatenate([piece.astype(F32), jnp.zeros((rows, 128), F32)], axis=1)
            moved = pltpu.roll(moved, extra, axis=1)
            lead = lax.broadcasted_iota(jnp.int32, (rows, 128), 1)
            dat[:, base : base + 128] = jnp.where(
                lead < extra, dat[:, base : base + 128].astype(F32), moved[:, :128]
            ).astype(BF16)
            dat[:, base + 128 : base + 128 + width] = moved[:, 128:].astype(BF16)
    astore = pltpu.make_async_copy(dat, dat_all, lsem.at[4])
    astore.start()
    for copy in copies:
        copy.wait()
    drain(sp.at[pl.ds(0, 2 * bands - 2)], ss)
    drain(bk.at[pl.ds(0, 2 * bands - 2)], rs)
    dstore.wait()
    astore.wait()


def local(
    atmos, kernels, w_one, w_two, w_flux, sea_mask, route,
    ocean_state, ct_atmos, ct_ocean, wo_one, wo_two,
):
    chans = lax.axis_size("chan")
    bands = lax.axis_size("band")
    rows, points = atmos.shape
    blocks = points // PTS
    quarter = PTS // chans
    lats = points // LON
    share = lats * (LON // quarter // chans + 1) * quarter
    width = share // lats
    slots = ocean_state.shape[2]
    hid = w_one.shape[2]
    full = rows * chans
    wide = wo_one.shape[1]
    total = wide * chans
    groups = bands // ZLEN
    flat = 1536
    big, little = 1088, 384
    size = flat // groups
    small = size // ZLEN
    vm = pl.BlockSpec(memory_space=VMEM)
    anywhere = pl.BlockSpec(memory_space=pl.ANY)

    ocean = VMEM((slots, quarter, PTS), BF16)
    points_first = VMEM((quarter, slots, PTS), BF16)
    split = VMEM((chans, rows, share), BF16)
    extended = VMEM((full, share + 2 * width), BF16)
    square = VMEM((full, share), BF16)
    grouped = VMEM((lats, width // PTS, chans, quarter, PTS), BF16)
    dat, dst, out = pl.pallas_call(
        main_kernel,
        out_shape=[
            jax.ShapeDtypeStruct((rows, points), BF16),
            jax.ShapeDtypeStruct((quarter, slots, PTS), BF16),
            jax.ShapeDtypeStruct((flat, 128), BF16),
        ],
        in_specs=[vm, vm, vm] + [anywhere] * 9,
        out_specs=[anywhere, anywhere, vm],
        scratch_shapes=[
            VMEM((8, 128), jnp.int32),
            pltpu.SMEM((8, 128), jnp.int32),
            VMEM((rows, points), BF16),
            VMEM((rows, points), BF16),
            split, split, extended, square, square,
            VMEM((8, 128), F32),
            VMEM((chans, 8, 128), F32),
            VMEM((full, 128), F32),
            VMEM((chans, full, hid), BF16),
            VMEM((chans, hid, full), BF16),
            VMEM((full, PTS), BF16),
            grouped,
            VMEM((blocks + 1 + 4 * lats, quarter, PTS), BF16),
            VMEM((1, points), F32),
            VMEM((chans, 1, share), F32),
            VMEM((chans, hid, share), BF16),
            VMEM((chans, hid, share), BF16),
            VMEM((rows, points), BF16),
            square, ocean, ocean, ocean, ocean, points_first, points_first, points_first,
            VMEM((2 * PTS, total), BF16),
            VMEM((total, PTS), BF16),
            VMEM((2 * ZLEN * quarter, 2 * ZLEN * quarter), BF16),
            VMEM((2 * PTS, total), F32),
            VMEM((PTS, total), F32),
            VMEM((blocks, quarter, PTS), BF16),
            grouped, square, extended, square, split,
            VMEM((chans, hid, share), BF16),
            VMEM((full, PTS), F32),
            VMEM((chans, 16, 128), F32),
            VMEM((chans, 16, 128), F32),
            VMEM((chans, big, 128), BF16),
            VMEM((2, big, 128), BF16),
            VMEM((big, 128), BF16),
            VMEM((3, big // 2, 128), BF16),
            VMEM((chans, little, 128), BF16),
            VMEM((2, little, 128), BF16),
            VMEM((little, 128), BF16),
            VMEM((3, little // 2, 128), BF16),
            VMEM((big, 128), F32),
            VMEM((little, 128), F32),
            VMEM((big // 2, 128), BF16),
            VMEM((little // 2, 128), BF16),
            VMEM((flat // 2, 128), BF16),
            VMEM((groups // 2, size, 128), BF16),
            VMEM((ZLEN, small, 128), F32),
            VMEM((ZLEN, small, 128), F32),
            VMEM((small, 128), F32),
            VMEM((ZLEN, small, 128), F32),
            VMEM((size, 128), BF16),
            DMA((5,)), DMA((7,)), DMA((2, 4)), DMA((2, 4)), DMA((3, 5)), DMA((3, 5)), DMA((4,)), DMA((4,)),
            DMA((3, 4)), DMA((3, 4)), DMA((lats, 4, 2)), DMA((lats, 4, 2)), DMA((4,)), DMA((4,)),
            DMA, DMA((groups,)), DMA, DMA,
            DMA((5,)), DMA((5,)), DMA((lats, 4)), DMA((lats, 4)), DMA((2,)), DMA((2,)),
            DMA((4,)), DMA((4,)), DMA((3, 4)), DMA((3, 4)), DMA((5,)), DMA((5,)),
            DMA((groups,)), DMA((groups,)), DMA((ZLEN,)), DMA((ZLEN,)),
            DMA((ZLEN,)), DMA((ZLEN,)), DMA((groups,)), DMA((groups,)),
        ],
        compiler_params=pltpu.CompilerParams(
            collective_id=0, has_side_effects=True, vmem_limit_bytes=LIMIT
        ),
    )(
        route.T, kernels.transpose(1, 0, 2), sea_mask.reshape(blocks, PTS), atmos, w_one[0], w_two[0],
        w_flux, wo_one, wo_two, ct_atmos, ocean_state, ct_ocean,
    )
    datmos, dk, dw1, dw2, dwf, dstate, do1, do2 = pl.pallas_call(
        finish_kernel,
        out_shape=[
            jax.ShapeDtypeStruct(dat.shape, BF16),
            jax.ShapeDtypeStruct((3, 1, rows), F32),
            jax.ShapeDtypeStruct((full, hid), F32),
            jax.ShapeDtypeStruct((hid, full), F32),
            jax.ShapeDtypeStruct((rows, PTS), F32),
            jax.ShapeDtypeStruct(dst.shape, BF16),
            jax.ShapeDtypeStruct((2 * PTS, wide), F32),
            jax.ShapeDtypeStruct((wide, PTS), F32),
        ],
        in_specs=[vm] * 3,
        out_specs=[vm] * 8,
        compiler_params=pltpu.CompilerParams(vmem_limit_bytes=LIMIT + (4 << 20)),
    )(dat, dst, out)
    return datmos, dk.transpose(1, 0, 2), dw1[None], dw2[None], dwf, dstate[:, None], do1, do2


def solution(mesh):
    in_specs = (
        P("chan", "band"),
        P(None, None, "chan"),
        P(None, None, "chan"),
        P(None, "chan", None),
        P("chan", None),
        P("band"),
        P("band", None),
        P(None, "band", None, None),
        P("chan", "band"),
        P(None, "band", None, None),
        P(None, "chan"),
        P("chan", None),
    )
    out_specs = (
        P("chan", "band"),
        P(None, None, "chan"),
        P(None, None, "chan"),
        P(None, "chan", None),
        P("chan", None),
        P("chan", "band", None, None),
        P(None, "chan"),
        P("chan", None),
    )
    return jax.shard_map(local, mesh=mesh, in_specs=in_specs, out_specs=out_specs, check_vma=False)
```

```python
import functools

import jax
import jax.numpy as jnp
from jax import lax
from jax.experimental import pallas as pl
from jax.experimental.pallas import tpu as pltpu
from jax.sharding import PartitionSpec as P

PTS = 128
LON = 1440
MESH = pl.DeviceIdType.MESH
F32 = jnp.float32
BF16 = jnp.bfloat16
VMEM = pltpu.VMEM
DMA = pltpu.SemaphoreType.DMA
ZLEN = 8
LIMIT = 56 * 1024 * 1024


def nn(a, b):
    return lax.dot_general(a, b, (((1,), (0,)), ((), ())), preferred_element_type=F32)


def tn(a, b):
    return lax.dot_general(a, b, (((0,), (0,)), ((), ())), preferred_element_type=F32)


def nt(a, b):
    return lax.dot_general(a, b, (((1,), (1,)), ((), ())), preferred_element_type=F32)


def sigmoid(v):
    return 0.5 * jnp.tanh(0.5 * v) + 0.5


def place():
    b, c = lax.axis_index("band"), lax.axis_index("chan")
    mate = (c // 2) * 2 + (1 - c % 2)
    return b, c, mate, (c + 2) % 4, (mate + 2) % 4


def send(src, dst, ssem, rsem, b, c):
    copy = pltpu.make_async_remote_copy(
        src_ref=src,
        dst_ref=dst,
        send_sem=ssem,
        recv_sem=rsem,
        device_id=(b, c),
        device_id_type=MESH,
    )
    copy.start()
    return copy


def drain(ref, sem):
    pltpu.make_async_copy(ref, ref, sem).wait()


def signal(b, c):
    pl.semaphore_signal(
        pltpu.get_barrier_semaphore(), inc=1, device_id=(b, c), device_id_type=MESH
    )


def taken(ref, start, width):
    extra = start % 128
    if extra == 0:
        return ref[:, start : start + width].astype(F32)
    wide = ref[:, start - extra : start - extra + width + 128].astype(F32)
    return pltpu.roll(wide, width + 128 - extra, axis=1)[:, :width]


def tables(row):
    blocks = row.shape[1]
    k = lax.broadcasted_iota(jnp.int32, (blocks, blocks), 0)
    j = lax.broadcasted_iota(jnp.int32, (blocks, blocks), 1)
    col = jnp.sum(jnp.where(k == j, row, 0), axis=1, keepdims=True)
    rank = jnp.sum(jnp.where((row == col) & (j < k), 1, 0), axis=1, keepdims=True)
    slot = col * 2 + rank
    k = lax.broadcasted_iota(jnp.int32, (blocks, 128), 0)
    s = lax.broadcasted_iota(jnp.int32, (blocks, 128), 1)
    inv = blocks + jnp.sum(jnp.where(slot == s, k - blocks, 0), axis=0, keepdims=True)
    back = jnp.sum(jnp.where(k == s, slot, 0), axis=0, keepdims=True)
    line = lax.broadcasted_iota(jnp.int32, (8, 128), 0)
    return jnp.where(line == 0, inv, back)


def finish_kernel(dat, dst, out, datmos, dk, dw1, dw2, dwf, dstate, do1, do2):
    half = out.shape[0] // 2
    datmos[...] = dat[...]
    dstate[...] = dst[...]
    dw1[:, :128] = out[:256].astype(F32)
    dw1[:, 128:] = out[256:512].astype(F32)
    dw2[:32, :128] = out[512:544].astype(F32)
    dw2[32:, :128] = out[half : half + 224].astype(F32)
    dw2[:, 128:] = out[half + 224 : half + 480].astype(F32)
    dwf[...] = out[half + 480 : half + 544].astype(F32)
    tile = out[544:560].astype(F32) + out[half + 544 : half + 560].astype(F32)
    for i in range(3):
        dk[i] = tile[i : i + 1, :64]
    do1[:192] = out[576:768].astype(F32)
    do1[192:] = out[half + 576 : half + 640].astype(F32)
    do2[...] = out[half + 640 :].astype(F32).T


def main_kernel(
    route, taps, sea, atmos_all, w_one, w_two, w_flux, wo_one, wo_two, ct_all, state_all, cot_all,
    dat_all, dst, out,
    tabv, table, atmos, dat, al, cl, ext, zb, alm, tapt, tapr, tapf, w1, w2, wf, fx, fm, mk, mk4, hid, slope,
    ctv0, ctb, sp, rf, bk, rb, st, ctv, ds, wa, wb, perm, go1, go2,
    dfp, dfb, gb, dext, dl, dq, dzacc, dubuf, gwf, gkp, gkr,
    gs, ra, hx, rw, gso, rao, hxo, rxo, own, owno, ownb, ownob, t, r1, fs, r2, fr, ag, tb,
    lsem, msem, hs, hr, ws, wr, ts, tr, as_, ar, fxs, fxr, cs, cr, ss, sr, rs, rr,
    os_, or_, dfs, dfr, h2s, h2r, gks, gkq, das, dar, s0, q0, s1, q1, s2, q2, s3, q3, s4, q4,
):
    b, c, mate, across, diag = place()
    bands = lax.axis_size("band")
    up, down = (b + bands - 1) % bands, (b + 1) % bands
    q, z = b // ZLEN, b % ZLEN
    groups = bands // ZLEN
    flip = ((q // 2) * 2 + (1 - q % 2)) * ZLEN + z
    rows, points = atmos.shape
    full, share = zb.shape
    lats = points // LON
    width = share // lats
    quarter = st.shape[0]
    blocks = dfp.shape[0]
    row_groups = LON // quarter
    few = row_groups // 4
    stride = few * quarter
    wide = wo_one.shape[1]
    peers = [(c + 2) % 4, (c + 1) % 4, (c + 3) % 4]
    order = (2, 1, 3)
    pairs = list(zip(order, peers))

    z_far = (4, 3, 5, 2, 6, 1, 7)
    turn = [(z + i) % ZLEN for i in z_far + (0,)]
    x, xs, side = q // 2, groups // 2, q % 2

    def column(n, way):
        m = n % 4
        dx = (2 + m + m // 2 + 2 * (m // 3)) % 4
        dy = 1 - n // 4
        return ((x + way * dx + xs) % xs) * 2 + (side + dy) % 2

    def greet(n, _):
        base = column(n, 1) * ZLEN
        for to in turn:
            signal(base + to, c)
        return 0

    lax.fori_loop(0, groups - 1, greet, 0)
    for to in turn[:-1]:
        signal(q * ZLEN + to, c)
    signal(flip, across)
    for d in (2, 1, 3):
        signal(b, (c + d) % 4)
    loads = [
        pltpu.make_async_copy(ct_all, ctv0, lsem.at[0]),
        pltpu.make_async_copy(
            state_all.at[pl.ds(pl.multiple_of(quarter * c, quarter), quarter), 0], st, lsem.at[1]
        ),
        pltpu.make_async_copy(
            cot_all.at[pl.ds(pl.multiple_of(quarter * c, quarter), quarter), 0], ctv, lsem.at[2]
        ),
    ]
    mine = pl.ds(pl.multiple_of(c * rows, rows), rows)
    mine_wide = pl.ds(pl.multiple_of(c * wide, wide), wide)
    sources = (w_one, w_two, w_flux, wo_one, wo_two)
    near = (w1.at[c], w2.at[c], wf.at[mine, :], wa.at[:, mine_wide], wb.at[mine_wide, :])
    early = [pltpu.make_async_copy(atmos_all, atmos, msem.at[5])]
    for i in range(5):
        early.append(pltpu.make_async_copy(sources[i], near[i], msem.at[i]))
    for load in early + loads:
        load.start()
    tabv[...] = tables(route[...])
    tcopy = pltpu.make_async_copy(tabv, table, msem.at[6])
    tcopy.start()
    early[0].wait()
    eye = lax.broadcasted_iota(jnp.int32, (rows, rows), 0) == lax.broadcasted_iota(
        jnp.int32, (rows, rows), 1
    )
    for r in (0, lats - 1) + tuple(range(1, lats - 1)):
        for j in range(4):
            al[j, :, r * width : (r + 1) * width] = taken(
                atmos, r * LON + j * stride, width
            ).astype(BF16)
    tapt[...] = jnp.zeros(tapt.shape, F32)
    for i in range(3):
        tapt[i : i + 1, :rows] = taps[i]
    tcopy.wait()
    pl.semaphore_wait(pltpu.get_barrier_semaphore(), bands - 1 + 4)

    cuts = (
        slice(0, width), slice((lats - 1) * width, lats * width), slice(width, (lats - 1) * width)
    )
    acopies = [[], [], []]

    def send_state(k):
        lo, hi = cuts[k].start, cuts[k].stop
        for d, to in pairs:
            acopies[k].append(
                send(
                    al.at[to, :, lo:hi], ext.at[mine, width + lo : width + hi],
                    as_.at[k, d], ar.at[k, d], b, to,
                )
            )

    send_state(0)
    send_state(1)
    theirs = pl.ds(pl.multiple_of(across * rows, rows), rows)
    theirs_wide = pl.ds(pl.multiple_of(across * wide, wide), wide)
    far = (
        w1.at[across], w2.at[across], wf.at[theirs, :],
        wa.at[:, theirs_wide], wb.at[theirs_wide, :],
    )
    first, second, third, tcopies = [], [], [], []
    for i in range(5):
        early[i + 1].wait()
        second.append(send(near[i], near[i], ws.at[1, i], wr.at[1, i], flip, across))
        first.append(send(near[i], near[i], ws.at[0, i], wr.at[0, i], b, mate))
    for d, to in pairs:
        tcopies.append(send(tapt, tapr.at[c], ts.at[d], tr.at[d], b, to))
    send_state(2)
    ext[mine, width : width + share] = al[c]
    tapr[c] = tapt[...]
    halo = []

    def send_halo(k, d):
        at = pl.ds(pl.multiple_of(rows * ((c + 4 - d) % 4), rows), rows)
        if k == 0:
            src, dst, to = (1, 2), (lats + 1, lats + 2), up
        else:
            src, dst, to = (lats, lats + 1), (0, 1), down
        halo.append(
            send(
                ext.at[at, src[0] * width : src[1] * width],
                ext.at[at, dst[0] * width : dst[1] * width],
                hs.at[k, d], hr.at[k, d], to, c,
            )
        )

    send_halo(0, 0)
    send_halo(1, 0)
    for k in (0, 1):
        for n, d in ((1, 1), (2, 3), (0, 2)):
            acopies[k][n].wait()
            send_halo(k, d)
    for i in range(points // PTS):
        mk[:, i * PTS : (i + 1) * PTS] = sea[i : i + 1, :].astype(F32)
    for r in range(lats):
        for j in range(4):
            mk4[j, :, r * width : (r + 1) * width] = taken(mk, r * LON + j * stride, width)
    for copy in tcopies:
        copy.wait()
    for j in range(4):
        for i in range(3):
            tapf[j * rows : (j + 1) * rows, i : i + 1] = jnp.sum(
                jnp.where(eye, tapr[j, i : i + 1, :rows], 0.0), axis=1, keepdims=True
            )
    t0, t1, t2 = tapf[:, 0:1], tapf[:, 1:2], tapf[:, 2:3]
    lane = lax.broadcasted_iota(jnp.int32, (1, share), 1) % width
    kept = jnp.where((lane < stride) | (c == 3), 1.0, 0.0)
    sea_kept = mk4[c] * kept
    for i in range(5):
        second[i].wait_recv()
        third.append(send(far[i], far[i], ws.at[2, i], wr.at[2, i], b, mate))
    for copy in acopies[2]:
        copy.wait()
    for i in range(3):
        first[i].wait()
        second[i].wait_send()
        third[i].wait()
    fcopies = []
    line = (1, 2, 0, 3)
    for r in line:
        if r == 0:
            for copy in halo:
                copy.wait()

            @pl.when(b == 0)
            def _():
                ext[:, :width] = jnp.zeros((full, width), BF16)

            @pl.when(b == bands - 1)
            def _():
                ext[:, (lats + 1) * width :] = jnp.zeros((full, width), BF16)

        cols = slice(r * width, (r + 1) * width)
        state = ext[:, (r + 1) * width : (r + 2) * width].astype(F32)
        zcol = (
            t0 * ext[:, r * width : (r + 1) * width].astype(F32)
            + t1 * state
            + t2 * ext[:, (r + 2) * width : (r + 3) * width].astype(F32)
        ).astype(BF16)
        zb[:, cols] = zcol
        total = None
        for i in range(4):
            u = tn(w1[i], zcol)
            sig = sigmoid(u)
            act = u * sig
            h = act.astype(BF16)
            hid[i, :, cols] = h
            slope[i, :, cols] = (sig + act * (1.0 - sig)).astype(BF16)
            piece = tn(w2[i], h)
            total = piece if total is None else total + piece
        acol = (state + total).astype(BF16)
        acol = (acol.astype(F32) * sea_kept[:, cols]).astype(BF16)
        alm[:, cols] = acol
        fx[r] = tn(acol, wf[...]).astype(BF16).reshape(fx.shape[1:])
        for d, to in pairs:
            i0 = (to + 3 * r + c) % 4
            k0 = (row_groups * r + few * c + i0) // 4
            twice = ((i0 + 1) // 4) * ((6 - c) // 4)
            k2 = k0 + 2 + twice * (blocks + 1 + 4 * c + r - k0 - 2)
            fcopies.append(
                send(
                    fx.at[r, 0:2, i0], fm.at[pl.ds(k0, 2)], fxs.at[r, d, 0], fxr.at[r, d, 0], b, to
                )
            )
            fcopies.append(
                send(
                    fx.at[r, 2:3, i0], fm.at[pl.ds(k2, 1)], fxs.at[r, d, 1], fxr.at[r, d, 1], b, to
                )
            )
        i0 = (2 * c + 3 * r) % 4
        k0 = (row_groups * r + few * c + i0) // 4
        twice = ((i0 + 1) // 4) * ((6 - c) // 4)
        k2 = k0 + 2 + twice * (blocks + 1 + 4 * c + r - k0 - 2)
        fm[pl.ds(k0, 2)] = fx[r, 0:2, i0]
        fm[k2] = fx[r, 2, i0]
    fm[blocks] = jnp.zeros(fm.shape[1:], BF16)
    span = 2 * ZLEN
    size = span * quarter
    r = lax.broadcasted_iota(jnp.int32, (size, size), 0)
    k = lax.broadcasted_iota(jnp.int32, (size, size), 1)
    perm[...] = jnp.where((r % span) * quarter + r // span == k, 1.0, 0.0).astype(BF16)
    go1[...] = jnp.zeros(go1.shape, F32)
    go2[...] = jnp.zeros(go2.shape, F32)
    for load in loads:
        load.wait()
    for i in range(3, 5):
        first[i].wait()
        second[i].wait_send()
        third[i].wait()
    for copy in fcopies:
        copy.wait()


    def couple(n, ways):
        base = column(n, 1) * ZLEN
        for i in range(span):
            sp[2 * base + i] = fm[table[0, 2 * base + i]]
        for way in ways:
            to = base + way
            send(sp.at[pl.ds(2 * to, 2)], rf.at[pl.ds(2 * b, 2)], ss, sr.at[n], to, c)

    def couple_all(n, _):
        couple(n, turn)
        return 0

    lax.fori_loop(0, groups - 1, couple_all, 0)
    couple(groups - 1, turn[:-1])
    rf[pl.ds(2 * b, 2)] = sp[pl.ds(2 * b, 2)]
    for r in range(lats):
        for j in range(4):
            cl[j, :, r * width : (r + 1) * width] = taken(
                ctv0, r * LON + j * stride, width
            ).astype(BF16)
    ctcopies = []
    for d, to in pairs:
        ctcopies.append(
            pltpu.make_async_remote_copy(
                src_ref=cl.at[to],
                dst_ref=ctb.at[mine, :],
                send_sem=cs.at[d],
                recv_sem=cr.at[d],
                device_id=(b, to),
                device_id_type=MESH,
            )
        )
    ctb[mine, :] = cl[c]

    def step(n, _):
        @pl.when(n < groups - 1)
        def _():
            drain(rf.at[pl.ds(0, span)], sr.at[n])

        @pl.when(n == groups - 1)
        def _():
            drain(rf.at[pl.ds(0, span - 2)], sr.at[n])

        @pl.when(n == groups // 2)
        def _():
            for copy in ctcopies:
                copy.start()

        src = column(n, -1)
        at = pl.ds(pl.multiple_of(src * span, span), span)
        force = nn(perm[...], rf[at].reshape(size, PTS)).astype(BF16)
        both = jnp.concatenate([st[:, at, :].reshape(size, PTS), force], axis=1)
        cot = ctv[:, at, :].reshape(size, PTS)
        pre = nn(both, wa[...])
        sig = sigmoid(pre)
        act = pre * sig
        grad = (nt(cot, wb[...]) * (sig + act * (1.0 - sig))).astype(BF16)
        back = nt(grad, wa[...])
        bk[at] = tn(perm[...], back[:, PTS:].astype(BF16)).astype(BF16).reshape(span, quarter, PTS)

        def give(way):
            to = src * ZLEN + way
            send(bk.at[pl.ds(2 * to, 2)], rb.at[pl.ds(2 * b, 2)], rs, rr, to, c)

        for way in turn[:-1]:
            give(way)

        @pl.when(n < groups - 1)
        def _():
            give(turn[-1])

        ds[:, at, :] = (
            (cot.astype(F32) + back[:, :PTS]).astype(BF16).reshape(quarter, span, PTS)
        )
        go2[...] += tn(cot, act.astype(BF16))
        go1[...] += tn(both, grad)
        return 0

    lax.fori_loop(0, groups, step, 0)
    dstore = pltpu.make_async_copy(ds, dst, lsem.at[3])
    dstore.start()
    rb[pl.ds(2 * b, 2)] = bk[pl.ds(2 * b, 2)]
    for i in range(4):
        gso[i, :256] = go1[:, i * 128 : i * 128 + 128].astype(BF16)
        gso[i, 256:] = go2[:, i * 128 : i * 128 + 128].astype(BF16)
    ocopies = [
        send(gso.at[diag], rao.at[1], os_.at[1], or_.at[1], b, mate),
        send(gso.at[mate], rao.at[0], os_.at[0], or_.at[0], b, mate),
    ]
    for copy in ctcopies:
        copy.wait()
    drain(rb.at[pl.ds(0, 2 * bands - 2)], rr)

    def unpack(k, _):
        dfp[k] = rb[table[1, k]]
        return 0

    lax.fori_loop(0, blocks, unpack, 0)
    dcopies = []
    for r in (0, 3, 1, 2):
        for d, to in pairs:
            i0 = (c + 3 * r + to) % 4
            k0 = (row_groups * r + few * to + i0) // 4
            dcopies.append(
                send(dfp.at[pl.ds(k0, 3)], dfb.at[r, :, i0], dfs.at[r, d], dfr.at[r, d], b, to)
            )
        i0 = (2 * c + 3 * r) % 4
        k0 = (row_groups * r + few * c + i0) // 4
        dfb[r, :, i0] = dfp[pl.ds(k0, 3)]
    for copy in ocopies:
        copy.wait()
    little, big = rxo.shape[1], rw.shape[1]
    kept_little = pl.ds(pl.multiple_of(little * side, little), little)
    sent_little = pl.ds(pl.multiple_of(little * (1 - side), little), little)
    kept_big = pl.ds(pl.multiple_of(big * side, big), big)
    sent_big = pl.ds(pl.multiple_of(big * (1 - side), big), big)
    hxo[...] = (gso[across].astype(F32) + rao[1].astype(F32)).astype(BF16)
    owno[...] = gso[c].astype(F32) + rao[0].astype(F32)
    ownob[...] = owno[sent_little].astype(BF16)
    for n, r in enumerate((0, 3, 1, 2)):
        for copy in dcopies[3 * n : 3 * n + 3]:
            copy.wait()
        cols = slice(r * width, (r + 1) * width)
        flux = dfb[r].reshape(width, PTS)
        gb[:, cols] = (
            ctb[:, cols].astype(F32) * kept[:, cols] + nt(wf[...], flux) * sea_kept[:, cols]
        ).astype(BF16)
    ocopies = [
        send(ownob, rxo.at[2], os_.at[4], or_.at[4], flip, c),
        send(hxo.at[kept_little], rxo.at[0], os_.at[2], or_.at[2], b, across),
        send(hxo.at[sent_little], rxo.at[1], os_.at[3], or_.at[3], flip, across),
    ]
    gwf[...] = nn(alm[...], dfb[...].reshape(share, PTS))
    wcopies = []
    halo = []
    for turn, i in enumerate((mate, c, diag, across)):
        for r in (0, 3, 1, 2):
            cols = slice(r * width, (r + 1) * width)
            du = (nn(w2[i], gb[:, cols]) * slope[i, :, cols].astype(F32)).astype(BF16)
            dubuf[:, cols] = du
            piece = nn(w1[i], du)
            if turn == 0:
                dzacc[:, cols] = piece
            elif turn < 3:
                dzacc[:, cols] += piece
            else:
                at = (r + 1) * width
                dext[:, at : at + width] = (dzacc[:, cols] + piece).astype(BF16)
                if r == 0:
                    halo.append(
                        send(
                            dext.at[:, at : at + width], dext.at[:, (lats + 1) * width :],
                            h2s.at[1], h2r.at[1], up, c,
                        )
                    )
                if r == 3:
                    halo.append(
                        send(
                            dext.at[:, at : at + width], dext.at[:, :width],
                            h2s.at[0], h2r.at[0], down, c,
                        )
                    )
        g1 = nt(zb[...], dubuf[...])
        g2 = nt(hid[i], gb[...])
        for j in range(2):
            gs[i, j * 256 : j * 256 + 256] = g1[:, j * 128 : j * 128 + 128].astype(BF16)
            gs[i, 512 + j * 256 : 768 + j * 256] = g2[:, j * 128 : j * 128 + 128].astype(BF16)
        gs[i, 1024:1088] = gwf[pl.ds(pl.multiple_of(rows * i, rows), rows), :].astype(BF16)
        if turn == 0:
            mcopies = [send(gs.at[mate], ra.at[0], s0.at[0], q0.at[0], b, mate)]
        if turn == 1:
            mcopies[0].wait()
            own[...] = gs[c].astype(F32) + ra[0].astype(F32)
            ownb[...] = own[sent_big].astype(BF16)
            wcopies.append(send(ownb, rw.at[2], s0.at[4], q0.at[4], flip, c))
        if turn == 2:
            mcopies.append(send(gs.at[diag], ra.at[1], s0.at[1], q0.at[1], b, mate))
        if turn == 3:
            mcopies[1].wait()
            hx[...] = (gs[across].astype(F32) + ra[1].astype(F32)).astype(BF16)
            wcopies.append(send(hx.at[kept_big], rw.at[0], s0.at[2], q0.at[2], b, across))
            wcopies.append(send(hx.at[sent_big], rw.at[1], s0.at[3], q0.at[3], flip, across))
    gkp[...] = jnp.zeros(gkp.shape, F32)
    for i in range(3):
        acc = jnp.zeros((full, 128), F32)
        for r in range(lats):
            prod = ext[:, (r + i) * width : (r + i + 1) * width].astype(F32) * dext[
                :, (r + 1) * width : (r + 2) * width
            ].astype(F32)
            for o in range(0, width, 128):
                acc = acc + prod[:, o : o + 128]
        acc = jnp.sum(acc, axis=1, keepdims=True)
        for j in range(4):
            gkp[j, i : i + 1, :rows] = jnp.sum(
                jnp.where(eye, acc[j * rows : (j + 1) * rows], 0.0), axis=0, keepdims=True
            )
    kcopies = []
    for d, to in pairs:
        kcopies.append(send(gkp.at[to], gkr.at[d], gks.at[d], gkq.at[d], b, to))
    dcopies = []

    def spread(r):
        cols = slice(r * width, (r + 1) * width)
        dl[:, cols] = (
            gb[:, cols].astype(F32)
            + t0 * dext[:, (r + 2) * width : (r + 3) * width].astype(F32)
            + t1 * dext[:, (r + 1) * width : (r + 2) * width].astype(F32)
            + t2 * dext[:, r * width : (r + 1) * width].astype(F32)
        ).astype(BF16)

    def send_back(k):
        lo, hi = cuts[k].start, cuts[k].stop
        for d, to in pairs:
            theirs = pl.ds(pl.multiple_of(rows * to, rows), rows)
            dcopies.append(
                send(dl.at[theirs, lo:hi], dq.at[c, :, lo:hi], das.at[k, d], dar.at[k, d], b, to)
            )

    spread(1)
    spread(2)
    for copy in ocopies:
        copy.wait()
    t[big + 32 :] = (
        owno[kept_little]
        + rxo[0].astype(F32)
        + rxo[1].astype(F32)
        + rxo[2].astype(F32)
    ).astype(BF16)
    for copy in kcopies:
        copy.wait()
    t[big : big + 16] = (gkp[c] + gkr[1] + gkr[2] + gkr[3]).astype(BF16)
    t[big + 16 : big + 32] = jnp.zeros((16, 128), BF16)
    for copy in wcopies:
        copy.wait()
    t[:big] = (
        own[kept_big] + rw[0].astype(F32) + rw[1].astype(F32) + rw[2].astype(F32)
    ).astype(BF16)
    size = r1.shape[1]
    copies = []
    for d in (2, 1, 3):
        to = (x + d) % xs
        cut = pl.ds(pl.multiple_of(to * size, size), size)
        copies.append(
            send(t.at[cut], r1.at[x], s1.at[d], q1.at[d], (2 * to + side) * ZLEN + z, c)
        )
    send_back(2)
    r1[x] = t[pl.ds(pl.multiple_of(x * size, size), size)]
    for copy in halo:
        copy.wait()

    @pl.when(b == 0)
    def _():
        dext[:, :width] = jnp.zeros((full, width), BF16)

    @pl.when(b == bands - 1)
    def _():
        dext[:, (lats + 1) * width :] = jnp.zeros((full, width), BF16)

    spread(0)
    send_back(0)
    spread(3)
    send_back(1)
    dq[c] = dl[mine, :]
    for copy in copies:
        copy.wait()
    total = r1[0].astype(F32)
    for i in range(1, xs):
        total = total + r1[i].astype(F32)
    fs[...] = total.reshape(fs.shape)
    copies = []
    for d in z_far:
        to = (z + d) % ZLEN
        copies.append(send(fs.at[to], r2.at[z], s2.at[d], q2.at[d], q * ZLEN + to, c))
    r2[z] = fs[z]
    for copy in copies:
        copy.wait()
    total = r2[0]
    for i in range(1, ZLEN):
        total = total + r2[i]
    fr[...] = total
    copies = []
    for d in z_far:
        to = (z + d) % ZLEN
        copies.append(send(fr, ag.at[z], s3.at[d], q3.at[d], q * ZLEN + to, c))
    ag[z] = total
    for copy in copies:
        copy.wait()
    tb[...] = ag[...].reshape(size, 128).astype(BF16)
    copies = []
    cut = pl.ds(pl.multiple_of((side * xs + x) * size, size), size)
    for n in range(groups - 1):
        copies.append(send(tb, out.at[cut], s4.at[n], q4.at[n], column(n, 1) * ZLEN + z, c))
    out[cut] = tb[...]
    for copy in dcopies:
        copy.wait()
    for r in range(lats):
        for j in range(4):
            start = r * LON + j * stride
            extra = start % 128
            piece = dq[j, :, r * width : (r + 1) * width]
            if extra == 0:
                dat[:, start : start + width] = piece
                continue
            base = start - extra
            moved = jnp.concatenate([piece.astype(F32), jnp.zeros((rows, 128), F32)], axis=1)
            moved = pltpu.roll(moved, extra, axis=1)
            lead = lax.broadcasted_iota(jnp.int32, (rows, 128), 1)
            dat[:, base : base + 128] = jnp.where(
                lead < extra, dat[:, base : base + 128].astype(F32), moved[:, :128]
            ).astype(BF16)
            dat[:, base + 128 : base + 128 + width] = moved[:, 128:].astype(BF16)
    astore = pltpu.make_async_copy(dat, dat_all, lsem.at[4])
    astore.start()
    for copy in copies:
        copy.wait()
    drain(sp.at[pl.ds(0, 2 * bands - 2)], ss)
    drain(bk.at[pl.ds(0, 2 * bands - 2)], rs)
    dstore.wait()
    astore.wait()


def local(
    atmos, kernels, w_one, w_two, w_flux, sea_mask, route,
    ocean_state, ct_atmos, ct_ocean, wo_one, wo_two,
):
    chans = lax.axis_size("chan")
    bands = lax.axis_size("band")
    rows, points = atmos.shape
    blocks = points // PTS
    quarter = PTS // chans
    lats = points // LON
    share = lats * (LON // quarter // chans + 1) * quarter
    width = share // lats
    slots = ocean_state.shape[2]
    hid = w_one.shape[2]
    full = rows * chans
    wide = wo_one.shape[1]
    total = wide * chans
    groups = bands // ZLEN
    flat = 1536
    big, little = 1088, 384
    size = flat // groups
    small = size // ZLEN
    vm = pl.BlockSpec(memory_space=VMEM)
    anywhere = pl.BlockSpec(memory_space=pl.ANY)

    ocean = VMEM((slots, quarter, PTS), BF16)
    points_first = VMEM((quarter, slots, PTS), BF16)
    split = VMEM((chans, rows, share), BF16)
    extended = VMEM((full, share + 2 * width), BF16)
    square = VMEM((full, share), BF16)
    grouped = VMEM((lats, width // PTS, chans, quarter, PTS), BF16)
    dat, dst, out = pl.pallas_call(
        main_kernel,
        out_shape=[
            jax.ShapeDtypeStruct((rows, points), BF16),
            jax.ShapeDtypeStruct((quarter, slots, PTS), BF16),
            jax.ShapeDtypeStruct((flat, 128), BF16),
        ],
        in_specs=[vm, vm, vm] + [anywhere] * 9,
        out_specs=[anywhere, anywhere, vm],
        scratch_shapes=[
            VMEM((8, 128), jnp.int32),
            pltpu.SMEM((8, 128), jnp.int32),
            VMEM((rows, points), BF16),
            VMEM((rows, points), BF16),
            split, split, extended, square, square,
            VMEM((8, 128), F32),
            VMEM((chans, 8, 128), F32),
            VMEM((full, 128), F32),
            VMEM((chans, full, hid), BF16),
            VMEM((chans, hid, full), BF16),
            VMEM((full, PTS), BF16),
            grouped,
            VMEM((blocks + 1 + 4 * lats, quarter, PTS), BF16),
            VMEM((1, points), F32),
            VMEM((chans, 1, share), F32),
            VMEM((chans, hid, share), BF16),
            VMEM((chans, hid, share), BF16),
            VMEM((rows, points), BF16),
            square, ocean, ocean, ocean, ocean, points_first, points_first, points_first,
            VMEM((2 * PTS, total), BF16),
            VMEM((total, PTS), BF16),
            VMEM((2 * ZLEN * quarter, 2 * ZLEN * quarter), BF16),
            VMEM((2 * PTS, total), F32),
            VMEM((PTS, total), F32),
            VMEM((blocks, quarter, PTS), BF16),
            grouped, square, extended, square, split,
            VMEM((full, share), F32),
            VMEM((hid, share), BF16),
            VMEM((full, PTS), F32),
            VMEM((chans, 16, 128), F32),
            VMEM((chans, 16, 128), F32),
            VMEM((chans, big, 128), BF16),
            VMEM((2, big, 128), BF16),
            VMEM((big, 128), BF16),
            VMEM((3, big // 2, 128), BF16),
            VMEM((chans, little, 128), BF16),
            VMEM((2, little, 128), BF16),
            VMEM((little, 128), BF16),
            VMEM((3, little // 2, 128), BF16),
            VMEM((big, 128), F32),
            VMEM((little, 128), F32),
            VMEM((big // 2, 128), BF16),
            VMEM((little // 2, 128), BF16),
            VMEM((flat // 2, 128), BF16),
            VMEM((groups // 2, size, 128), BF16),
            VMEM((ZLEN, small, 128), F32),
            VMEM((ZLEN, small, 128), F32),
            VMEM((small, 128), F32),
            VMEM((ZLEN, small, 128), F32),
            VMEM((size, 128), BF16),
            DMA((5,)), DMA((7,)), DMA((2, 4)), DMA((2, 4)), DMA((3, 5)), DMA((3, 5)), DMA((4,)), DMA((4,)),
            DMA((3, 4)), DMA((3, 4)), DMA((lats, 4, 2)), DMA((lats, 4, 2)), DMA((4,)), DMA((4,)),
            DMA, DMA((groups,)), DMA, DMA,
            DMA((5,)), DMA((5,)), DMA((lats, 4)), DMA((lats, 4)), DMA((2,)), DMA((2,)),
            DMA((4,)), DMA((4,)), DMA((3, 4)), DMA((3, 4)), DMA((5,)), DMA((5,)),
            DMA((groups,)), DMA((groups,)), DMA((ZLEN,)), DMA((ZLEN,)),
            DMA((ZLEN,)), DMA((ZLEN,)), DMA((groups,)), DMA((groups,)),
        ],
        compiler_params=pltpu.CompilerParams(
            collective_id=0, has_side_effects=True, vmem_limit_bytes=LIMIT
        ),
    )(
        route.T, kernels.transpose(1, 0, 2), sea_mask.reshape(blocks, PTS), atmos, w_one[0], w_two[0],
        w_flux, wo_one, wo_two, ct_atmos, ocean_state, ct_ocean,
    )
    datmos, dk, dw1, dw2, dwf, dstate, do1, do2 = pl.pallas_call(
        finish_kernel,
        out_shape=[
            jax.ShapeDtypeStruct(dat.shape, BF16),
            jax.ShapeDtypeStruct((3, 1, rows), F32),
            jax.ShapeDtypeStruct((full, hid), F32),
            jax.ShapeDtypeStruct((hid, full), F32),
            jax.ShapeDtypeStruct((rows, PTS), F32),
            jax.ShapeDtypeStruct(dst.shape, BF16),
            jax.ShapeDtypeStruct((2 * PTS, wide), F32),
            jax.ShapeDtypeStruct((wide, PTS), F32),
        ],
        in_specs=[vm] * 3,
        out_specs=[vm] * 8,
        compiler_params=pltpu.CompilerParams(vmem_limit_bytes=LIMIT + (4 << 20)),
    )(dat, dst, out)
    return datmos, dk.transpose(1, 0, 2), dw1[None], dw2[None], dwf, dstate[:, None], do1, do2


def solution(mesh):
    in_specs = (
        P("chan", "band"),
        P(None, None, "chan"),
        P(None, None, "chan"),
        P(None, "chan", None),
        P("chan", None),
        P("band"),
        P("band", None),
        P(None, "band", None, None),
        P("chan", "band"),
        P(None, "band", None, None),
        P(None, "chan"),
        P("chan", None),
    )
    out_specs = (
        P("chan", "band"),
        P(None, None, "chan"),
        P(None, None, "chan"),
        P(None, "chan", None),
        P("chan", None),
        P("chan", "band", None, None),
        P(None, "chan"),
        P("chan", None),
    )
    return jax.shard_map(local, mesh=mesh, in_specs=in_specs, out_specs=out_specs, check_vma=False)
```
